128 devices in a mesh: seg: 4 (over x), doc: 32 (over y, z, core).
Axes of the slice: x: 4, y: 4, z: 4, core: 2. Of those that a mesh axis runs over, the one named last changes fastest.
Arguments:
- tokens: bfloat16 [64, 512, 512], P('doc', 'seg'), may hold values from -6 to 6
- memory_start: bfloat16 [64, 64, 512], P('doc'), may hold values from -6 to 6
- doc_lengths: int32 [64, 8], P('doc'), may hold values from 1 to 448, 480 in all within a row
- attn_weights: bfloat16 [3, 4, 512, 512], replicated, as said below
- ffn_in: bfloat16 [512, 2048], replicated, may hold values from -0.25 to 0.25
- ffn_out: bfloat16 [2048, 512], replicated, may hold values from -0.125 to 0.125
- gains: float32 [5, 512], replicated, may hold values from 0.5 to 1.5
- forget_w: float32 [512], replicated, may hold values from -0.25 to 0.25
- forget_bias: float32 [64], replicated, may hold values from 1 to 3
- out_cotangent: bfloat16 [64, 512, 512], P('doc', 'seg'), may hold values from -6 to 6
- memory_cotangent: bfloat16 [64, 256, 512], P('doc', 'seg'), may hold values from -6 to 6
Outputs:
- activations: bfloat16 [64, 512, 512], P('doc', 'seg')
- memories: bfloat16 [64, 256, 512], P('doc', 'seg')
- grad_tokens: float32 [64, 512, 512], P('doc', 'seg')
- grad_memory: float32 [64, 256, 512], P('doc', 'seg')
- grad_attn: float32 [3, 4, 512, 512], replicated
- grad_ffn_in: float32 [512, 2048], replicated
- grad_ffn_out: float32 [2048, 512], replicated
- grad_gains: float32 [5, 512], replicated
- grad_forget_w: float32 [512], replicated
- grad_forget_bias: float32 [64], replicated
The draws below stay inside these ranges and needn't reach their ends.
Inputs may be any that keep to these rules, and one draw needn't show every extreme that they name: `doc_lengths`: each row sums to 480 and holds one document of 448 tokens. `attn_weights`: independent entries of scale 512 ** -0.5, the output projections four times that.
All inputs are finite; a program needn't handle non-finite values.
Results may differ from the reference program's by a relative error of at most 0.025.
Values may be sent and summed in bfloat16 or wider, within the bound.
A program may use at most 384 MiB of HBM per device.

```python
import math
import jax
import jax.numpy as jnp
import numpy as np
from jax import lax

D = 512
HEADS = 8
FF = 2048
SLOTS = 64
SEGLEN = 128
NDOC = 8
STREAMS = 64
LEN = 512
N_SEG = 4


def draw_attn_weights(key, part):
    key = jax.random.fold_in(key, 11)
    base = jax.random.normal(key, (3, 4, D, D), jnp.float32)
    factor = jnp.array([1.0, 1.0, 1.0, 4.0], jnp.float32)
    return (base * factor[None, :, None, None] * D ** (-0.5)).astype(jnp.bfloat16)


def block_levels(stream_key, dims, cuts, low, largest):
    factor_of = 1.0
    for axis_at, shards_of in cuts:
        draws = jax.random.uniform(jax.random.fold_in(jax.random.fold_in(stream_key, 6), axis_at), (shards_of,), jnp.float32, low / len(cuts), largest / len(cuts))
        factor_of = factor_of * jnp.repeat(jnp.exp(draws), dims[axis_at] // shards_of).reshape((-1,) + (1,) * (len(dims) - 1 - axis_at))
    return factor_of


def length_profile(count, total, bound, slope):
    loads = [(1 << 20) // math.isqrt(standing ** slope) + 1 for standing in range(2, count + 1)]
    surplus, holding = total - bound - (count - 1), [1] * (count - 1)
    while surplus > 0:
        movable = [i for i in range(count - 1) if holding[i] < bound]
        pool, remaining = sum([loads[i] for i in movable]), surplus
        for i in movable:
            more = min(bound - holding[i], max(1, remaining * loads[i] // pool), surplus)
            holding[i] = holding[i] + more
            surplus = surplus - more
    return np.array([bound] + holding)


def uneven_parts(own_key, number_of, total, limit, lean):
    if number_of == 2:
        one = jax.random.randint(own_key, (), max(1, total - limit), min(limit, total - 1) + 1)
        return jnp.stack([one, total - one])
    tallies = jnp.asarray(length_profile(number_of, total, limit, lean), jnp.int32)
    pairs = (number_of - 1) // 2
    giver, receiver = tallies[1:1 + 2 * pairs:2], tallies[2:2 + 2 * pairs:2]
    margin = jnp.minimum(giver - 1, limit - receiver)
    shifted = jax.random.randint(jax.random.fold_in(own_key, 1), (pairs,), 0, 1 << 20) % (margin + 1)
    tallies = tallies.at[1:1 + 2 * pairs:2].set(giver - shifted).at[2:2 + 2 * pairs:2].set(receiver + shifted)
    return tallies[jax.random.permutation(jax.random.fold_in(own_key, 2), number_of)]


def gaussian(stream_key, extent, scale, reach, shards=(), held_as=jnp.bfloat16):
    factor_of = block_levels(stream_key, extent, shards, -0.22, 0.18) if shards else 1.0
    values = jax.random.normal(stream_key, extent, jnp.float32) * scale * factor_of
    return jnp.minimum(jnp.maximum(values, -reach), reach).astype(held_as)


def setup_inputs(seed: int = 0) -> dict:
    splits = jax.random.split(jax.random.key(seed), 12)
    return {
        "tokens": gaussian(splits[0], (STREAMS, LEN, D), 1.0, 6.0, ((0, 32), (1, 4))),
        "memory_start": gaussian(splits[1], (STREAMS, SLOTS, D), 1.0, 6.0, ((0, 32),)),
        "doc_lengths": jax.vmap(lambda own: uneven_parts(own, NDOC, LEN - SEGLEN // 4, LEN - SEGLEN // 2, 2))(jax.random.split(splits[2], STREAMS)).reshape((STREAMS, NDOC)).astype(jnp.int32),
        "attn_weights": draw_attn_weights(jax.random.fold_in(splits[11], 71), 0),
        "ffn_in": gaussian(splits[4], (D, FF), D ** -0.5, 0.25),
        "ffn_out": gaussian(splits[5], (FF, D), FF ** -0.5, 0.125),
        "gains": jnp.clip(1.0 + 0.1 * jax.random.normal(splits[6], (5, D), jnp.float32), 0.5, 1.5),
        "forget_w": gaussian(splits[7], (D,), D ** -0.5, 0.25, (), jnp.float32),
        "forget_bias": jnp.clip(jax.random.uniform(splits[8], (SLOTS,), jnp.float32, 1.0, 3.0), 1.0, 3.0),
        "out_cotangent": gaussian(splits[9], (STREAMS, LEN, D), 1.0, 6.0, ((0, 32), (1, 4))),
        "memory_cotangent": gaussian(splits[10], (STREAMS, N_SEG * SLOTS, D), 1.0, 6.0, ((0, 32), (1, 4))),
    }


precise = lax.Precision.HIGHEST

@jax.custom_vjp
def low(v):
    return lax.optimization_barrier(v.astype(jnp.bfloat16)).astype(jnp.float32)

@jax.custom_vjp
def low_back(v):
    return v

def low_keep(v):
    return (low(v), None)

def low_pass(kept, grad):
    return (grad,)

def back_keep(v):
    return (v, None)

def back_low(kept, grad):
    return (low(grad),)
low.defvjp(low_keep, low_pass)
low_back.defvjp(back_keep, back_low)

def layer_norm(values, gain):
    row_mean = lax.optimization_barrier(jnp.mean(values, -1, keepdims=True))
    centered = values - row_mean
    spread = lax.optimization_barrier(jnp.mean(centered * centered, -1, keepdims=True))
    return centered * lax.rsqrt(spread + 1e-05) * gain

def project(low_in, weight):
    return low_back(jnp.dot(low_in, weight, precision=precise))

def attend(query, key_rows, value_rows, allowed):
    row_count, model_width = query.shape
    head_size = model_width // HEADS
    q_heads = low(query).reshape(row_count, HEADS, head_size)
    k_heads = low(key_rows).reshape(-1, HEADS, head_size)
    v_heads = low(value_rows).reshape(-1, HEADS, head_size)
    scores = low_back(jnp.einsum('qhd,khd->hqk', q_heads, k_heads, precision=precise) / math.sqrt(head_size))
    scores = jnp.where(allowed[None], scores, -1e+30)
    row_max = lax.optimization_barrier(jnp.max(scores, -1, keepdims=True))
    expd = jnp.exp(scores - row_max)
    probs = expd / lax.optimization_barrier(jnp.sum(expd, -1, keepdims=True))
    mixed = jnp.einsum('hqk,khd->qhd', low(probs), v_heads, precision=precise)
    return low_back(mixed.reshape(row_count, model_width))

def layer_one(seg_tokens, memory_in, doc_ids, attn, w_first, w_second, gain_rows, gate_w, gate_bias):
    seg_count = seg_tokens.shape[0]
    slot_count = memory_in.shape[0]
    memory = low_back(memory_in)
    normed_one = low(layer_norm(seg_tokens, gain_rows[0]))
    same_doc = doc_ids[:, None] == doc_ids[None, :]
    self_out = attend(project(normed_one, attn[0, 0]), project(normed_one, attn[0, 1]), project(normed_one, attn[0, 2]), same_doc)
    residual = seg_tokens + project(low(self_out), attn[0, 3])
    mem_norm = layer_norm(memory, gain_rows[4])
    mem_low = low(mem_norm)
    normed_two = low(layer_norm(residual, gain_rows[1]))
    every_slot = jnp.ones((seg_count, slot_count), dtype=bool)
    cross_out = attend(project(normed_two, attn[1, 0]), project(mem_low, attn[1, 1]), project(mem_low, attn[1, 2]), every_slot)
    residual = residual + project(low(cross_out), attn[1, 3])
    normed_three = low(layer_norm(residual, gain_rows[2]))
    hidden = low(jax.nn.gelu(project(normed_three, w_first)))
    outputs = residual + project(hidden, w_second)
    normed_four = low(layer_norm(outputs, gain_rows[3]))
    live_keys = jnp.broadcast_to((doc_ids < NDOC)[None, :], (slot_count, seg_count))
    written = attend(project(mem_low, attn[2, 0]), project(normed_four, attn[2, 1]), project(normed_four, attn[2, 2]), live_keys)
    update = project(low(written), attn[2, 3])
    forget = jax.nn.sigmoid(jnp.dot(mem_norm, gate_w, precision=precise) + gate_bias)[:, None]
    fresh = low(low_back(forget * memory + (1.0 - forget) * update))
    return (outputs, fresh)

def reference(tokens, memory_start, doc_lengths, attn_weights, ffn_in, ffn_out, gains, forget_w, forget_bias, out_cotangent, memory_cotangent):
    stream_count, total, model_width = tokens.shape
    seg_total = total // SEGLEN
    slot_count = memory_start.shape[1]
    doc_ends = jnp.cumsum(doc_lengths, -1)
    positions = jnp.arange(total, dtype=jnp.int32)
    doc_ids = lax.optimization_barrier(jnp.sum((doc_ends[:, None, :] <= positions[None, :, None]).astype(jnp.int32), -1))
    seg_docs = doc_ids.reshape(stream_count, seg_total, SEGLEN).transpose(1, 0, 2)
    run_all = jax.vmap(layer_one, in_axes=(0, 0, 0, None, None, None, None, None, None))

    def forward(tok_all, mem_first, shifts, attn, w_first, w_second, gain_rows, gate_w, gate_bias):
        seg_rows = tok_all.reshape(stream_count, seg_total, SEGLEN, model_width).transpose(1, 0, 2, 3)

        def advance(memory, item):
            rows_here, docs_here, shift_here = item
            outputs, fresh = run_all(rows_here, memory + shift_here, docs_here, attn, w_first, w_second, gain_rows, gate_w, gate_bias)
            return (fresh, (outputs, fresh))
        _, (outs_all, mems_all) = lax.scan(advance, mem_first, (seg_rows, seg_docs, shifts))
        acts = outs_all.transpose(1, 0, 2, 3).reshape(stream_count, total, model_width)
        mems = mems_all.transpose(1, 0, 2, 3).reshape(stream_count, seg_total * slot_count, model_width)
        return (acts, mems)
    shifts = jnp.zeros((seg_total, stream_count, slot_count, model_width), jnp.float32)
    primals = (tokens.astype(jnp.float32), memory_start.astype(jnp.float32), shifts, attn_weights.astype(jnp.float32), ffn_in.astype(jnp.float32), ffn_out.astype(jnp.float32), gains, forget_w, forget_bias)
    (acts, mems), pullback = jax.vjp(forward, *primals)
    grads = pullback((out_cotangent.astype(jnp.float32), memory_cotangent.astype(jnp.float32)))
    grad_shift = grads[2].transpose(1, 0, 2, 3).reshape(stream_count, seg_total * slot_count, model_width)
    return (acts.astype(jnp.bfloat16), mems.astype(jnp.bfloat16), grads[0], grad_shift, grads[3], grads[4], grads[5], grads[6], grads[7], grads[8])
```

```python
import functools

import jax
import jax.numpy as jnp
from jax import lax
from jax.experimental import pallas as pl
from jax.experimental.pallas import tpu as pltpu
from jax.sharding import PartitionSpec as P

HEADS = 8
NDOC = 8
D = 512
FF = 2048
SLOTS = 64
SEG = 128
NSEG = 4
ROWS = NSEG * SEG
MROWS = NSEG * SLOTS
PAIRS = 4
PAIR = 128
FCHUNK = 512
BLOCK = 256
NBLOCKS = 20

f32 = jnp.float32
bf16 = jnp.bfloat16


def dot(a, b):
    return lax.dot_general(a, b, (((1,), (0,)), ((), ())), preferred_element_type=f32)


def dot_nt(a, b):
    return lax.dot_general(a, b, (((1,), (1,)), ((), ())), preferred_element_type=f32)


def dot_tn(a, b):
    return lax.dot_general(a, b, (((0,), (0,)), ((), ())), preferred_element_type=f32)


def norm_stats(values):
    centered = values - jnp.mean(values, -1, keepdims=True)
    rstd = lax.rsqrt(jnp.mean(centered * centered, -1, keepdims=True) + 1e-05)
    return centered * rstd, rstd


def norm_back(grad, gain, xhat, rstd):
    scaled = grad * gain
    mean_one = jnp.mean(scaled, -1, keepdims=True)
    mean_two = jnp.mean(scaled * xhat, -1, keepdims=True)
    return rstd * (scaled - mean_one - xhat * mean_two)


def head_halves(values):
    low_half = lax.broadcasted_iota(jnp.int32, values.shape, 1) % PAIR < PAIR // 2
    return jnp.where(low_half, values, 0.0).astype(bf16), jnp.where(low_half, 0.0, values).astype(bf16)


def join_halves(stacked):
    rows = stacked.shape[0] // 2
    low_half = lax.broadcasted_iota(jnp.int32, (rows, PAIR), 1) < PAIR // 2
    return jnp.where(low_half, stacked[:rows], stacked[rows:])


def softmax_rows(scores):
    expd = jnp.exp(scores - jnp.max(scores, -1, keepdims=True))
    return expd * (1.0 / jnp.sum(expd, -1, keepdims=True))


def softmax_back(probs, grad):
    return probs * (grad - jnp.sum(probs * grad, -1, keepdims=True))


def gelu_both(u):
    square = u * u
    tanh = jnp.tanh(0.7978845608028654 * u * (1.0 + 0.044715 * square))
    half = 0.5 + 0.5 * tanh
    slope = half + u * half * (1.0 - tanh) * (0.7978845608028654 + 0.1070322243 * square)
    return u * half, slope


def layer_kernel(
    ends_ref, half_ref,
    tok_ref, mem_ref, ocot_ref, mcot_ref, attn_ref, win_ref, wout_ref, gains_ref, fw_ref, fb_ref,
    act_ref, mout_ref, gtok_ref, gmem_ref, dw_ref, small_ref,
    h_s, q_s, k_s, v_s, p_s, o_s, xh0_s, rs0_s,
    res_s, n1_s, xh1_s, rs1_s, cq_s, ck_s, cv_s, cp_s, co_s,
    n2_s, xh2_s, rs2_s, hid_s, gd_s,
    t_s, xh3_s, rs3_s, m_s, xh4_s, rs4_s, mlow_s, gate_s, upd_s, mprev_s,
    wq_s, wk_s, wv_s, wp_s, wo_s,
    gup_s, dwq_s, dwk_s, dwv_s, gyl_s, gul_s, gbl_s, dcq_s, dck_s, dcv_s,
    gb_s, gal_s, dq_s, dk_s, dv_s, gain_s, gm_s,
):
    gain = [gains_ref[i : i + 1, :] for i in range(5)]

    def doc_ids(shape, dim, base):
        pos = lax.broadcasted_iota(jnp.int32, shape, dim) + base
        ids = jnp.zeros(shape, jnp.int32)
        for j in range(NDOC):
            ids += (ends_ref[j] <= pos).astype(jnp.int32)
        return ids

    xhat, rstd = norm_stats(tok_ref[...].astype(f32))
    xh0_s[...] = xhat
    rs0_s[...] = rstd
    h = (xhat * gain[0]).astype(bf16)
    h_s[...] = h
    q_s[0], q_s[1] = head_halves(dot(h, attn_ref[0]) * 0.125)
    k_s[...] = dot(h, attn_ref[1]).astype(bf16)
    v_s[...] = dot(h, attn_ref[2]).astype(bf16)

    def self_forward(seg, carry):
        rows = pl.ds(pl.multiple_of(seg * SEG, SEG), SEG)
        same = doc_ids((SEG, SEG), 0, seg * SEG) == doc_ids((SEG, SEG), 1, seg * SEG)
        same = jnp.concatenate([same.astype(jnp.int32)] * 2, 0) > 0
        for pair in range(PAIRS):
            lanes = slice(pair * PAIR, (pair + 1) * PAIR)
            q_both = jnp.concatenate([q_s[0, rows, lanes], q_s[1, rows, lanes]], 0)
            scores = jnp.where(same, dot_nt(q_both, k_s[rows, lanes]), -1e30)
            probs = softmax_rows(scores).astype(bf16)
            p_s[seg, pair] = probs
            o_s[rows, lanes] = join_halves(dot(probs, v_s[rows, lanes])).astype(bf16)
        return carry

    lax.fori_loop(0, NSEG, self_forward, 0)
    res = tok_ref[...].astype(f32) + dot(o_s[...], attn_ref[3])
    res_s[...] = res
    xhat, rstd = norm_stats(res)
    xh1_s[...] = xhat
    rs1_s[...] = rstd
    n1 = (xhat * gain[1]).astype(bf16)
    n1_s[...] = n1
    cq_s[0], cq_s[1] = head_halves(dot(n1, attn_ref[4]) * 0.125)

    mprev_s[...] = mem_ref[...].astype(f32)

    def forward(seg, carry):
        rows = pl.ds(pl.multiple_of(seg * SEG, SEG), SEG)
        slots = pl.ds(pl.multiple_of(seg * SLOTS, SLOTS), SLOTS)
        mem = mprev_s[...]
        xhat, rstd = norm_stats(mem)
        xh4_s[slots, :] = xhat
        rs4_s[slots, :] = rstd
        m = xhat * gain[4]
        mlow = m.astype(bf16)
        mlow_s[slots, :] = mlow
        gate = jax.nn.sigmoid(jnp.sum(m * fw_ref[...], -1, keepdims=True) + fb_ref[...])
        gate_s[slots, :] = gate
        ck = dot(mlow, attn_ref[5]).astype(bf16)
        cv = dot(mlow, attn_ref[6]).astype(bf16)
        ck_s[slots, :] = ck
        cv_s[slots, :] = cv
        wq0, wq1 = head_halves(dot(mlow, attn_ref[8]) * 0.125)
        wq_s[0, slots, :] = wq0
        wq_s[1, slots, :] = wq1
        for pair in range(PAIRS):
            lanes = slice(pair * PAIR, (pair + 1) * PAIR)
            q_both = jnp.concatenate([cq_s[0, rows, lanes], cq_s[1, rows, lanes]], 0)
            probs = softmax_rows(dot_nt(q_both, ck[:, lanes])).astype(bf16)
            cp_s[seg, pair] = probs
            co_s[rows, lanes] = join_halves(dot(probs, cv[:, lanes])).astype(bf16)
        res = res_s[rows, :] + dot(co_s[rows, :], attn_ref[7])
        xhat, rstd = norm_stats(res)
        xh2_s[rows, :] = xhat
        rs2_s[rows, :] = rstd
        n2 = (xhat * gain[2]).astype(bf16)
        n2_s[rows, :] = n2
        for c in range(0, FF, FCHUNK):
            hid, slope = gelu_both(dot(n2, win_ref[:, c : c + FCHUNK]))
            hid = hid.astype(bf16)
            hid_s[rows, c : c + FCHUNK] = hid
            gd_s[rows, c : c + FCHUNK] = slope.astype(bf16)
            res = res + dot(hid, wout_ref[c : c + FCHUNK, :])
        act_ref[rows, :] = res.astype(bf16)
        xhat, rstd = norm_stats(res)
        xh3_s[rows, :] = xhat
        rs3_s[rows, :] = rstd
        t = (xhat * gain[3]).astype(bf16)
        t_s[rows, :] = t
        wk = dot(t, attn_ref[9]).astype(bf16)
        wv = dot(t, attn_ref[10]).astype(bf16)
        wk_s[rows, :] = wk
        wv_s[rows, :] = wv
        live = doc_ids((2 * SLOTS, SEG), 1, seg * SEG) < NDOC
        for pair in range(PAIRS):
            lanes = slice(pair * PAIR, (pair + 1) * PAIR)
            q_both = jnp.concatenate([wq0[:, lanes], wq1[:, lanes]], 0)
            scores = jnp.where(live, dot_nt(q_both, wk[:, lanes]), -1e30)
            probs = softmax_rows(scores).astype(bf16)
            wp_s[seg, pair] = probs
            wo_s[slots, lanes] = join_halves(dot(probs, wv[:, lanes])).astype(bf16)
        update = dot(wo_s[slots, :], attn_ref[11])
        upd_s[slots, :] = mem - update
        fresh = (update + gate * (mem - update)).astype(bf16)
        mout_ref[slots, :] = fresh
        mprev_s[...] = fresh.astype(f32)
        return carry

    lax.fori_loop(0, NSEG, forward, 0)

    gm_s[...] = jnp.zeros_like(gm_s)
    gain_s[...] = jnp.zeros_like(gain_s)
    small_ref[...] = jnp.zeros_like(small_ref)

    def backward(step, carry):
        seg = NSEG - 1 - step
        rows = pl.ds(pl.multiple_of(seg * SEG, SEG), SEG)
        slots = pl.ds(pl.multiple_of(seg * SLOTS, SLOTS), SLOTS)
        gz = (mcot_ref[slots, :].astype(f32) + gm_s[...]).astype(bf16).astype(f32)
        gate = gate_s[slots, :]
        dgate = jnp.sum(gz * upd_s[slots, :], -1, keepdims=True) * gate * (1.0 - gate)
        gup = ((1.0 - gate) * gz).astype(bf16)
        gup_s[slots, :] = gup
        xh4 = xh4_s[slots, :]
        small_ref[0:1, :] += jnp.sum(dgate * (xh4 * gain[4]), 0, keepdims=True)
        small_ref[8:72, 0:128] += jnp.broadcast_to(dgate, (SLOTS, 128))
        gm = dgate * fw_ref[...]
        g_o0, g_o1 = head_halves(dot_nt(gup, attn_ref[11]))
        for pair in range(PAIRS):
            lanes = slice(pair * PAIR, (pair + 1) * PAIR)
            probs = wp_s[seg, pair]
            g_both = jnp.concatenate([g_o0[:, lanes], g_o1[:, lanes]], 0)
            q_both = jnp.concatenate([wq_s[0, slots, lanes], wq_s[1, slots, lanes]], 0)
            ds = softmax_back(probs.astype(f32), dot_nt(g_both, wv_s[rows, lanes])).astype(bf16)
            dwv_s[rows, lanes] = dot_tn(probs, g_both).astype(bf16)
            dwk_s[rows, lanes] = dot_tn(ds, q_both).astype(bf16)
            dwq_s[slots, lanes] = (join_halves(dot(ds, wk_s[rows, lanes])) * 0.125).astype(bf16)
        gm = gm + dot_nt(dwq_s[slots, :], attn_ref[8])
        gt = dot_nt(dwk_s[rows, :], attn_ref[9]) + dot_nt(dwv_s[rows, :], attn_ref[10])
        xhat = xh3_s[rows, :]
        gain_s[3:4, :] += jnp.sum(gt * xhat, 0, keepdims=True)
        gy = ocot_ref[rows, :].astype(f32) + norm_back(gt, gain[3], xhat, rs3_s[rows, :])
        gyl = gy.astype(bf16)
        gyl_s[rows, :] = gyl
        gn2 = jnp.zeros((SEG, D), f32)
        for c in range(0, FF, FCHUNK):
            ghid = dot_nt(gyl, wout_ref[c : c + FCHUNK, :])
            gul = (ghid * gd_s[rows, c : c + FCHUNK].astype(f32)).astype(bf16)
            gul_s[rows, c : c + FCHUNK] = gul
            gn2 = gn2 + dot_nt(gul, win_ref[:, c : c + FCHUNK])
        xhat = xh2_s[rows, :]
        gain_s[2:3, :] += jnp.sum(gn2 * xhat, 0, keepdims=True)
        gb = gy + norm_back(gn2, gain[2], xhat, rs2_s[rows, :])
        gb_s[rows, :] = gb
        gbl = gb.astype(bf16)
        gbl_s[rows, :] = gbl
        g_o0, g_o1 = head_halves(dot_nt(gbl, attn_ref[7]))
        for pair in range(PAIRS):
            lanes = slice(pair * PAIR, (pair + 1) * PAIR)
            probs = cp_s[seg, pair]
            g_both = jnp.concatenate([g_o0[:, lanes], g_o1[:, lanes]], 0)
            q_both = jnp.concatenate([cq_s[0, rows, lanes], cq_s[1, rows, lanes]], 0)
            ds = softmax_back(probs.astype(f32), dot_nt(g_both, cv_s[slots, lanes])).astype(bf16)
            dcv_s[slots, lanes] = dot_tn(probs, g_both).astype(bf16)
            dck_s[slots, lanes] = dot_tn(ds, q_both).astype(bf16)
            dcq_s[rows, lanes] = (join_halves(dot(ds, ck_s[slots, lanes])) * 0.125).astype(bf16)
        gm = gm + dot_nt(dck_s[slots, :], attn_ref[5]) + dot_nt(dcv_s[slots, :], attn_ref[6])
        gain_s[4:5, :] += jnp.sum(gm * xh4, 0, keepdims=True)
        gmem = gate * gz + norm_back(gm, gain[4], xh4, rs4_s[slots, :])
        gmem = gmem.astype(bf16)
        gmem_ref[slots, :] = gmem
        gm_s[...] = gmem.astype(f32)
        return carry

    lax.fori_loop(0, NSEG, backward, 0)

    gn1 = dot_nt(dcq_s[...], attn_ref[4])
    xhat = xh1_s[...]
    gain_s[1:2, :] = jnp.sum(gn1 * xhat, 0, keepdims=True)
    ga = gb_s[...] + norm_back(gn1, gain[1], xhat, rs1_s[...])
    gb_s[...] = ga
    gal = ga.astype(bf16)
    gal_s[...] = gal
    g0, g1 = head_halves(dot_nt(gal, attn_ref[3]))
    cq_s[0] = g0
    cq_s[1] = g1

    def self_backward(seg, carry):
        rows = pl.ds(pl.multiple_of(seg * SEG, SEG), SEG)
        for pair in range(PAIRS):
            lanes = slice(pair * PAIR, (pair + 1) * PAIR)
            probs = p_s[seg, pair]
            g_both = jnp.concatenate([cq_s[0, rows, lanes], cq_s[1, rows, lanes]], 0)
            q_both = jnp.concatenate([q_s[0, rows, lanes], q_s[1, rows, lanes]], 0)
            ds = softmax_back(probs.astype(f32), dot_nt(g_both, v_s[rows, lanes])).astype(bf16)
            dv_s[rows, lanes] = dot_tn(probs, g_both).astype(bf16)
            dk_s[rows, lanes] = dot_tn(ds, q_both).astype(bf16)
            dq_s[rows, lanes] = (join_halves(dot(ds, k_s[rows, lanes])) * 0.125).astype(bf16)
        return carry

    lax.fori_loop(0, NSEG, self_backward, 0)
    gh = dot_nt(dq_s[...], attn_ref[0]) + dot_nt(dk_s[...], attn_ref[1]) + dot_nt(dv_s[...], attn_ref[2])
    xhat = xh0_s[...]
    gain_s[0:1, :] = jnp.sum(gh * xhat, 0, keepdims=True)
    gtok_ref[...] = (gb_s[...] + norm_back(gh, gain[0], xhat, rs0_s[...])).astype(bf16)
    small_ref[1:6, :] = gain_s[0:5, :]

    half = half_ref[0]
    cut = pl.ds(pl.multiple_of(half * BLOCK, BLOCK), BLOCK)
    pairs = [
        (h_s, dq_s), (h_s, dk_s), (h_s, dv_s), (o_s, gal_s),
        (n1_s, dcq_s), (mlow_s, dck_s), (mlow_s, dcv_s), (co_s, gbl_s),
        (mlow_s, dwq_s), (t_s, dwk_s), (t_s, dwv_s), (wo_s, gup_s),
    ]
    for i, (left, right) in enumerate(pairs):
        dw_ref[i] = dot_tn(left[:, cut], right[...]).astype(bf16)
    for i in range(4):
        dw_ref[12 + i] = dot_tn(n2_s[:, cut], gul_s[:, i * D : (i + 1) * D]).astype(bf16)
    for i in range(4):
        cut_i = pl.ds(pl.multiple_of(half * 4 * BLOCK + i * BLOCK, BLOCK), BLOCK)
        dw_ref[16 + i] = dot_tn(hid_s[:, cut_i], gyl_s[...]).astype(bf16)


def run_layer(ends, half, tok, mem, ocot, mcot, attn, win, wout, gains, fw, fb):
    def rows(dtype=bf16, width=D):
        return pltpu.VMEM((ROWS, width), dtype)

    def slots(dtype=bf16, width=D):
        return pltpu.VMEM((MROWS, width), dtype)

    def two(count):
        return pltpu.VMEM((2, count, D), bf16)

    scratch = [
        rows(), two(ROWS), rows(), rows(), pltpu.VMEM((NSEG, PAIRS, 2 * SEG, SEG), bf16), rows(),
        rows(f32), rows(f32, 1),
        rows(f32), rows(), rows(f32), rows(f32, 1), two(ROWS), slots(), slots(),
        pltpu.VMEM((NSEG, PAIRS, 2 * SEG, SLOTS), bf16), rows(),
        rows(), rows(f32), rows(f32, 1), rows(bf16, FF), rows(bf16, FF),
        rows(), rows(f32), rows(f32, 1), slots(f32), slots(f32), slots(f32, 1), slots(), slots(f32, 1),
        slots(f32), pltpu.VMEM((SLOTS, D), f32),
        two(MROWS), rows(), rows(), pltpu.VMEM((NSEG, PAIRS, 2 * SLOTS, SEG), bf16), slots(),
        slots(), slots(), rows(), rows(), rows(), rows(bf16, FF), rows(), rows(), slots(), slots(),
        rows(f32), rows(), rows(), rows(), rows(), pltpu.VMEM((8, D), f32), pltpu.VMEM((SLOTS, D), f32),
    ]
    smem = pl.BlockSpec(memory_space=pltpu.SMEM)
    vmem = pl.BlockSpec(memory_space=pltpu.VMEM)
    return pl.pallas_call(
        layer_kernel,
        out_shape=(
            jax.ShapeDtypeStruct((ROWS, D), bf16),
            jax.ShapeDtypeStruct((MROWS, D), bf16),
            jax.ShapeDtypeStruct((ROWS, D), bf16),
            jax.ShapeDtypeStruct((MROWS, D), bf16),
            jax.ShapeDtypeStruct((NBLOCKS, BLOCK, D), bf16),
            jax.ShapeDtypeStruct((72, D), f32),
        ),
        in_specs=[smem] * 2 + [vmem] * 10,
        out_specs=[vmem] * 6,
        scratch_shapes=scratch,
        compiler_params=pltpu.CompilerParams(vmem_limit_bytes=60 << 20),
        name="layer",
    )(ends, half, tok, mem, ocot, mcot, attn, win, wout, gains, fw, fb)


def body(
    tokens, memory_start, doc_lengths, attn_weights, ffn_in, ffn_out, gains, forget_w, forget_bias,
    out_cotangent, memory_cotangent,
):
    section = lax.axis_index("seg")
    stream, half = section % 2, section // 2

    def one_stream(value):
        gathered = lax.all_gather(value, "seg", axis=0)
        picked = lax.dynamic_index_in_dim(gathered, stream, 1, keepdims=False)
        return picked.reshape(-1, D)

    ends = lax.dynamic_index_in_dim(jnp.cumsum(doc_lengths, -1).astype(jnp.int32), stream, 0, keepdims=False)
    acts, mems, gtok, gmem, dw, small = run_layer(
        ends, half.reshape(1).astype(jnp.int32),
        one_stream(tokens), lax.dynamic_index_in_dim(memory_start, stream, 0, keepdims=False),
        one_stream(out_cotangent), one_stream(memory_cotangent),
        attn_weights.reshape(12, D, D), ffn_in, ffn_out, gains, forget_w.reshape(1, D), forget_bias.reshape(SLOTS, 1),
    )

    def both_streams(value):
        parts = value.reshape(NSEG, -1, D)
        return lax.all_to_all(parts, "seg", 0, 0)[:2]

    acts, mems, gtok, gmem = (both_streams(v) for v in (acts, mems, gtok, gmem))
    whole = jnp.stack([jnp.where(half == i, dw, 0) for i in range(2)], 1)
    whole, small = lax.psum((whole, jnp.where(half == 0, small, 0)), ("seg", "doc"))
    whole = whole.astype(f32)
    grad_attn = whole[:12].reshape(3, 4, D, D)
    grad_in = whole[12:16].transpose(1, 2, 0, 3).reshape(D, FF)
    grad_out = whole[16:20].transpose(1, 0, 2, 3).reshape(FF, D)
    return (
        acts, mems, gtok.astype(f32), gmem.astype(f32), grad_attn, grad_in, grad_out,
        small[1:6], small[0], small[8:72, 0],
    )


def solution(mesh):
    return jax.shard_map(
        body,
        mesh=mesh,
        in_specs=(
            P("doc", "seg", None), P("doc", None, None), P("doc", None), P(), P(), P(), P(), P(), P(),
            P("doc", "seg", None), P("doc", "seg", None),
        ),
        out_specs=(
            P("doc", "seg", None), P("doc", "seg", None), P("doc", "seg", None), P("doc", "seg", None),
            P(), P(), P(), P(), P(), P(),
        ),
        check_vma=False,
    )
```

```python
import functools

import jax
import jax.numpy as jnp
from jax import lax
from jax.experimental import pallas as pl
from jax.experimental.pallas import tpu as pltpu
from jax.sharding import PartitionSpec as P

HEADS = 8
NDOC = 8
D = 512
FF = 2048
SLOTS = 64
SEG = 128
NSEG = 4
ROWS = NSEG * SEG
MROWS = NSEG * SLOTS
PAIRS = 4
PAIR = 128
FCHUNK = 512
BLOCK = 256
NBLOCKS = 20
LANES = 128
LANE_CUTS = D // LANES
FLAT = NBLOCKS * BLOCK * LANE_CUTS
MESH = pl.DeviceIdType.MESH

f32 = jnp.float32
bf16 = jnp.bfloat16


def dot(a, b):
    return lax.dot_general(a, b, (((1,), (0,)), ((), ())), preferred_element_type=f32)


def dot_nt(a, b):
    return lax.dot_general(a, b, (((1,), (1,)), ((), ())), preferred_element_type=f32)


def dot_tn(a, b):
    return lax.dot_general(a, b, (((0,), (0,)), ((), ())), preferred_element_type=f32)


def norm_stats(values):
    centered = values - jnp.mean(values, -1, keepdims=True)
    rstd = lax.rsqrt(jnp.mean(centered * centered, -1, keepdims=True) + 1e-05)
    return centered * rstd, rstd


def norm_back(grad, gain, xhat, rstd):
    scaled = grad * gain
    mean_one = jnp.mean(scaled, -1, keepdims=True)
    mean_two = jnp.mean(scaled * xhat, -1, keepdims=True)
    return rstd * (scaled - mean_one - xhat * mean_two)


def head_halves(values):
    low_half = lax.broadcasted_iota(jnp.int32, values.shape, 1) % PAIR < PAIR // 2
    return jnp.where(low_half, values, 0.0).astype(bf16), jnp.where(low_half, 0.0, values).astype(bf16)


def join_halves(stacked):
    rows = stacked.shape[0] // 2
    low_half = lax.broadcasted_iota(jnp.int32, (rows, PAIR), 1) < PAIR // 2
    return jnp.where(low_half, stacked[:rows], stacked[rows:])


def softmax_rows(scores):
    expd = jnp.exp(scores - jnp.max(scores, -1, keepdims=True))
    return expd * (1.0 / jnp.sum(expd, -1, keepdims=True))


def softmax_back(probs, grad):
    return probs * (grad - jnp.sum(probs * grad, -1, keepdims=True))


def gelu_both(u):
    square = u * u
    tanh = jnp.tanh(0.7978845608028654 * u * (1.0 + 0.044715 * square))
    half = 0.5 + 0.5 * tanh
    slope = half + u * half * (1.0 - tanh) * (0.7978845608028654 + 0.1070322243 * square)
    return u * half, slope


def layer_kernel(
    half_ref, len_ref,
    tok_ref, mem_ref, ocot_ref, mcot_ref, attn_ref, win_ref, wout_ref, gains_ref, fw_ref, fb_ref,
    act_ref, mout_ref, gtok_ref, gmem_ref, dw_ref, small_ref,
    h_s, q_s, k_s, v_s, p_s, o_s, xh0_s, rs0_s,
    res_s, n1_s, xh1_s, rs1_s, cq_s, ck_s, cv_s, cp_s, co_s,
    n2_s, xh2_s, rs2_s, hid_s, gd_s,
    t_s, xh3_s, rs3_s, m_s, xh4_s, rs4_s, mlow_s, gate_s, upd_s, mprev_s,
    wq_s, wk_s, wv_s, wp_s, wo_s,
    gup_s, dwq_s, dwk_s, dwv_s, gyl_s, gul_s, gbl_s, dcq_s, dck_s, dcv_s,
    gb_s, gal_s, dq_s, dk_s, dv_s, gain_s, gm_s, bias_s,
):
    gain = [gains_ref[i : i + 1, :] for i in range(5)]

    def doc_ids(shape, dim, base):
        pos = lax.broadcasted_iota(jnp.int32, shape, dim) + base
        ids = jnp.zeros(shape, jnp.int32)
        end = jnp.zeros((1, 1), jnp.int32)
        for j in range(NDOC):
            end += len_ref[0:1, j : j + 1]
            ids += (end <= pos).astype(jnp.int32)
        return ids

    xhat, rstd = norm_stats(tok_ref[...].astype(f32))
    xh0_s[...] = xhat
    rs0_s[...] = rstd
    h = (xhat * gain[0]).astype(bf16)
    h_s[...] = h
    q_s[0], q_s[1] = head_halves(dot(h, attn_ref[0]) * 0.125)
    k_s[...] = dot(h, attn_ref[1]).astype(bf16)
    v_s[...] = dot(h, attn_ref[2]).astype(bf16)

    def self_forward(seg, carry):
        rows = pl.ds(pl.multiple_of(seg * SEG, SEG), SEG)
        same = doc_ids((SEG, SEG), 0, seg * SEG) == doc_ids((SEG, SEG), 1, seg * SEG)
        same = jnp.concatenate([same.astype(jnp.int32)] * 2, 0) > 0
        for pair in range(PAIRS):
            lanes = slice(pair * PAIR, (pair + 1) * PAIR)
            q_both = jnp.concatenate([q_s[0, rows, lanes], q_s[1, rows, lanes]], 0)
            scores = jnp.where(same, dot_nt(q_both, k_s[rows, lanes]), -1e30)
            probs = softmax_rows(scores).astype(bf16)
            p_s[seg, pair] = probs
            o_s[rows, lanes] = join_halves(dot(probs, v_s[rows, lanes])).astype(bf16)
        return carry

    lax.fori_loop(0, NSEG, self_forward, 0)
    res = tok_ref[...].astype(f32) + dot(o_s[...], attn_ref[3])
    res_s[...] = res
    xhat, rstd = norm_stats(res)
    xh1_s[...] = xhat
    rs1_s[...] = rstd
    n1 = (xhat * gain[1]).astype(bf16)
    n1_s[...] = n1
    cq_s[0], cq_s[1] = head_halves(dot(n1, attn_ref[4]) * 0.125)

    mprev_s[...] = mem_ref[...].astype(f32)

    def forward(seg, carry):
        rows = pl.ds(pl.multiple_of(seg * SEG, SEG), SEG)
        slots = pl.ds(pl.multiple_of(seg * SLOTS, SLOTS), SLOTS)
        mem = mprev_s[...]
        xhat, rstd = norm_stats(mem)
        xh4_s[slots, :] = xhat
        rs4_s[slots, :] = rstd
        m = xhat * gain[4]
        mlow = m.astype(bf16)
        mlow_s[slots, :] = mlow
        gate = jax.nn.sigmoid(jnp.sum(m * fw_ref[...], -1, keepdims=True) + fb_ref[...])
        gate_s[slots, :] = gate
        ck = dot(mlow, attn_ref[5]).astype(bf16)
        cv = dot(mlow, attn_ref[6]).astype(bf16)
        ck_s[slots, :] = ck
        cv_s[slots, :] = cv
        wq0, wq1 = head_halves(dot(mlow, attn_ref[8]) * 0.125)
        wq_s[0, slots, :] = wq0
        wq_s[1, slots, :] = wq1
        for pair in range(PAIRS):
            lanes = slice(pair * PAIR, (pair + 1) * PAIR)
            q_both = jnp.concatenate([cq_s[0, rows, lanes], cq_s[1, rows, lanes]], 0)
            probs = softmax_rows(dot_nt(q_both, ck[:, lanes])).astype(bf16)
            cp_s[seg, pair] = probs
            co_s[rows, lanes] = join_halves(dot(probs, cv[:, lanes])).astype(bf16)
        res = res_s[rows, :] + dot(co_s[rows, :], attn_ref[7])
        xhat, rstd = norm_stats(res)
        xh2_s[rows, :] = xhat
        rs2_s[rows, :] = rstd
        n2 = (xhat * gain[2]).astype(bf16)
        n2_s[rows, :] = n2
        for c in range(0, FF, FCHUNK):
            hid, slope = gelu_both(dot(n2, win_ref[:, c : c + FCHUNK]))
            hid = hid.astype(bf16)
            hid_s[rows, c : c + FCHUNK] = hid
            gd_s[rows, c : c + FCHUNK] = slope.astype(bf16)
            res = res + dot(hid, wout_ref[c : c + FCHUNK, :])
        act_ref[rows, :] = res.astype(bf16)
        xhat, rstd = norm_stats(res)
        xh3_s[rows, :] = xhat
        rs3_s[rows, :] = rstd
        t = (xhat * gain[3]).astype(bf16)
        t_s[rows, :] = t
        wk = dot(t, attn_ref[9]).astype(bf16)
        wv = dot(t, attn_ref[10]).astype(bf16)
        wk_s[rows, :] = wk
        wv_s[rows, :] = wv
        live = doc_ids((2 * SLOTS, SEG), 1, seg * SEG) < NDOC
        for pair in range(PAIRS):
            lanes = slice(pair * PAIR, (pair + 1) * PAIR)
            q_both = jnp.concatenate([wq0[:, lanes], wq1[:, lanes]], 0)
            scores = jnp.where(live, dot_nt(q_both, wk[:, lanes]), -1e30)
            probs = softmax_rows(scores).astype(bf16)
            wp_s[seg, pair] = probs
            wo_s[slots, lanes] = join_halves(dot(probs, wv[:, lanes])).astype(bf16)
        update = dot(wo_s[slots, :], attn_ref[11])
        upd_s[slots, :] = mem - update
        fresh = (update + gate * (mem - update)).astype(bf16)
        mout_ref[slots, :] = fresh
        mprev_s[...] = fresh.astype(f32)
        return carry

    lax.fori_loop(0, NSEG, forward, 0)

    gm_s[...] = jnp.zeros_like(gm_s)
    gain_s[...] = jnp.zeros_like(gain_s)
    small_ref[...] = jnp.zeros_like(small_ref)
    bias_s[...] = jnp.zeros_like(bias_s)

    def backward(step, carry):
        seg = NSEG - 1 - step
        rows = pl.ds(pl.multiple_of(seg * SEG, SEG), SEG)
        slots = pl.ds(pl.multiple_of(seg * SLOTS, SLOTS), SLOTS)
        gz = (mcot_ref[slots, :].astype(f32) + gm_s[...]).astype(bf16).astype(f32)
        gate = gate_s[slots, :]
        dgate = jnp.sum(gz * upd_s[slots, :], -1, keepdims=True) * gate * (1.0 - gate)
        gup = ((1.0 - gate) * gz).astype(bf16)
        gup_s[slots, :] = gup
        xh4 = xh4_s[slots, :]
        small_ref[0:1, :] += jnp.sum(dgate * (xh4 * gain[4]), 0, keepdims=True)
        bias_s[...] += jnp.broadcast_to(dgate, (SLOTS, LANES))
        gm = dgate * fw_ref[...]
        g_o0, g_o1 = head_halves(dot_nt(gup, attn_ref[11]))
        for pair in range(PAIRS):
            lanes = slice(pair * PAIR, (pair + 1) * PAIR)
            probs = wp_s[seg, pair]
            g_both = jnp.concatenate([g_o0[:, lanes], g_o1[:, lanes]], 0)
            q_both = jnp.concatenate([wq_s[0, slots, lanes], wq_s[1, slots, lanes]], 0)
            ds = softmax_back(probs.astype(f32), dot_nt(g_both, wv_s[rows, lanes])).astype(bf16)
            dwv_s[rows, lanes] = dot_tn(probs, g_both).astype(bf16)
            dwk_s[rows, lanes] = dot_tn(ds, q_both).astype(bf16)
            dwq_s[slots, lanes] = (join_halves(dot(ds, wk_s[rows, lanes])) * 0.125).astype(bf16)
        gm = gm + dot_nt(dwq_s[slots, :], attn_ref[8])
        gt = dot_nt(dwk_s[rows, :], attn_ref[9]) + dot_nt(dwv_s[rows, :], attn_ref[10])
        xhat = xh3_s[rows, :]
        gain_s[3:4, :] += jnp.sum(gt * xhat, 0, keepdims=True)
        gy = ocot_ref[rows, :].astype(f32) + norm_back(gt, gain[3], xhat, rs3_s[rows, :])
        gyl = gy.astype(bf16)
        gyl_s[rows, :] = gyl
        gn2 = jnp.zeros((SEG, D), f32)
        for c in range(0, FF, FCHUNK):
            ghid = dot_nt(gyl, wout_ref[c : c + FCHUNK, :])
            gul = (ghid * gd_s[rows, c : c + FCHUNK].astype(f32)).astype(bf16)
            gul_s[rows, c : c + FCHUNK] = gul
            gn2 = gn2 + dot_nt(gul, win_ref[:, c : c + FCHUNK])
        xhat = xh2_s[rows, :]
        gain_s[2:3, :] += jnp.sum(gn2 * xhat, 0, keepdims=True)
        gb = gy + norm_back(gn2, gain[2], xhat, rs2_s[rows, :])
        gb_s[rows, :] = gb
        gbl = gb.astype(bf16)
        gbl_s[rows, :] = gbl
        g_o0, g_o1 = head_halves(dot_nt(gbl, attn_ref[7]))
        for pair in range(PAIRS):
            lanes = slice(pair * PAIR, (pair + 1) * PAIR)
            probs = cp_s[seg, pair]
            g_both = jnp.concatenate([g_o0[:, lanes], g_o1[:, lanes]], 0)
            q_both = jnp.concatenate([cq_s[0, rows, lanes], cq_s[1, rows, lanes]], 0)
            ds = softmax_back(probs.astype(f32), dot_nt(g_both, cv_s[slots, lanes])).astype(bf16)
            dcv_s[slots, lanes] = dot_tn(probs, g_both).astype(bf16)
            dck_s[slots, lanes] = dot_tn(ds, q_both).astype(bf16)
            dcq_s[rows, lanes] = (join_halves(dot(ds, ck_s[slots, lanes])) * 0.125).astype(bf16)
        gm = gm + dot_nt(dck_s[slots, :], attn_ref[5]) + dot_nt(dcv_s[slots, :], attn_ref[6])
        gain_s[4:5, :] += jnp.sum(gm * xh4, 0, keepdims=True)
        gmem = gate * gz + norm_back(gm, gain[4], xh4, rs4_s[slots, :])
        gmem = gmem.astype(bf16)
        gmem_ref[slots, :] = gmem
        gm_s[...] = gmem.astype(f32)
        return carry

    lax.fori_loop(0, NSEG, backward, 0)

    gn1 = dot_nt(dcq_s[...], attn_ref[4])
    xhat = xh1_s[...]
    gain_s[1:2, :] = jnp.sum(gn1 * xhat, 0, keepdims=True)
    ga = gb_s[...] + norm_back(gn1, gain[1], xhat, rs1_s[...])
    gb_s[...] = ga
    gal = ga.astype(bf16)
    gal_s[...] = gal
    g0, g1 = head_halves(dot_nt(gal, attn_ref[3]))
    cq_s[0] = g0
    cq_s[1] = g1

    def self_backward(seg, carry):
        rows = pl.ds(pl.multiple_of(seg * SEG, SEG), SEG)
        for pair in range(PAIRS):
            lanes = slice(pair * PAIR, (pair + 1) * PAIR)
            probs = p_s[seg, pair]
            g_both = jnp.concatenate([cq_s[0, rows, lanes], cq_s[1, rows, lanes]], 0)
            q_both = jnp.concatenate([q_s[0, rows, lanes], q_s[1, rows, lanes]], 0)
            ds = softmax_back(probs.astype(f32), dot_nt(g_both, v_s[rows, lanes])).astype(bf16)
            dv_s[rows, lanes] = dot_tn(probs, g_both).astype(bf16)
            dk_s[rows, lanes] = dot_tn(ds, q_both).astype(bf16)
            dq_s[rows, lanes] = (join_halves(dot(ds, k_s[rows, lanes])) * 0.125).astype(bf16)
        return carry

    lax.fori_loop(0, NSEG, self_backward, 0)
    gh = dot_nt(dq_s[...], attn_ref[0]) + dot_nt(dk_s[...], attn_ref[1]) + dot_nt(dv_s[...], attn_ref[2])
    xhat = xh0_s[...]
    gain_s[0:1, :] = jnp.sum(gh * xhat, 0, keepdims=True)
    gtok_ref[...] = (gb_s[...] + norm_back(gh, gain[0], xhat, rs0_s[...])).astype(bf16)
    small_ref[1:6, :] = gain_s[0:5, :]
    small_ref[6:7, 0:SLOTS] = jnp.transpose(bias_s[...])[0:1, :]

    half = half_ref[0]
    cut = pl.ds(pl.multiple_of(half * BLOCK, BLOCK), BLOCK)
    pairs = [
        (h_s, dq_s), (h_s, dk_s), (h_s, dv_s), (o_s, gal_s),
        (n1_s, dcq_s), (mlow_s, dck_s), (mlow_s, dcv_s), (co_s, gbl_s),
        (mlow_s, dwq_s), (t_s, dwk_s), (t_s, dwv_s), (wo_s, gup_s),
    ]

    def put(i, value):
        value = value.astype(bf16)
        for j in range(LANE_CUTS):
            dw_ref[i, j] = value[:, j * LANES : (j + 1) * LANES]

    for i, (left, right) in enumerate(pairs):
        put(i, dot_tn(left[:, cut], right[...]))
    for i in range(4):
        put(12 + i, dot_tn(n2_s[:, cut], gul_s[:, i * D : (i + 1) * D]))
    for i in range(4):
        cut_i = pl.ds(pl.multiple_of(half * 4 * BLOCK + i * BLOCK, BLOCK), BLOCK)
        put(16 + i, dot_tn(hid_s[:, cut_i], gyl_s[...]))


def run_layer(half, lens, tok, mem, ocot, mcot, attn, win, wout, gains, fw, fb):
    def rows(dtype=bf16, width=D):
        return pltpu.VMEM((ROWS, width), dtype)

    def slots(dtype=bf16, width=D):
        return pltpu.VMEM((MROWS, width), dtype)

    def two(count):
        return pltpu.VMEM((2, count, D), bf16)

    scratch = [
        rows(), two(ROWS), rows(), rows(), pltpu.VMEM((NSEG, PAIRS, 2 * SEG, SEG), bf16), rows(),
        rows(f32), rows(f32, 1),
        rows(f32), rows(), rows(f32), rows(f32, 1), two(ROWS), slots(), slots(),
        pltpu.VMEM((NSEG, PAIRS, 2 * SEG, SLOTS), bf16), rows(),
        rows(), rows(f32), rows(f32, 1), rows(bf16, FF), rows(bf16, FF),
        rows(), rows(f32), rows(f32, 1), slots(f32), slots(f32), slots(f32, 1), slots(), slots(f32, 1),
        slots(f32), pltpu.VMEM((SLOTS, D), f32),
        two(MROWS), rows(), rows(), pltpu.VMEM((NSEG, PAIRS, 2 * SLOTS, SEG), bf16), slots(),
        slots(), slots(), rows(), rows(), rows(), rows(bf16, FF), rows(), rows(), slots(), slots(),
        rows(f32), rows(), rows(), rows(), rows(), pltpu.VMEM((8, D), f32), pltpu.VMEM((SLOTS, D), f32),
        pltpu.VMEM((SLOTS, LANES), f32),
    ]
    smem = pl.BlockSpec(memory_space=pltpu.SMEM)
    vmem = pl.BlockSpec(memory_space=pltpu.VMEM)
    return pl.pallas_call(
        layer_kernel,
        out_shape=(
            jax.ShapeDtypeStruct((ROWS, D), bf16),
            jax.ShapeDtypeStruct((MROWS, D), bf16),
            jax.ShapeDtypeStruct((ROWS, D), bf16),
            jax.ShapeDtypeStruct((MROWS, D), bf16),
            jax.ShapeDtypeStruct((NBLOCKS, LANE_CUTS, BLOCK, LANES), bf16),
            jax.ShapeDtypeStruct((8, D), f32),
        ),
        in_specs=[smem] + [vmem] * 11,
        out_specs=[vmem] * 6,
        scratch_shapes=scratch,
        compiler_params=pltpu.CompilerParams(vmem_limit_bytes=60 << 20),
        name="layer",
    )(half, lens, tok, mem, ocot, mcot, attn, win, wout, gains, fw, fb)


def my_place():
    doc = lax.axis_index("doc")
    return lax.axis_index("seg"), doc // 8, (doc // 2) % 4, doc % 2


def device_at(x, y, z, core):
    return (x, y * 8 + z * 2 + core)


def remote(src, dst, send_sem, recv_sem, device):
    return pltpu.make_async_remote_copy(
        src_ref=src, dst_ref=dst, send_sem=send_sem, recv_sem=recv_sem, device_id=device, device_id_type=MESH
    )


def signal(sem, device):
    pl.semaphore_signal(sem, inc=1, device_id=device, device_id_type=MESH)


def gather_kernel(
    tok_ref, ocot_ref, mcot_ref, mem_ref, len_ref,
    tok_out, ocot_out, mcot_out, mem_out, len_out,
    send_sem, recv_sem, local_sem,
):
    x, y, z, core = my_place()
    owner, stream = x // 2, x % 2
    barrier = pltpu.get_barrier_semaphore()
    own = (owner == core).astype(jnp.int32)
    for src in range(NSEG):

        @pl.when(jnp.logical_or(src != x, owner != core))
        def _():
            signal(barrier, device_at(src, y, z, owner))

    pl.semaphore_wait(barrier, 4 - own)

    def copies(src_stream, seg):
        return [
            (tok_ref.at[src_stream], tok_out.at[seg]),
            (ocot_ref.at[src_stream], ocot_out.at[seg]),
            (mcot_ref.at[src_stream], mcot_out.at[seg]),
        ]

    for s in range(2):
        for to_core in range(2):
            chip = 2 * core + s
            here = jnp.logical_and(chip == x, core == to_core)
            for i, (src, dst) in enumerate(copies(s, x)):

                @pl.when(jnp.logical_not(here))
                def _():
                    remote(src, dst, send_sem.at[s, to_core, i], recv_sem.at[x, i], device_at(chip, y, z, to_core)).start()

                @pl.when(here)
                def _():
                    pltpu.make_async_copy(src, dst, local_sem.at[i]).start()

    for i, (src, dst) in enumerate([(mem_ref, mem_out), (len_ref, len_out)]):

        @pl.when(owner == core)
        def _():
            copy = remote(src.at[stream], dst, send_sem.at[2, 0, i], recv_sem.at[4, i], device_at(x, y, z, 1 - core))
            copy.start()
            local = pltpu.make_async_copy(src.at[stream], dst, local_sem.at[3 + i])
            local.start()
            local.wait()
            copy.wait_send()

        @pl.when(owner != core)
        def _():
            remote(src.at[stream], dst, send_sem.at[2, 0, i], recv_sem.at[4, i], device_at(x, y, z, 1 - core)).wait_recv()

    for s in range(2):
        for to_core in range(2):
            chip = 2 * core + s
            here = jnp.logical_and(chip == x, core == to_core)
            for i, (src, dst) in enumerate(copies(s, x)):

                @pl.when(jnp.logical_not(here))
                def _():
                    remote(src, dst, send_sem.at[s, to_core, i], recv_sem.at[x, i], device_at(chip, y, z, to_core)).wait_send()

                @pl.when(here)
                def _():
                    pltpu.make_async_copy(src, dst, local_sem.at[i]).wait()

    for seg in range(NSEG):
        for i, (src, dst) in enumerate(copies(0, seg)):

            @pl.when(jnp.logical_or(seg != x, owner != core))
            def _():
                remote(src, dst, send_sem.at[0, 0, i], recv_sem.at[seg, i], device_at(seg, y, z, owner)).wait_recv()


def run_gather(tok, ocot, mcot, mem, lens):
    hbm = pl.BlockSpec(memory_space=pl.ANY)
    return pl.pallas_call(
        gather_kernel,
        out_shape=(
            jax.ShapeDtypeStruct((NSEG, SEG, D), bf16),
            jax.ShapeDtypeStruct((NSEG, SEG, D), bf16),
            jax.ShapeDtypeStruct((NSEG, SLOTS, D), bf16),
            jax.ShapeDtypeStruct((SLOTS, D), bf16),
            jax.ShapeDtypeStruct((8, LANES), jnp.int32),
        ),
        in_specs=[hbm] * 5,
        out_specs=[hbm] * 5,
        scratch_shapes=[
            pltpu.SemaphoreType.DMA((3, 2, 3)),
            pltpu.SemaphoreType.DMA((5, 3)),
            pltpu.SemaphoreType.DMA((5,)),
        ],
        compiler_params=pltpu.CompilerParams(collective_id=1, has_side_effects=True),
        name="gather_stream",
    )(tok, ocot, mcot, mem, lens)


CHUNKS = ((3, 4, 3), (3, 3, 4))
UNIT = 16


def reduce_kernel(
    dw_ref, act_ref, mout_ref, gtok_ref, gmem_ref, small_ref,
    full_ref, act_out, mout_out, gtok_out, gmem_out, small_out,
    near_s, far_s, e_s, f_s, sums_s,
    send_sem, recv_sem, out_send, out_recv, small_send, small_recv, local_sem,
):
    place = my_place()
    x, y, z, core = place
    owner, stream = x // 2, x % 2
    sibling = device_at(x, y, z, 1 - core)
    barrier = pltpu.get_barrier_semaphore()

    def along(axis, coordinate):
        there = list(place)
        there[axis] = coordinate
        return device_at(*there)

    for axis in range(3):
        for step in range(1, 4):
            signal(barrier, along(axis, (place[axis] + step) % 4))
    signal(barrier, sibling)
    for k in range(2):

        @pl.when(jnp.logical_or(2 * core + k != x, owner != core))
        def _():
            signal(barrier, device_at(2 * core + k, y, z, owner))

    pl.semaphore_wait(barrier, 12 - (owner == core).astype(jnp.int32))

    def rows(start, count):
        return pl.ds(pl.multiple_of(start, UNIT), count)

    def result_copies(k):
        seg = 2 * core + k
        return [
            (act_ref.at[rows(seg * SEG, SEG)], act_out),
            (mout_ref.at[rows(seg * SLOTS, SLOTS)], mout_out),
            (gtok_ref.at[rows(seg * SEG, SEG)], gtok_out),
            (gmem_ref.at[rows(seg * SLOTS, SLOTS)], gmem_out),
        ]

    def results(do):
        for k in range(2):
            here = jnp.logical_and(2 * core + k == x, owner == core)
            peer = device_at(2 * core + k, y, z, owner)
            for i, (src, dst) in enumerate(result_copies(k)):

                @pl.when(jnp.logical_not(here))
                def _():
                    do(
                        remote(src, dst.at[stream], out_send.at[k, i], out_recv.at[stream, i], peer),
                        remote(src, dst.at[k], out_send.at[k, i], out_recv.at[k, i], peer),
                    )

                @pl.when(here)
                def _():
                    do(pltpu.make_async_copy(src, dst.at[stream], local_sem.at[i]), None)

    def small_copies(axis):
        src = small_ref if axis == 0 else sums_s.at[axis - 1, 4]
        here = place[axis]
        return [
            remote(
                src, sums_s.at[axis, here], small_send.at[axis, step - 1], small_recv.at[axis, step - 1],
                along(axis, (here + step) % 4),
            )
            for step in range(1, 4)
        ]

    def small_start(axis):
        sums_s[axis, place[axis]] = small_ref[...] if axis == 0 else sums_s[axis - 1, 4]
        for copy in small_copies(axis):
            copy.start()

    def small_finish(axis):
        for copy in small_copies(axis):
            copy.wait()
        total = (sums_s[axis, 0] + sums_s[axis, 1]) + (sums_s[axis, 2] + sums_s[axis, 3])
        sums_s[axis, 4] = total
        if axis == 2:
            small_out[...] = total

    def part_steps(chunk, part):
        r = CHUNKS[chunk][part] * UNIT
        base = 64 * UNIT * (sum(sum(c) for c in CHUNKS[:chunk]) + sum(CHUNKS[chunk][:part]))
        axes = [(part + i) % 3 for i in range(3)]
        i1, i2, i3 = (place[a] for a in axes)
        right, left = along(axes[0], (i1 + 1) % 4), along(axes[0], (i1 + 3) % 4)
        sems = iter(range(40))
        near, far, mid, low_ = near_s[chunk][part], far_s[chunk][part], e_s[chunk][part], f_s[chunk][part]

        def copy(src, dst, device):
            i = next(sems)
            return remote(src, dst, send_sem.at[chunk, part, i], recv_sem.at[chunk, part, i], device)

        def block(b, first=0, count=16):
            return rows(base + (b % 4) * 16 * r + first * r, count * r)

        def add(refs):
            total = refs[0][...].astype(f32)
            for ref in refs[1:]:
                total += ref[...].astype(f32)
            return total.astype(bf16)

        half0, half1 = pl.ds(0, 8 * r), pl.ds(8 * r, 8 * r)
        a = copy(dw_ref.at[block(i1 + 2, 0, 8)], near.at[0], right)
        b = copy(dw_ref.at[block(i1 + 2, 8, 8)], near.at[1], left)
        c1 = copy(dw_ref.at[block(i1 + 1, 8, 8)], far.at[0, half1], right)
        d0 = copy(dw_ref.at[block(i1 + 3, 0, 8)], far.at[1, half0], left)
        for one in (a, b, c1, d0):
            one.start()
        yield
        a.wait()
        near[0] = add([near.at[0], dw_ref.at[block(i1 + 1, 0, 8)]])
        c0 = copy(near.at[0], far.at[0, half0], right)
        c0.start()
        b.wait()
        near[1] = add([near.at[1], dw_ref.at[block(i1 + 3, 8, 8)]])
        d1 = copy(near.at[1], far.at[1, half1], left)
        d1.start()
        yield
        for one in (c1, d0, c0, d1):
            one.wait()
        far[0] = add([far.at[0], far.at[1], dw_ref.at[block(i1)]])
        two = [
            copy(far.at[0, rows((i2 + s) % 4 * 4 * r, 4 * r)], mid.at[s - 1], along(axes[1], (i2 + s) % 4))
            for s in range(1, 4)
        ]
        for one in two:
            one.start()
        yield
        for one in two:
            one.wait()
        mid[0] = add([mid.at[0], mid.at[1], mid.at[2], far.at[0, rows(i2 * 4 * r, 4 * r)]])
        three = [
            copy(mid.at[0, rows((i3 + s) % 4 * r, r)], low_.at[s - 1], along(axes[2], (i3 + s) % 4))
            for s in range(1, 4)
        ]
        for one in three:
            one.start()
        yield
        for one in three:
            one.wait()
        mine = full_ref.at[core]
        home = block(i1, i2 * 4 + i3, 1)
        mine[home, :] = add([low_.at[0], low_.at[1], low_.at[2], mid.at[0, rows(i3 * r, r)]])
        back = [copy(mine.at[home], mine.at[home], along(axes[2], (i3 + s) % 4)) for s in range(1, 4)]
        for one in back:
            one.start()
        yield
        for one in back:
            one.wait()
        home = block(i1, i2 * 4, 4)
        back = [copy(mine.at[home], mine.at[home], along(axes[1], (i2 + s) % 4)) for s in range(1, 4)]
        for one in back:
            one.start()
        yield
        for one in back:
            one.wait()
        home = block(i1)
        to_right = copy(mine.at[home], mine.at[home], right)
        to_left = copy(mine.at[home], mine.at[home], left)
        over = [copy(mine.at[home], mine.at[home], sibling)]
        for one in (to_right, to_left, over[0]):
            one.start()
        yield
        to_right.wait()
        from_left = block(i1 + 3)
        on_right = copy(mine.at[block(i1 + 3, 0, 8)], mine.at[block(i1 + 3, 0, 8)], right)
        on_right.start()
        over.append(copy(mine.at[from_left], mine.at[from_left], sibling))
        over[-1].start()
        to_left.wait()
        from_right = block(i1 + 1)
        on_left = copy(mine.at[block(i1 + 1, 8, 8)], mine.at[block(i1 + 1, 8, 8)], left)
        on_left.start()
        over.append(copy(mine.at[from_right], mine.at[from_right], sibling))
        over[-1].start()
        yield
        on_right.wait()
        on_left.wait()
        opposite = block(i1 + 2)
        over.append(copy(mine.at[opposite], mine.at[opposite], sibling))
        over[-1].start()
        yield
        for one in over:
            one.wait()
        yield

    def chunk_steps(chunk):
        parts = [part_steps(chunk, part) for part in range(3)]
        for _ in range(10):
            for part in parts:
                next(part)
            yield

    first, second = chunk_steps(0), chunk_steps(1)
    next(first)
    results(lambda copy, back: copy.start())
    small_start(0)
    next(first)
    next(second)
    next(first)
    small_finish(0)
    small_start(1)
    next(second)
    next(first)
    small_finish(1)
    small_start(2)
    next(second)
    next(first)
    small_finish(2)
    for _ in range(5):
        next(second)
        next(first)
    next(second)
    next(second)

    def finish(copy, back):
        if back is None:
            copy.wait()
        else:
            copy.wait_send()
            back.wait_recv()

    results(finish)


def run_reduce(dw, acts, mems, gtok, gmem, small):
    vmem = pl.BlockSpec(memory_space=pltpu.VMEM)
    hbm = pl.BlockSpec(memory_space=pl.ANY)

    def buffers(*shape_of):
        return [[pltpu.VMEM(shape_of[0](count * UNIT), bf16) for count in chunk] for chunk in CHUNKS]

    return pl.pallas_call(
        reduce_kernel,
        out_shape=(
            jax.ShapeDtypeStruct((2, FLAT, LANES), bf16),
            jax.ShapeDtypeStruct((2, SEG, D), bf16),
            jax.ShapeDtypeStruct((2, SLOTS, D), bf16),
            jax.ShapeDtypeStruct((2, SEG, D), bf16),
            jax.ShapeDtypeStruct((2, SLOTS, D), bf16),
            jax.ShapeDtypeStruct((8, D), f32),
        ),
        in_specs=[vmem] + [hbm] * 4 + [vmem],
        out_specs=[vmem] + [hbm] * 4 + [vmem],
        scratch_shapes=[
            buffers(lambda r: (2, 8 * r, LANES)),
            buffers(lambda r: (2, 16 * r, LANES)),
            buffers(lambda r: (3, 4 * r, LANES)),
            buffers(lambda r: (3, r, LANES)),
            pltpu.VMEM((3, 5, 8, D), f32),
            pltpu.SemaphoreType.DMA((2, 3, 32)),
            pltpu.SemaphoreType.DMA((2, 3, 32)),
            pltpu.SemaphoreType.DMA((2, 4)),
            pltpu.SemaphoreType.DMA((2, 4)),
            pltpu.SemaphoreType.DMA((3, 3)),
            pltpu.SemaphoreType.DMA((3, 3)),
            pltpu.SemaphoreType.DMA((4,)),
        ],
        compiler_params=pltpu.CompilerParams(collective_id=2, has_side_effects=True, vmem_limit_bytes=60 << 20),
        name="reduce_gradients",
    )(dw, acts, mems, gtok, gmem, small)


def widen_kernel(full_ref, attn_ref, in_ref, out_ref, full_s, wide_s, load_sem, store_sem):
    def load(i):
        return [
            pltpu.make_async_copy(full_ref.at[half, i], full_s.at[i, half], load_sem.at[i, half]) for half in range(2)
        ]

    def target(i, half):
        if i < 12:
            return attn_ref.at[i, pl.ds(half * BLOCK, BLOCK), :]
        if i < 16:
            return in_ref.at[pl.ds(half * BLOCK, BLOCK), pl.ds((i - 12) * D, D)]
        return out_ref.at[pl.ds(half * 4 * BLOCK + (i - 16) * BLOCK, BLOCK), :]

    def store(i, half):
        return pltpu.make_async_copy(wide_s.at[i, half], target(i, half), store_sem.at[i, half])

    for i in range(NBLOCKS):
        for copy in load(i):
            copy.start()
    for i in range(NBLOCKS):
        for half, copy in enumerate(load(i)):
            copy.wait()
            for j in range(LANE_CUTS):
                wide_s[i, half, :, j * LANES : (j + 1) * LANES] = full_s[i, half, j].astype(f32)
            store(i, half).start()
    for i in range(NBLOCKS):
        for half in range(2):
            store(i, half).wait()


def run_widen(full):
    hbm = pl.BlockSpec(memory_space=pl.ANY)
    return pl.pallas_call(
        widen_kernel,
        out_shape=(
            jax.ShapeDtypeStruct((12, D, D), f32),
            jax.ShapeDtypeStruct((D, FF), f32),
            jax.ShapeDtypeStruct((FF, D), f32),
        ),
        in_specs=[hbm],
        out_specs=[hbm] * 3,
        scratch_shapes=[
            pltpu.VMEM((NBLOCKS, 2, LANE_CUTS, BLOCK, LANES), bf16),
            pltpu.VMEM((NBLOCKS, 2, BLOCK, D), f32),
            pltpu.SemaphoreType.DMA((NBLOCKS, 2)),
            pltpu.SemaphoreType.DMA((NBLOCKS, 2)),
        ],
        compiler_params=pltpu.CompilerParams(vmem_limit_bytes=60 << 20),
        name="widen_gradients",
    )(full)


def body(
    tokens, memory_start, doc_lengths, attn_weights, ffn_in, ffn_out, gains, forget_w, forget_bias,
    out_cotangent, memory_cotangent,
):
    lens = jnp.broadcast_to(jnp.pad(doc_lengths, ((0, 0), (0, LANES - NDOC)))[:, None, :], (2, 8, LANES))
    tok, ocot, mcot, mem, lens = run_gather(tokens, out_cotangent, memory_cotangent, memory_start, lens)
    half = (lax.axis_index("doc") % 2).reshape(1).astype(jnp.int32)
    acts, mems, gtok, gmem, dw, small = run_layer(
        half, lens, tok.reshape(ROWS, D), mem, ocot.reshape(ROWS, D), mcot.reshape(MROWS, D),
        attn_weights.reshape(12, D, D), ffn_in, ffn_out, gains, forget_w.reshape(1, D), forget_bias.reshape(SLOTS, 1),
    )
    full, acts, mems, gtok, gmem, small = run_reduce(dw.reshape(FLAT, LANES), acts, mems, gtok, gmem, small)
    grad_attn, grad_in, grad_out = run_widen(full.reshape(2, NBLOCKS, LANE_CUTS, BLOCK, LANES))
    return (
        acts, mems, gtok.astype(f32), gmem.astype(f32), grad_attn.reshape(3, 4, D, D), grad_in, grad_out,
        small[1:6], small[0], small[6, :SLOTS],
    )


def solution(mesh):
    return jax.shard_map(
        body,
        mesh=mesh,
        in_specs=(
            P("doc", "seg", None), P("doc", None, None), P("doc", None), P(), P(), P(), P(), P(), P(),
            P("doc", "seg", None), P("doc", "seg", None),
        ),
        out_specs=(
            P("doc", "seg", None), P("doc", "seg", None), P("doc", "seg", None), P("doc", "seg", None),
            P(), P(), P(), P(), P(), P(),
        ),
        check_vma=False,
    )
```

```python
import functools

import jax
import jax.numpy as jnp
from jax import lax
from jax.experimental import pallas as pl
from jax.experimental.pallas import tpu as pltpu
from jax.sharding import PartitionSpec as P

HEADS = 8
NDOC = 8
D = 512
FF = 2048
SLOTS = 64
SEG = 128
NSEG = 4
ROWS = NSEG * SEG
MROWS = NSEG * SLOTS
PAIRS = 4
PAIR = 128
FCHUNK = 512
BLOCK = 256
NBLOCKS = 20
LANES = 128
LANE_CUTS = D // LANES
FLAT = NBLOCKS * BLOCK * LANE_CUTS
MESH = pl.DeviceIdType.MESH
SCALE = 0.125

f32 = jnp.float32
bf16 = jnp.bfloat16


def dot(a, b):
    return lax.dot_general(a, b, (((1,), (0,)), ((), ())), preferred_element_type=f32)


def dot_nt(a, b):
    return lax.dot_general(a, b, (((1,), (1,)), ((), ())), preferred_element_type=f32)


def dot_tn(a, b):
    return lax.dot_general(a, b, (((0,), (0,)), ((), ())), preferred_element_type=f32)


def norm_stats(values):
    centered = values - jnp.mean(values, -1, keepdims=True)
    rstd = lax.rsqrt(jnp.mean(centered * centered, -1, keepdims=True) + 1e-05)
    return centered * rstd, rstd


def norm_back(grad, gain, xhat, rstd):
    scaled = grad * gain
    mean_one = jnp.mean(scaled, -1, keepdims=True)
    mean_two = jnp.mean(scaled * xhat, -1, keepdims=True)
    return rstd * (scaled - mean_one - xhat * mean_two)


def head_halves(values):
    low_half = lax.broadcasted_iota(jnp.int32, values.shape, 1) % PAIR < PAIR // 2
    return jnp.where(low_half, values, 0.0).astype(bf16), jnp.where(low_half, 0.0, values).astype(bf16)


def join_halves(stacked):
    rows = stacked.shape[0] // 2
    low_half = lax.broadcasted_iota(jnp.int32, (rows, PAIR), 1) < PAIR // 2
    return jnp.where(low_half, stacked[:rows], stacked[rows:])


def softmax_rows(scores):
    expd = jnp.exp(scores - jnp.max(scores, -1, keepdims=True))
    return expd * (1.0 / jnp.sum(expd, -1, keepdims=True))


def softmax_back(probs, grad):
    return probs * (grad - jnp.sum(probs * grad, -1, keepdims=True))


def gelu_both(u):
    square = u * u
    tanh = jnp.tanh(0.7978845608028654 * u * (1.0 + 0.044715 * square))
    half = 0.5 + 0.5 * tanh
    slope = half + u * half * (1.0 - tanh) * (0.7978845608028654 + 0.1070322243 * square)
    return u * half, slope


CHUNKS = ((4, 4, 4), (2, 3, 3))
UNIT = 16

TURNED = (5, 6, 7, 8, 9, 10, 11)


def scratch_buffers():
    def rows(dtype=bf16, width=D):
        return pltpu.VMEM((ROWS, width), dtype)

    def slots(dtype=bf16, width=D):
        return pltpu.VMEM((MROWS, width), dtype)

    def two(count):
        return pltpu.VMEM((2, count, D), bf16)

    def parts(shape_of):
        return [[pltpu.VMEM(shape_of(count * UNIT), bf16) for count in chunk] for chunk in CHUNKS]

    dma = pltpu.SemaphoreType.DMA
    return dict(
        attn=pltpu.VMEM((12, D, D), bf16), win=pltpu.VMEM((D, FF), bf16), wout=pltpu.VMEM((FF, D), bf16),
        attn_t=pltpu.VMEM((len(TURNED), D, D), bf16), win_t=pltpu.VMEM((FF, D), bf16), wout_t=pltpu.VMEM((D, FF), bf16),
        tok=rows(), ocot=rows(), mcot=slots(), mem=pltpu.VMEM((SLOTS, D), bf16),
        lens_own=pltpu.VMEM((8, LANES), jnp.int32), lens=pltpu.VMEM((8, LANES), jnp.int32),
        act=rows(), mout=slots(), gtok=rows(), gmem=slots(),
        h=rows(), q=two(ROWS), k=rows(), v=rows(), p=pltpu.VMEM((NSEG, PAIRS, 2 * SEG, SEG), bf16), o=rows(),
        xh0=rows(), rs0=rows(f32, 1),
        res=rows(f32), n1=rows(), xh1=rows(), rs1=rows(f32, 1), cq=two(ROWS), ck=slots(), cv=slots(),
        cp=pltpu.VMEM((NSEG, PAIRS, 2 * SEG, SLOTS), bf16), co=rows(),
        n2=rows(), xh2=rows(), rs2=rows(f32, 1), hid=rows(bf16, FF), gd=rows(bf16, FF),
        t=rows(), xh3=rows(), rs3=rows(f32, 1),
        xh4=slots(f32), rs4=slots(f32, 1), mlow=slots(), gate=slots(f32, 1), upd=slots(f32),
        mprev=pltpu.VMEM((SLOTS, D), f32),
        wq=two(MROWS), wk=rows(), wv=rows(), wp=pltpu.VMEM((NSEG, PAIRS, 2 * SLOTS, SEG), bf16), wo=slots(),
        gup=slots(), dwq=slots(), dwk=rows(), dwv=rows(), gyl=rows(), gul=rows(bf16, FF), gbl=rows(),
        dcq=rows(), dck=slots(), dcv=slots(),
        gal=rows(), dq=rows(),
        gain=pltpu.VMEM((8, D), f32), gm=pltpu.VMEM((SLOTS, D), f32), bias=pltpu.VMEM((SLOTS, LANES), f32),
        dw=pltpu.VMEM((FLAT, LANES), bf16),
        near=parts(lambda r: (2, 8 * r, LANES)), far=parts(lambda r: (2, 16 * r, LANES)),
        mid=parts(lambda r: (3, 4 * r, LANES)), last=parts(lambda r: (3, r, LANES)),
        small=pltpu.VMEM((3, 5, 8, D), f32),
        in_send=dma((3, 2, 3)), in_recv=dma((5, 3)), in_local=dma((8,)), load=dma((4,)),
        send=dma((2, 3, 32)), recv=dma((2, 3, 32)), own=dma((2, 3)),
        out_send=dma((2, 4)), out_recv=dma((2, 4)), out_local=dma((4,)),
        small_send=dma((3, 3)), small_recv=dma((3, 3)),
    )


def my_place():
    doc = lax.axis_index("doc")
    return lax.axis_index("seg"), doc // 8, (doc // 2) % 4, doc % 2


def device_at(x, y, z, core):
    return (x, y * 8 + z * 2 + core)


def remote(src, dst, send_sem, recv_sem, device):
    return pltpu.make_async_remote_copy(
        src_ref=src, dst_ref=dst, send_sem=send_sem, recv_sem=recv_sem, device_id=device, device_id_type=MESH
    )


def signal(sem, device):
    pl.semaphore_signal(sem, inc=1, device_id=device, device_id_type=MESH)


def fused_kernel(
    tok_ref, ocot_ref, mcot_ref, mem_ref, len_ref, attn_ref, win_ref, wout_ref, gains_ref, fw_ref, fb_ref,
    full_ref, act_out, mout_out, gtok_out, gmem_out, small_out,
    s,
):
    place = my_place()
    x, y, z, core = place
    owner, stream = x // 2, x % 2
    mine_here = owner == core
    sibling = device_at(x, y, z, 1 - core)

    def along(axis, coordinate):
        there = list(place)
        there[axis] = coordinate
        return device_at(*there)

    loads = [
        pltpu.make_async_copy(attn_ref.at[pl.ds(0, 4)], s["attn"].at[pl.ds(0, 4)], s["load"].at[0]),
        pltpu.make_async_copy(attn_ref.at[pl.ds(4, 8)], s["attn"].at[pl.ds(4, 8)], s["load"].at[1]),
        pltpu.make_async_copy(win_ref, s["win"], s["load"].at[2]),
        pltpu.make_async_copy(wout_ref, s["wout"], s["load"].at[3]),
    ]
    for i in (1, 2, 3, 0):
        loads[i].start()

    barrier = pltpu.get_barrier_semaphore()
    for src in range(NSEG):

        @pl.when(jnp.logical_or(src != x, owner != core))
        def _():
            signal(barrier, device_at(src, y, z, owner))

    for axis in range(3):
        for step in range(1, 4):
            signal(barrier, along(axis, (place[axis] + step) % 4))
    signal(barrier, sibling)
    for k in range(2):

        @pl.when(jnp.logical_or(2 * core + k != x, owner != core))
        def _():
            signal(barrier, device_at(2 * core + k, y, z, owner))

    s["lens_own"][...] = jnp.zeros_like(s["lens_own"])
    s["lens_own"][0:2, 0:NDOC] = len_ref[...]
    pl.semaphore_wait(barrier, 16 - 2 * mine_here.astype(jnp.int32))

    arrays = [(tok_ref, s["tok"], SEG), (ocot_ref, s["ocot"], SEG), (mcot_ref, s["mcot"], SLOTS)]

    def gather_sends(i, do):
        src, dst, count = arrays[i]
        for st in range(2):
            chip = 2 * core + st
            for to_core in range(2):
                here = jnp.logical_and(chip == x, core == to_core)
                target = dst.at[pl.ds(pl.multiple_of(x * count, count), count)]

                @pl.when(jnp.logical_not(here))
                def _():
                    do(remote(
                        src.at[st], target, s["in_send"].at[st, to_core, i], s["in_recv"].at[x, i],
                        device_at(chip, y, z, to_core),
                    ))

                @pl.when(here)
                def _():
                    copy = pltpu.make_async_copy(src.at[st], target, s["in_local"].at[i])
                    if do is start:
                        copy.start()
                    else:
                        copy.wait()

    def gather_arrivals(i):
        src, dst, count = arrays[i]
        for seg in range(NSEG):

            @pl.when(jnp.logical_or(seg != x, owner != core))
            def _():
                remote(
                    src.at[0], dst.at[pl.ds(seg * count, count)], s["in_send"].at[0, 0, i], s["in_recv"].at[seg, i],
                    device_at(seg, y, z, owner),
                ).wait_recv()

    def start(copy):
        copy.start()

    def sent(copy):
        copy.wait_send()

    gather_sends(0, start)

    firsts = [(mem_ref.at[stream], s["mem"]), (s["lens_own"], s["lens"])]
    for i, (src, dst) in enumerate(firsts):

        @pl.when(mine_here)
        def _():
            remote(src, dst, s["in_send"].at[2, 0, i], s["in_recv"].at[4, i], sibling).start()
            pltpu.make_async_copy(src, dst, s["in_local"].at[3 + i]).start()

    for load in loads[1:]:
        load.wait()
    for i, index in enumerate(TURNED):
        s["attn_t"][i] = jnp.transpose(s["attn"][index])
    for c in range(0, FF, D):
        s["win_t"][c : c + D, :] = jnp.transpose(s["win"][:, c : c + D])
        s["wout_t"][:, c : c + D] = jnp.transpose(s["wout"][c : c + D, :])
    loads[0].wait()

    for i, (src, dst) in enumerate(firsts):

        @pl.when(mine_here)
        def _():
            remote(src, dst, s["in_send"].at[2, 0, i], s["in_recv"].at[4, i], sibling).wait_send()
            pltpu.make_async_copy(src, dst, s["in_local"].at[3 + i]).wait()

        @pl.when(jnp.logical_not(mine_here))
        def _():
            remote(src, dst, s["in_send"].at[2, 0, i], s["in_recv"].at[4, i], sibling).wait_recv()

    gather_sends(0, sent)
    gather_arrivals(0)
    gather_sends(1, start)
    gather_sends(2, start)

    attn, win, wout = s["attn"], s["win"], s["wout"]
    attn_t = {index: s["attn_t"].at[i] for i, index in enumerate(TURNED)}
    win_t, wout_t = s["win_t"], s["wout_t"]
    gain = [gains_ref[i : i + 1, :] for i in range(5)]
    forget_w = fw_ref[...]
    square = (SLOTS, SLOTS)
    diagonal = lax.broadcasted_iota(jnp.int32, square, 0) == lax.broadcasted_iota(jnp.int32, square, 1)
    forget_bias = jnp.sum(jnp.where(diagonal, jnp.broadcast_to(fb_ref[...], square), 0.0), -1, keepdims=True)

    def doc_ids(shape, dim, base):
        pos = lax.broadcasted_iota(jnp.int32, shape, dim) + base
        ids = jnp.zeros(shape, jnp.int32)
        end = jnp.zeros((1, 1), jnp.int32)
        for j in range(NDOC):
            end += s["lens"][pl.ds(stream, 1), j : j + 1]
            ids += (end <= pos).astype(jnp.int32)
        return ids

    xhat, rstd = norm_stats(s["tok"][...].astype(f32))
    s["xh0"][...] = xhat.astype(bf16)
    s["rs0"][...] = rstd
    h = (xhat * gain[0]).astype(bf16)
    s["h"][...] = h
    s["q"][0], s["q"][1] = head_halves(dot(h, attn[0]) * SCALE)
    s["k"][...] = dot(h, attn[1]).astype(bf16)
    s["v"][...] = dot(h, attn[2]).astype(bf16)

    def self_forward(seg, carry):
        rows = pl.ds(pl.multiple_of(seg * SEG, SEG), SEG)
        same = doc_ids((SEG, SEG), 0, seg * SEG) == doc_ids((SEG, SEG), 1, seg * SEG)
        same = jnp.concatenate([same.astype(jnp.int32)] * 2, 0) > 0
        for pair in range(PAIRS):
            lanes = slice(pair * PAIR, (pair + 1) * PAIR)
            q_both = jnp.concatenate([s["q"][0, rows, lanes], s["q"][1, rows, lanes]], 0)
            scores = jnp.where(same, dot_nt(q_both, s["k"][rows, lanes]), -1e30)
            probs = softmax_rows(scores).astype(bf16)
            s["p"][seg, pair] = probs
            s["o"][rows, lanes] = join_halves(dot(probs, s["v"][rows, lanes])).astype(bf16)
        return carry

    lax.fori_loop(0, NSEG, self_forward, 0)
    res = s["tok"][...].astype(f32) + dot(s["o"][...], attn[3])
    s["res"][...] = res
    xhat, rstd = norm_stats(res)
    s["xh1"][...] = xhat.astype(bf16)
    s["rs1"][...] = rstd
    n1 = (xhat * gain[1]).astype(bf16)
    s["n1"][...] = n1
    s["cq"][0], s["cq"][1] = head_halves(dot(n1, attn[4]) * SCALE)

    s["mprev"][...] = s["mem"][...].astype(f32)

    def forward(seg, carry):
        rows = pl.ds(pl.multiple_of(seg * SEG, SEG), SEG)
        slots = pl.ds(pl.multiple_of(seg * SLOTS, SLOTS), SLOTS)
        mem = s["mprev"][...]
        xhat, rstd = norm_stats(mem)
        s["xh4"][slots, :] = xhat
        s["rs4"][slots, :] = rstd
        m = xhat * gain[4]
        mlow = m.astype(bf16)
        s["mlow"][slots, :] = mlow
        gate = jax.nn.sigmoid(jnp.sum(m * forget_w, -1, keepdims=True) + forget_bias)
        s["gate"][slots, :] = gate
        ck = dot(mlow, attn[5]).astype(bf16)
        cv = dot(mlow, attn[6]).astype(bf16)
        s["ck"][slots, :] = ck
        s["cv"][slots, :] = cv
        wq0, wq1 = head_halves(dot(mlow, attn[8]) * SCALE)
        s["wq"][0, slots, :] = wq0
        s["wq"][1, slots, :] = wq1
        for pair in range(PAIRS):
            lanes = slice(pair * PAIR, (pair + 1) * PAIR)
            q_both = jnp.concatenate([s["cq"][0, rows, lanes], s["cq"][1, rows, lanes]], 0)
            probs = softmax_rows(dot_nt(q_both, ck[:, lanes])).astype(bf16)
            s["cp"][seg, pair] = probs
            s["co"][rows, lanes] = join_halves(dot(probs, cv[:, lanes])).astype(bf16)
        res = s["res"][rows, :] + dot(s["co"][rows, :], attn[7])
        xhat, rstd = norm_stats(res)
        s["xh2"][rows, :] = xhat.astype(bf16)
        s["rs2"][rows, :] = rstd
        n2 = (xhat * gain[2]).astype(bf16)
        s["n2"][rows, :] = n2
        for c in range(0, FF, FCHUNK):
            hid, slope = gelu_both(dot(n2, win[:, c : c + FCHUNK]))
            hid = hid.astype(bf16)
            s["hid"][rows, c : c + FCHUNK] = hid
            s["gd"][rows, c : c + FCHUNK] = slope.astype(bf16)
            res = res + dot(hid, wout[c : c + FCHUNK, :])
        s["act"][rows, :] = res.astype(bf16)
        xhat, rstd = norm_stats(res)
        s["xh3"][rows, :] = xhat.astype(bf16)
        s["rs3"][rows, :] = rstd
        t = (xhat * gain[3]).astype(bf16)
        s["t"][rows, :] = t
        wk = dot(t, attn[9]).astype(bf16)
        wv = dot(t, attn[10]).astype(bf16)
        s["wk"][rows, :] = wk
        s["wv"][rows, :] = wv
        live = doc_ids((2 * SLOTS, SEG), 1, seg * SEG) < NDOC
        for pair in range(PAIRS):
            lanes = slice(pair * PAIR, (pair + 1) * PAIR)
            q_both = jnp.concatenate([wq0[:, lanes], wq1[:, lanes]], 0)
            scores = jnp.where(live, dot_nt(q_both, wk[:, lanes]), -1e30)
            probs = softmax_rows(scores).astype(bf16)
            s["wp"][seg, pair] = probs
            s["wo"][slots, lanes] = join_halves(dot(probs, wv[:, lanes])).astype(bf16)
        update = dot(s["wo"][slots, :], attn[11])
        s["upd"][slots, :] = mem - update
        fresh = (update + gate * (mem - update)).astype(bf16)
        s["mout"][slots, :] = fresh
        s["mprev"][...] = fresh.astype(f32)
        return carry

    lax.fori_loop(0, NSEG, forward, 0)

    def rows_at(first, count):
        return pl.ds(pl.multiple_of(first, UNIT), count)

    def results(indices, do):
        for k in range(2):
            seg = 2 * core + k
            here = jnp.logical_and(seg == x, mine_here)
            peer = device_at(seg, y, z, owner)
            sources = [
                (s["act"].at[rows_at(seg * SEG, SEG)], act_out), (s["mout"].at[rows_at(seg * SLOTS, SLOTS)], mout_out),
                (s["gtok"].at[rows_at(seg * SEG, SEG)], gtok_out), (s["gmem"].at[rows_at(seg * SLOTS, SLOTS)], gmem_out),
            ]
            for i in indices:
                src, dst = sources[i]

                @pl.when(jnp.logical_not(here))
                def _():
                    do(
                        remote(src, dst.at[stream], s["out_send"].at[k, i], s["out_recv"].at[stream, i], peer),
                        remote(src, dst.at[k], s["out_send"].at[k, i], s["out_recv"].at[k, i], peer),
                    )

                @pl.when(here)
                def _():
                    do(pltpu.make_async_copy(src, dst.at[stream], s["out_local"].at[i]), None)

    def results_start(copy, back):
        copy.start()

    def results_finish(copy, back):
        if back is None:
            copy.wait()
        else:
            copy.wait_send()
            back.wait_recv()

    results((0, 1), results_start)
    for i in (1, 2):
        gather_sends(i, sent)
        gather_arrivals(i)

    s["gm"][...] = jnp.zeros_like(s["gm"])
    s["gain"][...] = jnp.zeros_like(s["gain"])
    s["bias"][...] = jnp.zeros_like(s["bias"])

    def backward(step, carry):
        seg = NSEG - 1 - step
        rows = pl.ds(pl.multiple_of(seg * SEG, SEG), SEG)
        slots = pl.ds(pl.multiple_of(seg * SLOTS, SLOTS), SLOTS)
        gz = (s["mcot"][slots, :].astype(f32) + s["gm"][...]).astype(bf16).astype(f32)
        gate = s["gate"][slots, :]
        dgate = jnp.sum(gz * s["upd"][slots, :], -1, keepdims=True) * gate * (1.0 - gate)
        gup = ((1.0 - gate) * gz).astype(bf16)
        s["gup"][slots, :] = gup
        xh4 = s["xh4"][slots, :]
        s["gain"][5:6, :] += jnp.sum(dgate * (xh4 * gain[4]), 0, keepdims=True)
        s["bias"][...] += jnp.broadcast_to(dgate, (SLOTS, LANES))
        gm = dgate * forget_w
        g_o0, g_o1 = head_halves(dot(gup, attn_t[11][...]))
        for pair in range(PAIRS):
            lanes = slice(pair * PAIR, (pair + 1) * PAIR)
            probs = s["wp"][seg, pair]
            g_both = jnp.concatenate([g_o0[:, lanes], g_o1[:, lanes]], 0)
            q_both = jnp.concatenate([s["wq"][0, slots, lanes], s["wq"][1, slots, lanes]], 0)
            ds = softmax_back(probs.astype(f32), dot_nt(g_both, s["wv"][rows, lanes])).astype(bf16)
            s["dwv"][rows, lanes] = dot_tn(probs, g_both).astype(bf16)
            s["dwk"][rows, lanes] = dot_tn(ds, q_both).astype(bf16)
            s["dwq"][slots, lanes] = (join_halves(dot(ds, s["wk"][rows, lanes])) * SCALE).astype(bf16)
        gm = gm + dot(s["dwq"][slots, :], attn_t[8][...])
        gt = dot(s["dwk"][rows, :], attn_t[9][...]) + dot(s["dwv"][rows, :], attn_t[10][...])
        xhat = s["xh3"][rows, :].astype(f32)
        s["gain"][3:4, :] += jnp.sum(gt * xhat, 0, keepdims=True)
        gy = s["ocot"][rows, :].astype(f32) + norm_back(gt, gain[3], xhat, s["rs3"][rows, :])
        gyl = gy.astype(bf16)
        s["gyl"][rows, :] = gyl
        gn2 = jnp.zeros((SEG, D), f32)
        for c in range(0, FF, FCHUNK):
            ghid = dot(gyl, wout_t[:, c : c + FCHUNK])
            gul = (ghid * s["gd"][rows, c : c + FCHUNK].astype(f32)).astype(bf16)
            s["gul"][rows, c : c + FCHUNK] = gul
            gn2 = gn2 + dot(gul, win_t[c : c + FCHUNK, :])
        xhat = s["xh2"][rows, :].astype(f32)
        s["gain"][2:3, :] += jnp.sum(gn2 * xhat, 0, keepdims=True)
        gb = gy + norm_back(gn2, gain[2], xhat, s["rs2"][rows, :])
        s["res"][rows, :] = gb
        gbl = gb.astype(bf16)
        s["gbl"][rows, :] = gbl
        g_o0, g_o1 = head_halves(dot(gbl, attn_t[7][...]))
        for pair in range(PAIRS):
            lanes = slice(pair * PAIR, (pair + 1) * PAIR)
            probs = s["cp"][seg, pair]
            g_both = jnp.concatenate([g_o0[:, lanes], g_o1[:, lanes]], 0)
            q_both = jnp.concatenate([s["cq"][0, rows, lanes], s["cq"][1, rows, lanes]], 0)
            ds = softmax_back(probs.astype(f32), dot_nt(g_both, s["cv"][slots, lanes])).astype(bf16)
            s["dcv"][slots, lanes] = dot_tn(probs, g_both).astype(bf16)
            s["dck"][slots, lanes] = dot_tn(ds, q_both).astype(bf16)
            s["dcq"][rows, lanes] = (join_halves(dot(ds, s["ck"][slots, lanes])) * SCALE).astype(bf16)
        gm = gm + dot(s["dck"][slots, :], attn_t[5][...]) + dot(s["dcv"][slots, :], attn_t[6][...])
        s["gain"][4:5, :] += jnp.sum(gm * xh4, 0, keepdims=True)
        gmem = gate * gz + norm_back(gm, gain[4], xh4, s["rs4"][slots, :])
        gmem = gmem.astype(bf16)
        s["gmem"][slots, :] = gmem
        s["gm"][...] = gmem.astype(f32)
        return carry

    lax.fori_loop(0, NSEG, backward, 0)

    cut = pl.ds(pl.multiple_of(core * BLOCK, BLOCK), BLOCK)

    def put(i, value):
        value = value.astype(bf16)
        for j in range(LANE_CUTS):
            s["dw"][(i * LANE_CUTS + j) * BLOCK : (i * LANE_CUTS + j + 1) * BLOCK, :] = value[:, j * LANES : (j + 1) * LANES]

    def put_products(base, names):
        for i, (left, right) in enumerate(names):
            put(base + i, dot_tn(s[left][:, cut], s[right][...]))

    put_products(0, [("mlow", "dwq"), ("t", "dwk"), ("t", "dwv"), ("wo", "gup")])
    for i in range(4):
        put(4 + i, dot_tn(s["n2"][:, cut], s["gul"][:, i * D : (i + 1) * D]))
    for i in range(4):
        cut_i = pl.ds(pl.multiple_of(core * 4 * BLOCK + i * BLOCK, BLOCK), BLOCK)
        put(8 + i, dot_tn(s["hid"][:, cut_i], s["gyl"][...]))

    def small_copies(axis):
        here = place[axis]
        return [
            remote(
                s["small"].at[axis, here], s["small"].at[axis, here], s["small_send"].at[axis, step - 1],
                s["small_recv"].at[axis, step - 1], along(axis, (here + step) % 4),
            )
            for step in range(1, 4)
        ]

    def small_start(axis, value):
        s["small"][axis, place[axis]] = value
        for copy in small_copies(axis):
            copy.start()

    def small_finish(axis):
        for copy in small_copies(axis):
            copy.wait()
        return (s["small"][axis, 0] + s["small"][axis, 1]) + (s["small"][axis, 2] + s["small"][axis, 3])

    def part_steps(chunk, part):
        r = CHUNKS[chunk][part] * UNIT
        base = 64 * UNIT * (sum(sum(c) for c in CHUNKS[:chunk]) + sum(CHUNKS[chunk][:part]))
        axes = [(part + i) % 3 for i in range(3)]
        i1, i2, i3 = (place[a] for a in axes)
        right, left = along(axes[0], (i1 + 1) % 4), along(axes[0], (i1 + 3) % 4)
        sems = iter(range(40))
        near, far, mid, last = (s[name][chunk][part] for name in ("near", "far", "mid", "last"))
        dw = s["dw"]

        def copy(src, dst, device):
            i = next(sems)
            return remote(src, dst, s["send"].at[chunk, part, i], s["recv"].at[chunk, part, i], device)

        def block(b, first=0, count=16):
            return rows_at(base + (b % 4) * 16 * r + first * r, count * r)

        def add(refs):
            total = refs[0][...].astype(f32)
            for ref in refs[1:]:
                total += ref[...].astype(f32)
            return total.astype(bf16)

        half0, half1 = pl.ds(0, 8 * r), pl.ds(8 * r, 8 * r)
        a = copy(dw.at[block(i1 + 2, 0, 8)], near.at[0], right)
        b = copy(dw.at[block(i1 + 2, 8, 8)], near.at[1], left)
        c1 = copy(dw.at[block(i1 + 1, 8, 8)], far.at[0, half1], right)
        d0 = copy(dw.at[block(i1 + 3, 0, 8)], far.at[1, half0], left)
        for one in (a, b, c1, d0):
            one.start()
        yield
        a.wait()
        near[0] = add([near.at[0], dw.at[block(i1 + 1, 0, 8)]])
        c0 = copy(near.at[0], far.at[0, half0], right)
        c0.start()
        b.wait()
        near[1] = add([near.at[1], dw.at[block(i1 + 3, 8, 8)]])
        d1 = copy(near.at[1], far.at[1, half1], left)
        d1.start()
        yield
        for one in (c1, d0, c0, d1):
            one.wait()
        far[0] = add([far.at[0], far.at[1], dw.at[block(i1)]])
        two = [
            copy(far.at[0, rows_at((i2 + step) % 4 * 4 * r, 4 * r)], mid.at[step - 1], along(axes[1], (i2 + step) % 4))
            for step in range(1, 4)
        ]
        for one in two:
            one.start()
        yield
        for one in two:
            one.wait()
        mid[0] = add([mid.at[0], mid.at[1], mid.at[2], far.at[0, rows_at(i2 * 4 * r, 4 * r)]])
        three = [
            copy(mid.at[0, rows_at((i3 + step) % 4 * r, r)], last.at[step - 1], along(axes[2], (i3 + step) % 4))
            for step in range(1, 4)
        ]
        for one in three:
            one.start()
        yield
        for one in three:
            one.wait()
        mine = full_ref.at[core]
        home = block(i1, i2 * 4 + i3, 1)
        last[0] = add([last.at[0], last.at[1], last.at[2], mid.at[0, rows_at(i3 * r, r)]])
        keep = pltpu.make_async_copy(last.at[0], mine.at[home], s["own"].at[chunk, part])
        back = [copy(last.at[0], mine.at[home], along(axes[2], (i3 + step) % 4)) for step in range(1, 4)]
        for one in [keep] + back:
            one.start()
        yield
        for one in [keep] + back:
            one.wait()
        home = block(i1, i2 * 4, 4)
        back = [copy(mine.at[home], mine.at[home], along(axes[1], (i2 + step) % 4)) for step in range(1, 4)]
        for one in back:
            one.start()
        yield
        for one in back:
            one.wait()
        home = block(i1)
        to_right = copy(mine.at[home], mine.at[home], right)
        to_left = copy(mine.at[home], mine.at[home], left)
        over = [copy(mine.at[home], mine.at[home], sibling)]
        for one in (to_right, to_left, over[0]):
            one.start()
        yield
        to_right.wait()
        from_left = block(i1 + 3)
        on_right = copy(mine.at[block(i1 + 3, 0, 8)], mine.at[block(i1 + 3, 0, 8)], right)
        on_right.start()
        over.append(copy(mine.at[from_left], mine.at[from_left], sibling))
        over[-1].start()
        to_left.wait()
        from_right = block(i1 + 1)
        on_left = copy(mine.at[block(i1 + 1, 8, 8)], mine.at[block(i1 + 1, 8, 8)], left)
        on_left.start()
        over.append(copy(mine.at[from_right], mine.at[from_right], sibling))
        over[-1].start()
        yield
        on_right.wait()
        on_left.wait()
        opposite = block(i1 + 2)
        over.append(copy(mine.at[opposite], mine.at[opposite], sibling))
        over[-1].start()
        yield
        for one in over:
            one.wait()
        yield

    def chunk_steps(chunk):
        parts = [part_steps(chunk, part) for part in range(3)]
        for _ in range(10):
            for part in parts:
                next(part)
            yield

    first, second = chunk_steps(0), chunk_steps(1)
    next(first)

    gn1 = dot_nt(s["dcq"][...], attn[4])
    xhat = s["xh1"][...].astype(f32)
    s["gain"][1:2, :] = jnp.sum(gn1 * xhat, 0, keepdims=True)
    ga = s["res"][...] + norm_back(gn1, gain[1], xhat, s["rs1"][...])
    s["res"][...] = ga
    gal = ga.astype(bf16)
    s["gal"][...] = gal
    g0, g1 = head_halves(dot_nt(gal, attn[3]))
    s["cq"][0] = g0
    s["cq"][1] = g1

    def self_backward(seg, carry):
        rows = pl.ds(pl.multiple_of(seg * SEG, SEG), SEG)
        for pair in range(PAIRS):
            lanes = slice(pair * PAIR, (pair + 1) * PAIR)
            probs = s["p"][seg, pair]
            g_both = jnp.concatenate([s["cq"][0, rows, lanes], s["cq"][1, rows, lanes]], 0)
            q_both = jnp.concatenate([s["q"][0, rows, lanes], s["q"][1, rows, lanes]], 0)
            ds = softmax_back(probs.astype(f32), dot_nt(g_both, s["v"][rows, lanes])).astype(bf16)
            s["gyl"][rows, lanes] = dot_tn(probs, g_both).astype(bf16)
            s["t"][rows, lanes] = dot_tn(ds, q_both).astype(bf16)
            s["dq"][rows, lanes] = (join_halves(dot(ds, s["k"][rows, lanes])) * SCALE).astype(bf16)
        return carry

    lax.fori_loop(0, NSEG, self_backward, 0)
    next(first)
    gh = dot_nt(s["dq"][...], attn[0]) + dot_nt(s["t"][...], attn[1]) + dot_nt(s["gyl"][...], attn[2])
    xhat = s["xh0"][...].astype(f32)
    s["gain"][0:1, :] = jnp.sum(gh * xhat, 0, keepdims=True)
    s["gtok"][...] = (s["res"][...] + norm_back(gh, gain[0], xhat, s["rs0"][...])).astype(bf16)
    s["gain"][6:7, 0:SLOTS] = jnp.sum(jnp.where(diagonal, s["bias"][:, 0:SLOTS], 0.0), 0, keepdims=True)
    put_products(12, [("h", "dq"), ("h", "t"), ("h", "gyl"), ("o", "gal")])
    put_products(16, [("n1", "dcq"), ("mlow", "dck"), ("mlow", "dcv"), ("co", "gbl")])

    next(second)
    small_start(0, s["gain"][...])
    next(first)
    results((2, 3), results_start)
    next(second)
    next(first)
    total = small_finish(0)
    small_start(1, total)
    next(second)
    next(first)
    total = small_finish(1)
    small_start(2, total)
    next(second)
    next(first)
    small_out[...] = small_finish(2)
    next(second)
    next(first)
    next(second)
    next(second)
    next(first)
    next(second)
    next(first)
    next(second)
    next(first)
    next(second)
    results((0, 1, 2, 3), results_finish)


def run_fused(tok, ocot, mcot, mem, lens, attn, win, wout, gains, fw, fb):
    vmem = pl.BlockSpec(memory_space=pltpu.VMEM)
    hbm = pl.BlockSpec(memory_space=pl.ANY)
    return pl.pallas_call(
        fused_kernel,
        out_shape=(
            jax.ShapeDtypeStruct((2, FLAT, LANES), bf16),
            jax.ShapeDtypeStruct((2, SEG, D), bf16),
            jax.ShapeDtypeStruct((2, SLOTS, D), bf16),
            jax.ShapeDtypeStruct((2, SEG, D), bf16),
            jax.ShapeDtypeStruct((2, SLOTS, D), bf16),
            jax.ShapeDtypeStruct((8, D), f32),
        ),
        in_specs=[hbm] * 4 + [vmem] + [hbm] * 3 + [vmem] * 3,
        out_specs=[hbm] * 5 + [vmem],
        scratch_shapes=[scratch_buffers()],
        compiler_params=pltpu.CompilerParams(collective_id=1, has_side_effects=True, vmem_limit_bytes=62 << 20),
        name="layer_and_sums",
    )(tok, ocot, mcot, mem, lens, attn, win, wout, gains, fw, fb)


def widen_kernel(
    full_ref, act_ref, mem_ref, gtok_ref, gmem_ref, small_ref,
    attn_ref, in_ref, out_ref, act_out, mem_out, gtok_out, gmem_out, gains_out, fw_out, fb_out,
    full_s, wide_s, load_sem, store_sem,
):
    def load(i):
        return [
            pltpu.make_async_copy(full_ref.at[half, i], full_s.at[i, half], load_sem.at[i, half]) for half in range(2)
        ]

    def target(i, half):
        if i < 4:
            return attn_ref.at[8 + i, pl.ds(half * BLOCK, BLOCK), :]
        if i < 8:
            return in_ref.at[pl.ds(half * BLOCK, BLOCK), pl.ds((i - 4) * D, D)]
        if i < 12:
            return out_ref.at[pl.ds(half * 4 * BLOCK + (i - 8) * BLOCK, BLOCK), :]
        return attn_ref.at[i - 12, pl.ds(half * BLOCK, BLOCK), :]

    def store(i, half):
        return pltpu.make_async_copy(wide_s.at[i, half], target(i, half), store_sem.at[i, half])

    for i in range(NBLOCKS):
        for copy in load(i):
            copy.start()
    act_out[...] = act_ref[...]
    mem_out[...] = mem_ref[...]
    gtok_out[...] = gtok_ref[...].astype(f32)
    gmem_out[...] = gmem_ref[...].astype(f32)
    gains_out[...] = small_ref[0:5, :]
    fw_out[...] = small_ref[5:6, :]
    fb_out[...] = small_ref[6:7, 0:SLOTS]
    for i in range(NBLOCKS):
        for half, copy in enumerate(load(i)):
            copy.wait()
            for j in range(LANE_CUTS):
                wide_s[i, half, :, j * LANES : (j + 1) * LANES] = full_s[i, half, j].astype(f32)
            store(i, half).start()
    for i in range(NBLOCKS):
        for half in range(2):
            store(i, half).wait()


def run_widen(full, *others):
    hbm = pl.BlockSpec(memory_space=pl.ANY)
    vmem = pl.BlockSpec(memory_space=pltpu.VMEM)
    return pl.pallas_call(
        widen_kernel,
        out_shape=(
            jax.ShapeDtypeStruct((12, D, D), f32),
            jax.ShapeDtypeStruct((D, FF), f32),
            jax.ShapeDtypeStruct((FF, D), f32),
            jax.ShapeDtypeStruct((2, SEG, D), bf16),
            jax.ShapeDtypeStruct((2, SLOTS, D), bf16),
            jax.ShapeDtypeStruct((2, SEG, D), f32),
            jax.ShapeDtypeStruct((2, SLOTS, D), f32),
            jax.ShapeDtypeStruct((5, D), f32),
            jax.ShapeDtypeStruct((1, D), f32),
            jax.ShapeDtypeStruct((1, SLOTS), f32),
        ),
        in_specs=[hbm] + [vmem] * 5,
        out_specs=[hbm] * 3 + [vmem] * 7,
        scratch_shapes=[
            pltpu.VMEM((NBLOCKS, 2, LANE_CUTS, BLOCK, LANES), bf16),
            pltpu.VMEM((NBLOCKS, 2, BLOCK, D), f32),
            pltpu.SemaphoreType.DMA((NBLOCKS, 2)),
            pltpu.SemaphoreType.DMA((NBLOCKS, 2)),
        ],
        compiler_params=pltpu.CompilerParams(vmem_limit_bytes=60 << 20),
        name="widen_gradients",
    )(full, *others)


def body(
    tokens, memory_start, doc_lengths, attn_weights, ffn_in, ffn_out, gains, forget_w, forget_bias,
    out_cotangent, memory_cotangent,
):
    full, *others = run_fused(
        tokens, out_cotangent, memory_cotangent, memory_start, doc_lengths,
        attn_weights.reshape(12, D, D), ffn_in, ffn_out, gains, forget_w.reshape(1, D), forget_bias.reshape(1, SLOTS),
    )
    grad_attn, grad_in, grad_out, acts, mems, gtok, gmem, grad_gains, grad_fw, grad_fb = run_widen(
        full.reshape(2, NBLOCKS, LANE_CUTS, BLOCK, LANES), *others
    )
    return (
        acts, mems, gtok, gmem, grad_attn.reshape(3, 4, D, D), grad_in, grad_out,
        grad_gains, grad_fw.reshape(D), grad_fb.reshape(SLOTS),
    )


def solution(mesh):
    return jax.shard_map(
        body,
        mesh=mesh,
        in_specs=(
            P("doc", "seg", None), P("doc", None, None), P("doc", None), P(), P(), P(), P(), P(), P(),
            P("doc", "seg", None), P("doc", "seg", None),
        ),
        out_specs=(
            P("doc", "seg", None), P("doc", "seg", None), P("doc", "seg", None), P("doc", "seg", None),
            P(), P(), P(), P(), P(), P(),
        ),
        check_vma=False,
    )
```

```python
import functools

import jax
import jax.numpy as jnp
from jax import lax
from jax.experimental import pallas as pl
from jax.experimental.pallas import tpu as pltpu
from jax.sharding import PartitionSpec as P

HEADS = 8
NDOC = 8
D = 512
FF = 2048
SLOTS = 64
SEG = 128
NSEG = 4
ROWS = NSEG * SEG
MROWS = NSEG * SLOTS
PAIRS = 4
PAIR = 128
FCHUNK = 512
BLOCK = 256
NBLOCKS = 20
LANES = 128
LANE_CUTS = D // LANES
FLAT = NBLOCKS * BLOCK * LANE_CUTS
MESH = pl.DeviceIdType.MESH
SCALE = 0.125

f32 = jnp.float32
bf16 = jnp.bfloat16


def dot(a, b):
    return lax.dot_general(a, b, (((1,), (0,)), ((), ())), preferred_element_type=f32)


def dot_nt(a, b):
    return lax.dot_general(a, b, (((1,), (1,)), ((), ())), preferred_element_type=f32)


def dot_tn(a, b):
    return lax.dot_general(a, b, (((0,), (0,)), ((), ())), preferred_element_type=f32)


def norm_stats(values):
    centered = values - jnp.mean(values, -1, keepdims=True)
    rstd = lax.rsqrt(jnp.mean(centered * centered, -1, keepdims=True) + 1e-05)
    return centered * rstd, rstd


def norm_back(grad, gain, xhat, rstd):
    scaled = grad * gain
    mean_one = jnp.mean(scaled, -1, keepdims=True)
    mean_two = jnp.mean(scaled * xhat, -1, keepdims=True)
    return rstd * (scaled - mean_one - xhat * mean_two)


def head_halves(values):
    low_half = lax.broadcasted_iota(jnp.int32, values.shape, 1) % PAIR < PAIR // 2
    return jnp.where(low_half, values, 0.0).astype(bf16), jnp.where(low_half, 0.0, values).astype(bf16)


def join_halves(stacked):
    rows = stacked.shape[0] // 2
    low_half = lax.broadcasted_iota(jnp.int32, (rows, PAIR), 1) < PAIR // 2
    return jnp.where(low_half, stacked[:rows], stacked[rows:])


def attend(queries, keys, values, bias):
    scores = jnp.concatenate([dot_nt(k, q) for k, q in zip(keys, queries)], 1) + bias
    expd = jnp.exp(scores - jnp.max(scores, 0, keepdims=True))
    probs = (expd * (1.0 / jnp.sum(expd, 0, keepdims=True))).astype(bf16)
    width = queries[0].shape[0]
    mixed = [join_halves(dot_tn(probs[:, i * width : (i + 1) * width], v)) for i, v in enumerate(values)]
    return probs, jnp.concatenate(mixed, 1).astype(bf16)


def attend_back(probs, grads, queries, keys, values):
    width = queries[0].shape[0]
    wide = probs.astype(f32)
    dp = jnp.concatenate([dot_nt(v, g) for v, g in zip(values, grads)], 1)
    ds = (wide * (dp - jnp.sum(wide * dp, 0, keepdims=True))).astype(bf16)
    cuts = [slice(i * width, (i + 1) * width) for i in range(PAIRS)]
    dq = [join_halves(dot_tn(ds[:, cut], k)) for cut, k in zip(cuts, keys)]
    dk = [dot(ds[:, cut], q) for cut, q in zip(cuts, queries)]
    dv = [dot(probs[:, cut], g) for cut, g in zip(cuts, grads)]
    join = lambda parts: jnp.concatenate(parts, 1)
    return (join(dq) * SCALE).astype(bf16), join(dk).astype(bf16), join(dv).astype(bf16)


def pair_lanes(values):
    return [values[:, i * PAIR : (i + 1) * PAIR] for i in range(PAIRS)]


def pair_queries(first, second):
    return [jnp.concatenate(halves, 0) for halves in zip(pair_lanes(first), pair_lanes(second))]


def gelu_both(u):
    square = u * u
    tanh = jnp.tanh(0.7978845608028654 * u * (1.0 + 0.044715 * square))
    half = 0.5 + 0.5 * tanh
    slope = half + u * half * (1.0 - tanh) * (0.7978845608028654 + 0.1070322243 * square)
    return u * half, slope


CHUNKS = ((5, 6, 5), (1, 1, 2))
UNIT = 16

TURNED = (5, 6, 7, 8, 9, 10, 11)


def scratch_buffers():
    def rows(dtype=bf16, width=D):
        return pltpu.VMEM((ROWS, width), dtype)

    def slots(dtype=bf16, width=D):
        return pltpu.VMEM((MROWS, width), dtype)

    def two(count):
        return pltpu.VMEM((2, count, D), bf16)

    def parts(shape_of):
        return [[pltpu.VMEM(shape_of(count * UNIT), bf16) for count in chunk] for chunk in CHUNKS]

    dma = pltpu.SemaphoreType.DMA
    return dict(
        attn=pltpu.VMEM((12, D, D), bf16), win=pltpu.VMEM((D, FF), bf16), wout=pltpu.VMEM((FF, D), bf16),
        attn_t=pltpu.VMEM((len(TURNED), D, D), bf16), win_t=pltpu.VMEM((FF, D), bf16), wout_t=pltpu.VMEM((D, FF), bf16),
        tok=rows(), ocot=rows(), mcot=slots(), mem=pltpu.VMEM((SLOTS, D), bf16),
        lens_own=pltpu.VMEM((8, LANES), jnp.int32), lens=pltpu.VMEM((8, LANES), jnp.int32),
        act=rows(), mout=slots(), gtok=rows(), gmem=slots(),
        h=rows(), q=two(ROWS), k=rows(), v=rows(), p=pltpu.VMEM((NSEG, SEG, HEADS * SEG), bf16), o=rows(),
        xh0=rows(), rs0=rows(f32, 1),
        res=rows(f32), n1=rows(), xh1=rows(), rs1=rows(f32, 1), cq=two(ROWS), ck=slots(), cv=slots(),
        cp=pltpu.VMEM((NSEG, SLOTS, HEADS * SEG), bf16), co=rows(),
        n2=rows(), xh2=rows(), rs2=rows(f32, 1), hid=rows(bf16, FF), gd=rows(bf16, FF),
        t=rows(), xh3=rows(), rs3=rows(f32, 1),
        xh4=slots(f32), rs4=slots(f32, 1), mlow=slots(), gate=slots(f32, 1), upd=slots(f32),
        mprev=pltpu.VMEM((SLOTS, D), f32),
        wq=two(MROWS), wk=rows(), wv=rows(), wp=pltpu.VMEM((NSEG, SEG, HEADS * SLOTS), bf16), wo=slots(),
        gup=slots(), dwq=slots(), dwk=rows(), dwv=rows(), gyl=rows(), gul=rows(bf16, FF), gbl=rows(),
        dcq=rows(), dck=slots(), dcv=slots(),
        gal=rows(), dq=rows(),
        gain=pltpu.VMEM((8, D), f32), gm=pltpu.VMEM((SLOTS, D), f32), bias=pltpu.VMEM((SLOTS, LANES), f32),
        dw=pltpu.VMEM((FLAT, LANES), bf16),
        near=parts(lambda r: (2, 8 * r, LANES)), far=parts(lambda r: (3, 16 * r, LANES)),
        mid=parts(lambda r: (3, 4 * r, LANES)), last=parts(lambda r: (3, r, LANES)),
        small=pltpu.VMEM((3, 5, 8, D), f32),
        in_send=dma((3, 2, 3)), in_recv=dma((5, 3)), pass_send=dma((4, 3)), pass_recv=dma((4, 3)), in_local=dma((8,)), load=dma((4,)),
        send=dma((2, 3, 32)), recv=dma((2, 3, 32)), own=dma((2, 3)),
        out_send=dma((2, 4)), out_recv=dma((2, 4)), out_local=dma((4,)),
        small_send=dma((3, 3)), small_recv=dma((3, 3)),
    )


def my_place():
    doc = lax.axis_index("doc")
    return lax.axis_index("seg"), doc // 8, (doc // 2) % 4, doc % 2


def device_at(x, y, z, core):
    return (x, y * 8 + z * 2 + core)


def remote(src, dst, send_sem, recv_sem, device):
    return pltpu.make_async_remote_copy(
        src_ref=src, dst_ref=dst, send_sem=send_sem, recv_sem=recv_sem, device_id=device, device_id_type=MESH
    )


def signal(sem, device):
    pl.semaphore_signal(sem, inc=1, device_id=device, device_id_type=MESH)


def fused_kernel(
    tok_ref, ocot_ref, mcot_ref, mem_ref, len_ref, attn_ref, win_ref, wout_ref, gains_ref, fw_ref, fb_ref,
    full_ref, act_out, mout_out, gtok_out, gmem_out, small_out,
    s,
):
    place = my_place()
    x, y, z, core = place
    owner, stream = x // 2, x % 2
    mine_here = owner == core
    sibling = device_at(x, y, z, 1 - core)

    def along(axis, coordinate):
        there = list(place)
        there[axis] = coordinate
        return device_at(*there)

    def rows_at(first, count):
        return pl.ds(pl.multiple_of(first, UNIT), count)

    loads = [
        pltpu.make_async_copy(attn_ref.at[pl.ds(0, 4)], s["attn"].at[pl.ds(0, 4)], s["load"].at[0]),
        pltpu.make_async_copy(attn_ref.at[pl.ds(4, 8)], s["attn"].at[pl.ds(4, 8)], s["load"].at[1]),
        pltpu.make_async_copy(win_ref, s["win"], s["load"].at[2]),
        pltpu.make_async_copy(wout_ref, s["wout"], s["load"].at[3]),
    ]
    for i in (1, 2, 3, 0):
        loads[i].start()

    barrier = pltpu.get_barrier_semaphore()
    for step in range(1, 4):
        signal(barrier, device_at((x + step) % 4, y, z, owner))
    for axis in range(3):
        for step in range(1, 4):
            signal(barrier, along(axis, (place[axis] + step) % 4))
    signal(barrier, sibling)
    for k in range(2):

        @pl.when(jnp.logical_or(2 * core + k != x, owner != core))
        def _():
            signal(barrier, device_at(2 * core + k, y, z, owner))

    s["lens_own"][...] = jnp.zeros_like(s["lens_own"])
    s["lens_own"][0:2, 0:NDOC] = len_ref[...]
    pl.semaphore_wait(barrier, 16 - 3 * mine_here.astype(jnp.int32))

    arrays = [(tok_ref, s["tok"], SEG), (ocot_ref, s["ocot"], SEG), (mcot_ref, s["mcot"], SLOTS)]

    def gather_sends(i, start):
        src, dst, count = arrays[i]
        half = count // 2
        for st in range(2):
            chip = 2 * core + st

            @pl.when(chip != x)
            def _():
                for to_core in range(2):
                    copy = remote(
                        src.at[st, pl.ds(to_core * half, half)], dst.at[rows_at(x * count + to_core * half, half)],
                        s["in_send"].at[st, to_core, i], s["in_recv"].at[x, i], device_at(chip, y, z, to_core),
                    )
                    copy.start() if start else copy.wait_send()

            @pl.when(chip == x)
            def _():
                target = dst.at[rows_at(x * count, count)]
                local = pltpu.make_async_copy(src.at[st], target, s["in_local"].at[i])
                copy = remote(src.at[st], target, s["in_send"].at[st, 0, i], s["in_recv"].at[x, i], sibling)
                if start:
                    local.start()
                    copy.start()
                else:
                    local.wait()
                    copy.wait_send()

    def gather_forward(i):
        src, dst, count = arrays[i]
        half = count // 2
        copies = []
        for step in (1, 3, 2):
            seg = (x + step) % 4
            part = dst.at[rows_at(seg * count + core * half, half)]
            remote(
                part, part, s["in_send"].at[0, 0, i], s["in_recv"].at[seg, i], device_at(seg, y, z, owner)
            ).wait_recv()
            copies.append(remote(part, part, s["pass_send"].at[step, i], s["pass_recv"].at[step, i], sibling))
            copies[-1].start()
        return copies

    def gather_finish(i, copies):
        src, dst, count = arrays[i]
        gather_sends(i, False)
        for copy in copies:
            copy.wait()

        @pl.when(jnp.logical_not(mine_here))
        def _():
            whole = dst.at[rows_at(x * count, count)]
            remote(whole, whole, s["in_send"].at[0, 0, i], s["in_recv"].at[x, i], sibling).wait_recv()

    gather_sends(0, True)

    firsts = [(mem_ref.at[stream], s["mem"]), (s["lens_own"], s["lens"])]
    for i, (src, dst) in enumerate(firsts):

        @pl.when(mine_here)
        def _():
            remote(src, dst, s["in_send"].at[2, 0, i], s["in_recv"].at[4, i], sibling).start()
            pltpu.make_async_copy(src, dst, s["in_local"].at[3 + i]).start()

    for load in loads[1:]:
        load.wait()
    for i, index in enumerate(TURNED):
        s["attn_t"][i] = jnp.transpose(s["attn"][index])
    for c in range(0, FF, D):
        s["win_t"][c : c + D, :] = jnp.transpose(s["win"][:, c : c + D])
        s["wout_t"][:, c : c + D] = jnp.transpose(s["wout"][c : c + D, :])
    loads[0].wait()

    for i, (src, dst) in enumerate(firsts):

        @pl.when(mine_here)
        def _():
            remote(src, dst, s["in_send"].at[2, 0, i], s["in_recv"].at[4, i], sibling).wait_send()
            pltpu.make_async_copy(src, dst, s["in_local"].at[3 + i]).wait()

        @pl.when(jnp.logical_not(mine_here))
        def _():
            remote(src, dst, s["in_send"].at[2, 0, i], s["in_recv"].at[4, i], sibling).wait_recv()

    gather_finish(0, gather_forward(0))
    gather_sends(1, True)
    gather_sends(2, True)

    attn, win, wout = s["attn"], s["win"], s["wout"]
    attn_t = {index: s["attn_t"].at[i] for i, index in enumerate(TURNED)}
    win_t, wout_t = s["win_t"], s["wout_t"]
    gain = [gains_ref[i : i + 1, :] for i in range(5)]
    forget_w = fw_ref[...]
    square = (SLOTS, SLOTS)
    diagonal = lax.broadcasted_iota(jnp.int32, square, 0) == lax.broadcasted_iota(jnp.int32, square, 1)
    forget_bias = jnp.sum(jnp.where(diagonal, jnp.broadcast_to(fb_ref[...], square), 0.0), -1, keepdims=True)

    ends = []
    for j in range(NDOC):
        ends.append(s["lens"][pl.ds(stream, 1), j : j + 1] + (ends[-1] if ends else 0))

    def doc_ids(shape, dim, base):
        pos = lax.broadcasted_iota(jnp.int32, shape, dim) + base
        return sum((end <= pos).astype(jnp.int32) for end in ends)

    xhat, rstd = norm_stats(s["tok"][...].astype(f32))
    s["xh0"][...] = xhat.astype(bf16)
    s["rs0"][...] = rstd
    h = (xhat * gain[0]).astype(bf16)
    s["h"][...] = h
    s["q"][0], s["q"][1] = head_halves(dot(h, attn[0]) * SCALE)
    s["k"][...] = dot(h, attn[1]).astype(bf16)
    s["v"][...] = dot(h, attn[2]).astype(bf16)

    def self_forward(seg, carry):
        rows = pl.ds(pl.multiple_of(seg * SEG, SEG), SEG)
        same = doc_ids((SEG, SEG), 0, seg * SEG) == doc_ids((SEG, SEG), 1, seg * SEG)
        bias = jnp.concatenate([jnp.where(same, 0.0, -1e30)] * HEADS, 1)
        s["p"][seg], s["o"][rows, :] = attend(
            pair_queries(s["q"][0, rows, :], s["q"][1, rows, :]), pair_lanes(s["k"][rows, :]), pair_lanes(s["v"][rows, :]), bias
        )
        return carry

    lax.fori_loop(0, NSEG, self_forward, 0)
    res = s["tok"][...].astype(f32) + dot(s["o"][...], attn[3])
    s["res"][...] = res
    xhat, rstd = norm_stats(res)
    s["xh1"][...] = xhat.astype(bf16)
    s["rs1"][...] = rstd
    n1 = (xhat * gain[1]).astype(bf16)
    s["n1"][...] = n1
    s["cq"][0], s["cq"][1] = head_halves(dot(n1, attn[4]) * SCALE)

    passed = [gather_forward(1), gather_forward(2)]

    s["mprev"][...] = s["mem"][...].astype(f32)

    def forward(seg, carry):
        rows = pl.ds(pl.multiple_of(seg * SEG, SEG), SEG)
        slots = pl.ds(pl.multiple_of(seg * SLOTS, SLOTS), SLOTS)
        mem = s["mprev"][...]
        xhat, rstd = norm_stats(mem)
        s["xh4"][slots, :] = xhat
        s["rs4"][slots, :] = rstd
        m = xhat * gain[4]
        mlow = m.astype(bf16)
        s["mlow"][slots, :] = mlow
        gate = jax.nn.sigmoid(jnp.sum(m * forget_w, -1, keepdims=True) + forget_bias)
        s["gate"][slots, :] = gate
        ck = dot(mlow, attn[5]).astype(bf16)
        cv = dot(mlow, attn[6]).astype(bf16)
        s["ck"][slots, :] = ck
        s["cv"][slots, :] = cv
        wq0, wq1 = head_halves(dot(mlow, attn[8]) * SCALE)
        s["wq"][0, slots, :] = wq0
        s["wq"][1, slots, :] = wq1
        s["cp"][seg], co = attend(
            pair_queries(s["cq"][0, rows, :], s["cq"][1, rows, :]), pair_lanes(ck), pair_lanes(cv), 0.0
        )
        s["co"][rows, :] = co
        res = s["res"][rows, :] + dot(co, attn[7])
        xhat, rstd = norm_stats(res)
        s["xh2"][rows, :] = xhat.astype(bf16)
        s["rs2"][rows, :] = rstd
        n2 = (xhat * gain[2]).astype(bf16)
        s["n2"][rows, :] = n2
        for c in range(0, FF, FCHUNK):
            hid, slope = gelu_both(dot(n2, win[:, c : c + FCHUNK]))
            hid = hid.astype(bf16)
            s["hid"][rows, c : c + FCHUNK] = hid
            s["gd"][rows, c : c + FCHUNK] = slope.astype(bf16)
            res = res + dot(hid, wout[c : c + FCHUNK, :])
        s["act"][rows, :] = res.astype(bf16)
        xhat, rstd = norm_stats(res)
        s["xh3"][rows, :] = xhat.astype(bf16)
        s["rs3"][rows, :] = rstd
        t = (xhat * gain[3]).astype(bf16)
        s["t"][rows, :] = t
        wk = dot(t, attn[9]).astype(bf16)
        wv = dot(t, attn[10]).astype(bf16)
        s["wk"][rows, :] = wk
        s["wv"][rows, :] = wv
        pos = lax.broadcasted_iota(jnp.int32, (SEG, HEADS * SLOTS), 0) + seg * SEG
        s["wp"][seg], wo = attend(
            pair_queries(wq0, wq1), pair_lanes(wk), pair_lanes(wv), jnp.where(pos < ends[-1], 0.0, -1e30)
        )
        s["wo"][slots, :] = wo
        update = dot(wo, attn[11])
        s["upd"][slots, :] = mem - update
        fresh = (update + gate * (mem - update)).astype(bf16)
        s["mout"][slots, :] = fresh
        s["mprev"][...] = fresh.astype(f32)
        return carry

    lax.fori_loop(0, NSEG, forward, 0)

    def results(indices, do):
        for k in range(2):
            seg = 2 * core + k
            here = jnp.logical_and(seg == x, mine_here)
            peer = device_at(seg, y, z, owner)
            sources = [
                (s["act"].at[rows_at(seg * SEG, SEG)], act_out), (s["mout"].at[rows_at(seg * SLOTS, SLOTS)], mout_out),
                (s["gtok"].at[rows_at(seg * SEG, SEG)], gtok_out), (s["gmem"].at[rows_at(seg * SLOTS, SLOTS)], gmem_out),
            ]
            for i in indices:
                src, dst = sources[i]

                @pl.when(jnp.logical_not(here))
                def _():
                    do(
                        remote(src, dst.at[stream], s["out_send"].at[k, i], s["out_recv"].at[stream, i], peer),
                        remote(src, dst.at[k], s["out_send"].at[k, i], s["out_recv"].at[k, i], peer),
                    )

                @pl.when(here)
                def _():
                    do(pltpu.make_async_copy(src, dst.at[stream], s["out_local"].at[i]), None)

    def results_start(copy, back):
        copy.start()

    def results_finish(copy, back):
        if back is None:
            copy.wait()
        else:
            copy.wait_send()
            back.wait_recv()

    results((0, 1), results_start)
    for i in (1, 2):
        gather_finish(i, passed[i - 1])

    s["gm"][...] = jnp.zeros_like(s["gm"])
    s["gain"][...] = jnp.zeros_like(s["gain"])
    s["bias"][...] = jnp.zeros_like(s["bias"])

    def backward(step, carry):
        seg = NSEG - 1 - step
        rows = pl.ds(pl.multiple_of(seg * SEG, SEG), SEG)
        slots = pl.ds(pl.multiple_of(seg * SLOTS, SLOTS), SLOTS)
        gz = (s["mcot"][slots, :].astype(f32) + s["gm"][...]).astype(bf16).astype(f32)
        gate = s["gate"][slots, :]
        dgate = jnp.sum(gz * s["upd"][slots, :], -1, keepdims=True) * gate * (1.0 - gate)
        gup = ((1.0 - gate) * gz).astype(bf16)
        s["gup"][slots, :] = gup
        xh4 = s["xh4"][slots, :]
        s["gain"][5:6, :] += jnp.sum(dgate * (xh4 * gain[4]), 0, keepdims=True)
        s["bias"][...] += jnp.broadcast_to(dgate, (SLOTS, LANES))
        gm = dgate * forget_w
        dwq, dwk, dwv = attend_back(
            s["wp"][seg], pair_queries(*head_halves(dot(gup, attn_t[11][...]))),
            pair_queries(s["wq"][0, slots, :], s["wq"][1, slots, :]),
            pair_lanes(s["wk"][rows, :]), pair_lanes(s["wv"][rows, :]),
        )
        s["dwq"][slots, :] = dwq
        s["dwk"][rows, :] = dwk
        s["dwv"][rows, :] = dwv
        gt = dot(dwk, attn_t[9][...]) + dot(dwv, attn_t[10][...])
        gm = gm + dot(dwq, attn_t[8][...])
        xhat = s["xh3"][rows, :].astype(f32)
        s["gain"][3:4, :] += jnp.sum(gt * xhat, 0, keepdims=True)
        gy = s["ocot"][rows, :].astype(f32) + norm_back(gt, gain[3], xhat, s["rs3"][rows, :])
        gyl = gy.astype(bf16)
        s["gyl"][rows, :] = gyl
        gn2 = jnp.zeros((SEG, D), f32)
        for c in range(0, FF, FCHUNK):
            ghid = dot(gyl, wout_t[:, c : c + FCHUNK])
            gul = (ghid * s["gd"][rows, c : c + FCHUNK].astype(f32)).astype(bf16)
            s["gul"][rows, c : c + FCHUNK] = gul
            gn2 = gn2 + dot(gul, win_t[c : c + FCHUNK, :])
        xhat = s["xh2"][rows, :].astype(f32)
        s["gain"][2:3, :] += jnp.sum(gn2 * xhat, 0, keepdims=True)
        gb = gy + norm_back(gn2, gain[2], xhat, s["rs2"][rows, :])
        s["res"][rows, :] = gb
        gbl = gb.astype(bf16)
        s["gbl"][rows, :] = gbl
        dcq, dck, dcv = attend_back(
            s["cp"][seg], pair_queries(*head_halves(dot(gbl, attn_t[7][...]))),
            pair_queries(s["cq"][0, rows, :], s["cq"][1, rows, :]),
            pair_lanes(s["ck"][slots, :]), pair_lanes(s["cv"][slots, :]),
        )
        s["dcq"][rows, :] = dcq
        s["dck"][slots, :] = dck
        s["dcv"][slots, :] = dcv
        gm = gm + dot(dck, attn_t[5][...]) + dot(dcv, attn_t[6][...])
        s["gain"][4:5, :] += jnp.sum(gm * xh4, 0, keepdims=True)
        gmem = gate * gz + norm_back(gm, gain[4], xh4, s["rs4"][slots, :])
        gmem = gmem.astype(bf16)
        s["gmem"][slots, :] = gmem
        s["gm"][...] = gmem.astype(f32)
        return carry

    lax.fori_loop(0, NSEG, backward, 0)

    cut = pl.ds(pl.multiple_of(core * BLOCK, BLOCK), BLOCK)

    def put(i, value):
        value = value.astype(bf16)
        for j in range(LANE_CUTS):
            s["dw"][(i * LANE_CUTS + j) * BLOCK : (i * LANE_CUTS + j + 1) * BLOCK, :] = value[:, j * LANES : (j + 1) * LANES]

    def put_products(base, names):
        for i, (left, right) in enumerate(names):
            put(base + i, dot_tn(s[left][:, cut], s[right][...]))

    put_products(0, [("mlow", "dwq"), ("t", "dwk"), ("t", "dwv"), ("wo", "gup")])
    for i in range(4):
        put(4 + i, dot_tn(s["n2"][:, cut], s["gul"][:, i * D : (i + 1) * D]))
    for i in range(4):
        cut_i = pl.ds(pl.multiple_of(core * 4 * BLOCK + i * BLOCK, BLOCK), BLOCK)
        put(8 + i, dot_tn(s["hid"][:, cut_i], s["gyl"][...]))
    put_products(12, [("n1", "dcq"), ("mlow", "dck"), ("mlow", "dcv"), ("co", "gbl")])

    def small_copies(axis):
        here = place[axis]
        return [
            remote(
                s["small"].at[axis, here], s["small"].at[axis, here], s["small_send"].at[axis, step - 1],
                s["small_recv"].at[axis, step - 1], along(axis, (here + step) % 4),
            )
            for step in range(1, 4)
        ]

    def small_start(axis, value):
        s["small"][axis, place[axis]] = value
        for copy in small_copies(axis):
            copy.start()

    def small_finish(axis):
        for copy in small_copies(axis):
            copy.wait()
        return (s["small"][axis, 0] + s["small"][axis, 1]) + (s["small"][axis, 2] + s["small"][axis, 3])

    def part_steps(chunk, part):
        r = CHUNKS[chunk][part] * UNIT
        base = 64 * UNIT * (sum(sum(c) for c in CHUNKS[:chunk]) + sum(CHUNKS[chunk][:part]))
        axes = [(part + i) % 3 for i in range(3)]
        i1, i2, i3 = (place[a] for a in axes)
        right, left = along(axes[0], (i1 + 1) % 4), along(axes[0], (i1 + 3) % 4)
        sems = iter(range(40))
        near, far, mid, last = (s[name][chunk][part] for name in ("near", "far", "mid", "last"))
        dw = s["dw"]

        def copy(src, dst, device):
            i = next(sems)
            return remote(src, dst, s["send"].at[chunk, part, i], s["recv"].at[chunk, part, i], device)

        def block(b, first=0, count=16):
            return rows_at(base + (b % 4) * 16 * r + first * r, count * r)

        def add(refs):
            total = refs[0][...].astype(f32)
            for ref in refs[1:]:
                total += ref[...].astype(f32)
            return total.astype(bf16)

        half0, half1 = pl.ds(0, 8 * r), pl.ds(8 * r, 8 * r)
        a = copy(dw.at[block(i1 + 2, 0, 8)], near.at[0], right)
        b = copy(dw.at[block(i1 + 2, 8, 8)], near.at[1], left)
        c1 = copy(dw.at[block(i1 + 1, 8, 8)], far.at[0, half1], right)
        d0 = copy(dw.at[block(i1 + 3, 0, 8)], far.at[1, half0], left)
        for one in (a, b, c1, d0):
            one.start()
        yield
        a.wait()
        near[0] = add([near.at[0], dw.at[block(i1 + 1, 0, 8)]])
        c0 = copy(near.at[0], far.at[0, half0], right)
        c0.start()
        b.wait()
        near[1] = add([near.at[1], dw.at[block(i1 + 3, 8, 8)]])
        d1 = copy(near.at[1], far.at[1, half1], left)
        d1.start()
        yield
        for one in (c1, d0, c0, d1):
            one.wait()
        far[0] = add([far.at[0], far.at[1], dw.at[block(i1)]])
        two = [
            copy(far.at[0, rows_at((i2 + step) % 4 * 4 * r, 4 * r)], mid.at[step - 1], along(axes[1], (i2 + step) % 4))
            for step in range(1, 4)
        ]
        for one in two:
            one.start()
        yield
        for one in two:
            one.wait()
        mid[0] = add([mid.at[0], mid.at[1], mid.at[2], far.at[0, rows_at(i2 * 4 * r, 4 * r)]])
        three = [
            copy(mid.at[0, rows_at((i3 + step) % 4 * r, r)], last.at[step - 1], along(axes[2], (i3 + step) % 4))
            for step in range(1, 4)
        ]
        for one in three:
            one.start()
        yield
        for one in three:
            one.wait()
        mine = full_ref.at[core]
        home = block(i1, i2 * 4 + i3, 1)
        last[0] = add([last.at[0], last.at[1], last.at[2], mid.at[0, rows_at(i3 * r, r)]])
        keep = pltpu.make_async_copy(last.at[0], mine.at[home], s["own"].at[chunk, part])
        back = [copy(last.at[0], mine.at[home], along(axes[2], (i3 + step) % 4)) for step in range(1, 4)]
        for one in [keep] + back:
            one.start()
        yield
        for one in [keep] + back:
            one.wait()
        home = block(i1, i2 * 4, 4)
        back = [copy(mine.at[home], mine.at[home], along(axes[1], (i2 + step) % 4)) for step in range(1, 4)]
        for one in back:
            one.start()
        yield
        for one in back:
            one.wait()
        home = block(i1)
        to_right = copy(mine.at[home], mine.at[home], right)
        to_left = copy(mine.at[home], mine.at[home], left)
        over = [copy(mine.at[home], mine.at[home], sibling)]
        for one in (to_right, to_left, over[0]):
            one.start()
        yield
        to_right.wait()
        from_left = block(i1 + 3)
        on_right = copy(mine.at[block(i1 + 3, 0, 8)], mine.at[block(i1 + 3, 0, 8)], right)
        on_right.start()
        over.append(copy(mine.at[from_left], mine.at[from_left], sibling))
        over[-1].start()
        to_left.wait()
        from_right = block(i1 + 1)
        on_left = copy(mine.at[block(i1 + 1, 8, 8)], mine.at[block(i1 + 1, 8, 8)], left)
        on_left.start()
        over.append(copy(mine.at[from_right], mine.at[from_right], sibling))
        over[-1].start()
        yield
        on_right.wait()
        on_left.wait()
        opposite = block(i1 + 2)
        over.append(copy(mine.at[opposite], mine.at[opposite], sibling))
        over[-1].start()
        yield
        for one in over:
            one.wait()
        yield

    def short_part_steps(chunk, part):
        r = CHUNKS[chunk][part] * UNIT
        base = 64 * UNIT * (sum(sum(c) for c in CHUNKS[:chunk]) + sum(CHUNKS[chunk][:part]))
        axes = [(part + i) % 3 for i in range(3)]
        i1, i2, i3 = (place[a] for a in axes)
        sems = iter(range(40))
        far, mid, last = (s[name][chunk][part] for name in ("far", "mid", "last"))
        dw, mine = s["dw"], full_ref.at[core]

        def copy(src, dst, device):
            i = next(sems)
            return remote(src, dst, s["send"].at[chunk, part, i], s["recv"].at[chunk, part, i], device)

        def block(first, count):
            return rows_at(base + first * r, count * r)

        def add(refs):
            total = refs[0][...].astype(f32)
            for ref in refs[1:]:
                total += ref[...].astype(f32)
            return total.astype(bf16)

        def others(axis, i):
            return [((i + step) % 4, step - 1, along(axis, (i + step) % 4)) for step in range(1, 4)]

        def all_do(copies, do):
            for one in copies:
                getattr(one, do)()

        one = [copy(dw.at[block(b * 16, 16)], far.at[slot], to) for b, slot, to in others(axes[0], i1)]
        all_do(one, "start")
        yield
        all_do(one, "wait")
        far[0] = add([far.at[0], far.at[1], far.at[2], dw.at[block(i1 * 16, 16)]])
        two = [
            copy(far.at[0, rows_at(b * 4 * r, 4 * r)], mid.at[slot], to) for b, slot, to in others(axes[1], i2)
        ]
        all_do(two, "start")
        yield
        all_do(two, "wait")
        mid[0] = add([mid.at[0], mid.at[1], mid.at[2], far.at[0, rows_at(i2 * 4 * r, 4 * r)]])
        three = [copy(mid.at[0, rows_at(b * r, r)], last.at[slot], to) for b, slot, to in others(axes[2], i3)]
        all_do(three, "start")
        yield
        all_do(three, "wait")
        last[0] = add([last.at[0], last.at[1], last.at[2], mid.at[0, rows_at(i3 * r, r)]])
        home = block(i1 * 16 + i2 * 4 + i3, 1)
        keep = pltpu.make_async_copy(last.at[0], mine.at[home], s["own"].at[chunk, part])
        back = [copy(last.at[0], mine.at[home], to) for _, _, to in others(axes[2], i3)]
        all_do([keep] + back, "start")
        yield
        all_do([keep] + back, "wait")
        home = block(i1 * 16 + i2 * 4, 4)
        back = [copy(mine.at[home], mine.at[home], to) for _, _, to in others(axes[1], i2)]
        all_do(back, "start")
        yield
        all_do(back, "wait")
        home = block(i1 * 16, 16)
        back = [copy(mine.at[home], mine.at[home], to) for _, _, to in others(axes[0], i1)]
        over = [copy(mine.at[home], mine.at[home], sibling)]
        all_do(back + over, "start")
        yield
        all_do(back, "wait")
        for b, _, _ in others(axes[0], i1):
            over.append(copy(mine.at[block(b * 16, 16)], mine.at[block(b * 16, 16)], sibling))
            over[-1].start()
        yield
        all_do(over, "wait")
        yield

    def chunk_steps(chunk):
        parts = [(part_steps if chunk == 0 else short_part_steps)(chunk, part) for part in range(3)]
        for _ in range(10 if chunk == 0 else 8):
            for part in parts:
                next(part)
            yield

    first, second = chunk_steps(0), chunk_steps(1)
    next(first)

    gn1 = dot_nt(s["dcq"][...], attn[4])
    xhat = s["xh1"][...].astype(f32)
    s["gain"][1:2, :] = jnp.sum(gn1 * xhat, 0, keepdims=True)
    ga = s["res"][...] + norm_back(gn1, gain[1], xhat, s["rs1"][...])
    s["res"][...] = ga
    gal = ga.astype(bf16)
    s["gal"][...] = gal
    g0, g1 = head_halves(dot_nt(gal, attn[3]))
    s["cq"][0] = g0
    s["cq"][1] = g1

    def self_backward(seg, carry):
        rows = pl.ds(pl.multiple_of(seg * SEG, SEG), SEG)
        s["dq"][rows, :], s["t"][rows, :], s["gyl"][rows, :] = attend_back(
            s["p"][seg], pair_queries(s["cq"][0, rows, :], s["cq"][1, rows, :]),
            pair_queries(s["q"][0, rows, :], s["q"][1, rows, :]),
            pair_lanes(s["k"][rows, :]), pair_lanes(s["v"][rows, :]),
        )
        return carry

    lax.fori_loop(0, NSEG - 1, self_backward, 0)
    next(first)
    lax.fori_loop(NSEG - 1, NSEG, self_backward, 0)
    gh = dot_nt(s["dq"][...], attn[0]) + dot_nt(s["t"][...], attn[1]) + dot_nt(s["gyl"][...], attn[2])
    xhat = s["xh0"][...].astype(f32)
    s["gain"][0:1, :] = jnp.sum(gh * xhat, 0, keepdims=True)
    s["gtok"][...] = (s["res"][...] + norm_back(gh, gain[0], xhat, s["rs0"][...])).astype(bf16)
    s["gain"][6:7, 0:SLOTS] = jnp.sum(jnp.where(diagonal, s["bias"][:, 0:SLOTS], 0.0), 0, keepdims=True)
    put_products(16, [("h", "dq"), ("h", "t"), ("h", "gyl"), ("o", "gal")])

    next(second)
    small_start(0, s["gain"][...])
    results((2, 3), results_start)
    next(first)
    next(second)
    total = small_finish(0)
    small_start(1, total)
    next(first)
    next(second)
    total = small_finish(1)
    small_start(2, total)
    next(first)
    next(second)
    small_out[...] = small_finish(2)
    next(first)
    next(second)
    next(first)
    next(second)
    next(first)
    next(second)
    next(first)
    next(first)
    next(second)
    results((0, 1, 2, 3), results_finish)


def run_fused(tok, ocot, mcot, mem, lens, attn, win, wout, gains, fw, fb):
    vmem = pl.BlockSpec(memory_space=pltpu.VMEM)
    hbm = pl.BlockSpec(memory_space=pl.ANY)
    return pl.pallas_call(
        fused_kernel,
        out_shape=(
            jax.ShapeDtypeStruct((2, FLAT, LANES), bf16),
            jax.ShapeDtypeStruct((2, SEG, D), bf16),
            jax.ShapeDtypeStruct((2, SLOTS, D), bf16),
            jax.ShapeDtypeStruct((2, SEG, D), bf16),
            jax.ShapeDtypeStruct((2, SLOTS, D), bf16),
            jax.ShapeDtypeStruct((8, D), f32),
        ),
        in_specs=[hbm] * 4 + [vmem] + [hbm] * 3 + [vmem] * 3,
        out_specs=[hbm] * 5 + [vmem],
        scratch_shapes=[scratch_buffers()],
        compiler_params=pltpu.CompilerParams(collective_id=1, has_side_effects=True, vmem_limit_bytes=62 << 20),
        name="layer_and_sums",
    )(tok, ocot, mcot, mem, lens, attn, win, wout, gains, fw, fb)


def widen_kernel(
    full_ref, act_ref, mem_ref, gtok_ref, gmem_ref, small_ref,
    attn_ref, in_ref, out_ref, act_out, mem_out, gtok_out, gmem_out, gains_out, fw_out, fb_out,
    full_s, wide_s, load_sem, store_sem,
):
    def load(i):
        return [
            pltpu.make_async_copy(full_ref.at[half, i], full_s.at[i, half], load_sem.at[i, half]) for half in range(2)
        ]

    def target(i, half):
        if i < 4:
            return attn_ref.at[8 + i, pl.ds(half * BLOCK, BLOCK), :]
        if i < 8:
            return in_ref.at[pl.ds(half * BLOCK, BLOCK), pl.ds((i - 4) * D, D)]
        if i < 12:
            return out_ref.at[pl.ds(half * 4 * BLOCK + (i - 8) * BLOCK, BLOCK), :]
        return attn_ref.at[i - 8 if i < 16 else i - 16, pl.ds(half * BLOCK, BLOCK), :]

    def store(i, half):
        return pltpu.make_async_copy(wide_s.at[i, half], target(i, half), store_sem.at[i, half])

    for i in range(NBLOCKS):
        for copy in load(i):
            copy.start()
    act_out[...] = act_ref[...]
    mem_out[...] = mem_ref[...]
    gtok_out[...] = gtok_ref[...].astype(f32)
    gmem_out[...] = gmem_ref[...].astype(f32)
    gains_out[...] = small_ref[0:5, :]
    fw_out[...] = small_ref[5:6, :]
    fb_out[...] = small_ref[6:7, 0:SLOTS]
    for i in range(NBLOCKS):
        for half, copy in enumerate(load(i)):
            copy.wait()
            for j in range(LANE_CUTS):
                wide_s[i, half, :, j * LANES : (j + 1) * LANES] = full_s[i, half, j].astype(f32)
            store(i, half).start()
    for i in range(NBLOCKS):
        for half in range(2):
            store(i, half).wait()


def run_widen(full, *others):
    hbm = pl.BlockSpec(memory_space=pl.ANY)
    vmem = pl.BlockSpec(memory_space=pltpu.VMEM)
    return pl.pallas_call(
        widen_kernel,
        out_shape=(
            jax.ShapeDtypeStruct((12, D, D), f32),
            jax.ShapeDtypeStruct((D, FF), f32),
            jax.ShapeDtypeStruct((FF, D), f32),
            jax.ShapeDtypeStruct((2, SEG, D), bf16),
            jax.ShapeDtypeStruct((2, SLOTS, D), bf16),
            jax.ShapeDtypeStruct((2, SEG, D), f32),
            jax.ShapeDtypeStruct((2, SLOTS, D), f32),
            jax.ShapeDtypeStruct((5, D), f32),
            jax.ShapeDtypeStruct((1, D), f32),
            jax.ShapeDtypeStruct((1, SLOTS), f32),
        ),
        in_specs=[hbm] + [vmem] * 5,
        out_specs=[hbm] * 3 + [vmem] * 7,
        scratch_shapes=[
            pltpu.VMEM((NBLOCKS, 2, LANE_CUTS, BLOCK, LANES), bf16),
            pltpu.VMEM((NBLOCKS, 2, BLOCK, D), f32),
            pltpu.SemaphoreType.DMA((NBLOCKS, 2)),
            pltpu.SemaphoreType.DMA((NBLOCKS, 2)),
        ],
        compiler_params=pltpu.CompilerParams(vmem_limit_bytes=60 << 20),
        name="widen_gradients",
    )(full, *others)


def body(
    tokens, memory_start, doc_lengths, attn_weights, ffn_in, ffn_out, gains, forget_w, forget_bias,
    out_cotangent, memory_cotangent,
):
    full, *others = run_fused(
        tokens, out_cotangent, memory_cotangent, memory_start, doc_lengths,
        attn_weights.reshape(12, D, D), ffn_in, ffn_out, gains, forget_w.reshape(1, D), forget_bias.reshape(1, SLOTS),
    )
    grad_attn, grad_in, grad_out, acts, mems, gtok, gmem, grad_gains, grad_fw, grad_fb = run_widen(
        full.reshape(2, NBLOCKS, LANE_CUTS, BLOCK, LANES), *others
    )
    return (
        acts, mems, gtok, gmem, grad_attn.reshape(3, 4, D, D), grad_in, grad_out,
        grad_gains, grad_fw.reshape(D), grad_fb.reshape(SLOTS),
    )


def solution(mesh):
    return jax.shard_map(
        body,
        mesh=mesh,
        in_specs=(
            P("doc", "seg", None), P("doc", None, None), P("doc", None), P(), P(), P(), P(), P(), P(),
            P("doc", "seg", None), P("doc", "seg", None),
        ),
        out_specs=(
            P("doc", "seg", None), P("doc", "seg", None), P("doc", "seg", None), P("doc", "seg", None),
            P(), P(), P(), P(), P(), P(),
        ),
        check_vma=False,
    )
```

```python
import functools

import jax
import jax.numpy as jnp
from jax import lax
from jax.experimental import pallas as pl
from jax.experimental.pallas import tpu as pltpu
from jax.sharding import PartitionSpec as P

HEADS = 8
NDOC = 8
D = 512
FF = 2048
SLOTS = 64
SEG = 128
NSEG = 4
ROWS = NSEG * SEG
MROWS = NSEG * SLOTS
PAIRS = 4
PAIR = 128
FCHUNK = 512
BLOCK = 256
NBLOCKS = 20
LANES = 128
LANE_CUTS = D // LANES
FLAT = NBLOCKS * BLOCK * LANE_CUTS
MESH = pl.DeviceIdType.MESH
SCALE = 0.125

f32 = jnp.float32
bf16 = jnp.bfloat16


def dot(a, b):
    return lax.dot_general(a, b, (((1,), (0,)), ((), ())), preferred_element_type=f32)


def dot_nt(a, b):
    return lax.dot_general(a, b, (((1,), (1,)), ((), ())), preferred_element_type=f32)


def dot_tn(a, b):
    return lax.dot_general(a, b, (((0,), (0,)), ((), ())), preferred_element_type=f32)


def norm_stats(values):
    centered = values - jnp.mean(values, -1, keepdims=True)
    rstd = lax.rsqrt(jnp.mean(centered * centered, -1, keepdims=True) + 1e-05)
    return centered * rstd, rstd


def norm_back(grad, gain, xhat, rstd):
    scaled = grad * gain
    mean_one = jnp.mean(scaled, -1, keepdims=True)
    mean_two = jnp.mean(scaled * xhat, -1, keepdims=True)
    return rstd * (scaled - mean_one - xhat * mean_two)


def head_halves(values):
    low_half = lax.broadcasted_iota(jnp.int32, values.shape, 1) % PAIR < PAIR // 2
    return jnp.where(low_half, values, 0.0).astype(bf16), jnp.where(low_half, 0.0, values).astype(bf16)


def join_halves(stacked):
    rows = stacked.shape[0] // 2
    low_half = lax.broadcasted_iota(jnp.int32, (rows, PAIR), 1) < PAIR // 2
    return jnp.where(low_half, stacked[:rows], stacked[rows:])


def attend(queries, keys, values, bias):
    scores = jnp.concatenate([dot_nt(k, q) for k, q in zip(keys, queries)], 1) + bias
    expd = jnp.exp(scores - jnp.max(scores, 0, keepdims=True))
    probs = (expd * (1.0 / jnp.sum(expd, 0, keepdims=True))).astype(bf16)
    width = queries[0].shape[0]
    mixed = [join_halves(dot_tn(probs[:, i * width : (i + 1) * width], v)) for i, v in enumerate(values)]
    return probs, jnp.concatenate(mixed, 1).astype(bf16)


def attend_back(probs, grads, queries, keys, values):
    width = queries[0].shape[0]
    wide = probs.astype(f32)
    dp = jnp.concatenate([dot_nt(v, g) for v, g in zip(values, grads)], 1)
    ds = (wide * (dp - jnp.sum(wide * dp, 0, keepdims=True))).astype(bf16)
    cuts = [slice(i * width, (i + 1) * width) for i in range(PAIRS)]
    dq = [join_halves(dot_tn(ds[:, cut], k)) for cut, k in zip(cuts, keys)]
    dk = [dot(ds[:, cut], q) for cut, q in zip(cuts, queries)]
    dv = [dot(probs[:, cut], g) for cut, g in zip(cuts, grads)]
    join = lambda parts: jnp.concatenate(parts, 1)
    return (join(dq) * SCALE).astype(bf16), join(dk).astype(bf16), join(dv).astype(bf16)


def pair_lanes(values):
    return [values[:, i * PAIR : (i + 1) * PAIR] for i in range(PAIRS)]


def pair_queries(first, second):
    return [jnp.concatenate(halves, 0) for halves in zip(pair_lanes(first), pair_lanes(second))]


def gelu_both(u):
    square = u * u
    tanh = jnp.tanh(0.7978845608028654 * u * (1.0 + 0.044715 * square))
    half = 0.5 + 0.5 * tanh
    slope = half + u * half * (1.0 - tanh) * (0.7978845608028654 + 0.1070322243 * square)
    return u * half, slope


CHUNKS = ((2, 2, 2), (2, 2, 2), (1, 2, 2), (1, 1, 1))
UNIT = 16

TURNED = (5, 6, 7, 8, 9, 10, 11)


def scratch_buffers():
    def rows(dtype=bf16, width=D):
        return pltpu.VMEM((ROWS, width), dtype)

    def slots(dtype=bf16, width=D):
        return pltpu.VMEM((MROWS, width), dtype)

    def two(count):
        return pltpu.VMEM((2, count, D), bf16)

    def parts(shape_of):
        return [[pltpu.VMEM(shape_of(count * UNIT), bf16) for count in chunk] for chunk in CHUNKS]

    dma = pltpu.SemaphoreType.DMA
    return dict(
        attn=pltpu.VMEM((12, D, D), bf16), win=pltpu.VMEM((D, FF), bf16), wout=pltpu.VMEM((FF, D), bf16),
        attn_t=pltpu.VMEM((len(TURNED), D, D), bf16), win_t=pltpu.VMEM((FF, D), bf16), wout_t=pltpu.VMEM((D, FF), bf16),
        tok=rows(), ocot=rows(), mcot=slots(), mem=pltpu.VMEM((SLOTS, D), bf16),
        lens_own=pltpu.VMEM((8, LANES), jnp.int32), lens=pltpu.VMEM((8, LANES), jnp.int32),
        act=rows(), mout=slots(), gtok=rows(), gmem=slots(),
        h=rows(), q=two(ROWS), k=rows(), v=rows(), p=pltpu.VMEM((NSEG, SEG, HEADS * SEG), bf16), o=rows(),
        xh0=rows(), rs0=rows(f32, 1),
        res=rows(f32), n1=rows(), xh1=rows(), rs1=rows(f32, 1), cq=two(ROWS), ck=slots(), cv=slots(),
        cp=pltpu.VMEM((NSEG, SLOTS, HEADS * SEG), bf16), co=rows(),
        n2=rows(), xh2=rows(), rs2=rows(f32, 1), hid=rows(bf16, FF), gd=rows(bf16, FF),
        t=rows(), xh3=rows(), rs3=rows(f32, 1),
        xh4=slots(f32), rs4=slots(f32, 1), mlow=slots(), gate=slots(f32, 1), upd=slots(f32),
        wq=two(MROWS), wk=rows(), wv=rows(), wp=pltpu.VMEM((NSEG, SEG, HEADS * SLOTS), bf16), wo=slots(),
        gup=slots(), dwq=slots(), dwk=rows(), dwv=rows(), gyl=rows(), gul=rows(bf16, FF), gbl=rows(),
        dcq=rows(), dck=slots(), dcv=slots(),
        gal=rows(), dq=rows(), dk=rows(), dv=rows(),
        gain=pltpu.VMEM((8, D), f32), bias=pltpu.VMEM((SLOTS, LANES), f32),
        dw=pltpu.VMEM((FLAT, LANES), bf16),
        near=parts(lambda r: (2, 8 * r, LANES)), far=parts(lambda r: (2, 16 * r, LANES)),
        mid=parts(lambda r: (3, 4 * r, LANES)), quad=parts(lambda r: (4, 4 * r, LANES)), last=parts(lambda r: (4 * r, LANES)),
        small=pltpu.VMEM((3, 5, 8, D), f32),
        in_send=dma((2, 2, 3)), in_recv=dma((4, 3)), first_send=dma((2,)), first_recv=dma((2,)),
        pass_send=dma((3, 3)), pass_recv=dma((3, 3)), in_local=dma((8,)), load=dma((4,)),
        send=dma((len(CHUNKS),)), recv=dma((len(CHUNKS), 3, 10)), own=dma((len(CHUNKS), 3)),
        out_send=dma((2, 4)), out_recv=dma((2, 4)), out_local=dma((4,)),
        small_send=dma((3,)), small_recv=dma((3,)),
    )


def my_place():
    doc = lax.axis_index("doc")
    return lax.axis_index("seg"), doc // 8, (doc // 2) % 4, doc % 2


def device_at(x, y, z, core):
    return (x, y * 8 + z * 2 + core)


def remote(src, dst, send_sem, recv_sem, device):
    return pltpu.make_async_remote_copy(
        src_ref=src, dst_ref=dst, send_sem=send_sem, recv_sem=recv_sem, device_id=device, device_id_type=MESH
    )


def signal(sem, device):
    pl.semaphore_signal(sem, inc=1, device_id=device, device_id_type=MESH)


def fused_kernel(
    tok_ref, ocot_ref, mcot_ref, mem_ref, len_ref, attn_ref, win_ref, wout_ref, gains_ref, fw_ref, fb_ref,
    full_ref, act_out, mout_out, gtok_out, gmem_out, small_out,
    s,
):
    place = my_place()
    x, y, z, core = place
    owner, stream = x // 2, x % 2
    mine_here = owner == core
    sibling = device_at(x, y, z, 1 - core)

    def along(axis, coordinate):
        there = list(place)
        there[axis] = coordinate
        return device_at(*there)

    def rows_at(first, count):
        return pl.ds(pl.multiple_of(first, UNIT), count)

    loads = [
        pltpu.make_async_copy(attn_ref.at[pl.ds(0, 4)], s["attn"].at[pl.ds(0, 4)], s["load"].at[0]),
        pltpu.make_async_copy(attn_ref.at[pl.ds(4, 8)], s["attn"].at[pl.ds(4, 8)], s["load"].at[1]),
        pltpu.make_async_copy(win_ref, s["win"], s["load"].at[2]),
        pltpu.make_async_copy(wout_ref, s["wout"], s["load"].at[3]),
    ]
    for i in (1, 2, 3, 0):
        loads[i].start()

    barrier = pltpu.get_barrier_semaphore()
    for step in range(1, 4):
        signal(barrier, device_at((x + step) % 4, y, z, owner))
    for axis in range(3):
        for step in range(1, 4):
            signal(barrier, along(axis, (place[axis] + step) % 4))
    signal(barrier, sibling)
    for k in range(2):

        @pl.when(jnp.logical_or(2 * core + k != x, owner != core))
        def _():
            signal(barrier, device_at(2 * core + k, y, z, owner))

    s["lens_own"][...] = jnp.zeros_like(s["lens_own"])
    s["lens_own"][0:2, 0:NDOC] = len_ref[...]
    pl.semaphore_wait(barrier, 16 - 3 * mine_here.astype(jnp.int32))

    arrays = [(tok_ref, s["tok"], SEG), (ocot_ref, s["ocot"], SEG), (mcot_ref, s["mcot"], SLOTS)]

    def gather_sends(i, start):
        src, dst, count = arrays[i]
        half = count // 2
        for st in range(2):
            chip = 2 * core + st

            @pl.when(chip != x)
            def _():
                for to_core in range(2):
                    copy = remote(
                        src.at[st, pl.ds(to_core * half, half)], dst.at[rows_at(x * count + to_core * half, half)],
                        s["in_send"].at[st, to_core, i], s["in_recv"].at[x, i], device_at(chip, y, z, to_core),
                    )
                    copy.start() if start else copy.wait_send()

            @pl.when(chip == x)
            def _():
                target = dst.at[rows_at(x * count, count)]
                local = pltpu.make_async_copy(src.at[st], target, s["in_local"].at[i])
                copy = remote(src.at[st], target, s["in_send"].at[st, 0, i], s["in_recv"].at[x, i], sibling)
                if start:
                    local.start()
                    copy.start()
                else:
                    local.wait()
                    copy.wait_send()

    def gather_forward(i):
        src, dst, count = arrays[i]
        half = count // 2
        copies = []
        for step in (1, 3, 2):
            seg = (x + step) % 4
            part = dst.at[rows_at(seg * count + core * half, half)]
            remote(
                part, part, s["in_send"].at[0, 0, i], s["in_recv"].at[seg, i], device_at(seg, y, z, owner)
            ).wait_recv()
            copies.append(remote(part, part, s["pass_send"].at[step - 1, i], s["pass_recv"].at[step - 1, i], sibling))
            copies[-1].start()
        return copies

    def gather_finish(i, copies):
        src, dst, count = arrays[i]
        gather_sends(i, False)
        for copy in copies:
            copy.wait()

        @pl.when(jnp.logical_not(mine_here))
        def _():
            whole = dst.at[rows_at(x * count, count)]
            remote(whole, whole, s["in_send"].at[0, 0, i], s["in_recv"].at[x, i], sibling).wait_recv()

    gather_sends(0, True)

    firsts = [(mem_ref.at[stream], s["mem"]), (s["lens_own"], s["lens"])]
    for i, (src, dst) in enumerate(firsts):

        @pl.when(mine_here)
        def _():
            remote(src, dst, s["first_send"].at[i], s["first_recv"].at[i], sibling).start()
            pltpu.make_async_copy(src, dst, s["in_local"].at[3 + i]).start()

    for load in loads[1:]:
        load.wait()
    for i, index in enumerate(TURNED):
        s["attn_t"][i] = jnp.transpose(s["attn"][index])
    for c in range(0, FF, D):
        s["win_t"][c : c + D, :] = jnp.transpose(s["win"][:, c : c + D])
        s["wout_t"][:, c : c + D] = jnp.transpose(s["wout"][c : c + D, :])
    loads[0].wait()

    for i, (src, dst) in enumerate(firsts):

        @pl.when(mine_here)
        def _():
            remote(src, dst, s["first_send"].at[i], s["first_recv"].at[i], sibling).wait_send()
            pltpu.make_async_copy(src, dst, s["in_local"].at[3 + i]).wait()

        @pl.when(jnp.logical_not(mine_here))
        def _():
            remote(src, dst, s["first_send"].at[i], s["first_recv"].at[i], sibling).wait_recv()

    gather_finish(0, gather_forward(0))
    gather_sends(1, True)
    gather_sends(2, True)

    attn, win, wout = s["attn"], s["win"], s["wout"]
    attn_t = {index: s["attn_t"].at[i] for i, index in enumerate(TURNED)}
    win_t, wout_t = s["win_t"], s["wout_t"]
    gain = [gains_ref[i : i + 1, :] for i in range(5)]
    forget_w = fw_ref[...]
    square = (SLOTS, SLOTS)
    diagonal = lax.broadcasted_iota(jnp.int32, square, 0) == lax.broadcasted_iota(jnp.int32, square, 1)
    forget_bias = jnp.sum(jnp.where(diagonal, jnp.broadcast_to(fb_ref[...], square), 0.0), -1, keepdims=True)

    ends = []
    for j in range(NDOC):
        ends.append(s["lens"][pl.ds(stream, 1), j : j + 1] + (ends[-1] if ends else 0))

    def doc_ids(shape, dim, base):
        pos = lax.broadcasted_iota(jnp.int32, shape, dim) + base
        return sum((end <= pos).astype(jnp.int32) for end in ends)

    def row_cut(seg):
        return slice(seg * SEG, (seg + 1) * SEG)

    def slot_cut(seg):
        return slice(seg * SLOTS, (seg + 1) * SLOTS)

    def together(*works):
        works = list(works)
        while works:
            for work in list(works):
                try:
                    next(work)
                except StopIteration:
                    works.remove(work)

    def self_forward(seg):
        rows = row_cut(seg)
        tok = s["tok"][rows, :].astype(f32)
        xhat, rstd = norm_stats(tok)
        s["xh0"][rows, :] = xhat.astype(bf16)
        s["rs0"][rows, :] = rstd
        h = (xhat * gain[0]).astype(bf16)
        s["h"][rows, :] = h
        yield
        q0, q1 = head_halves(dot(h, attn[0]) * SCALE)
        s["q"][0, rows, :] = q0
        s["q"][1, rows, :] = q1
        yield
        k = dot(h, attn[1]).astype(bf16)
        v = dot(h, attn[2]).astype(bf16)
        s["k"][rows, :] = k
        s["v"][rows, :] = v
        yield
        same = doc_ids((SEG, SEG), 0, seg * SEG) == doc_ids((SEG, SEG), 1, seg * SEG)
        bias = jnp.concatenate([jnp.where(same, 0.0, -1e30)] * HEADS, 1)
        s["p"][seg], o = attend(pair_queries(q0, q1), pair_lanes(k), pair_lanes(v), bias)
        s["o"][rows, :] = o
        yield
        res = tok + dot(o, attn[3])
        s["res"][rows, :] = res
        xhat, rstd = norm_stats(res)
        s["xh1"][rows, :] = xhat.astype(bf16)
        s["rs1"][rows, :] = rstd
        n1 = (xhat * gain[1]).astype(bf16)
        s["n1"][rows, :] = n1
        yield
        s["cq"][0, rows, :], s["cq"][1, rows, :] = head_halves(dot(n1, attn[4]) * SCALE)
        yield

    def forward(seg, mem):
        rows, slots = row_cut(seg), slot_cut(seg)
        xhat, rstd = norm_stats(mem)
        s["xh4"][slots, :] = xhat
        s["rs4"][slots, :] = rstd
        m = xhat * gain[4]
        mlow = m.astype(bf16)
        s["mlow"][slots, :] = mlow
        ck = dot(mlow, attn[5]).astype(bf16)
        cv = dot(mlow, attn[6]).astype(bf16)
        s["ck"][slots, :] = ck
        s["cv"][slots, :] = cv
        yield
        s["cp"][seg], co = attend(
            pair_queries(s["cq"][0, rows, :], s["cq"][1, rows, :]), pair_lanes(ck), pair_lanes(cv), 0.0
        )
        s["co"][rows, :] = co
        yield
        res = s["res"][rows, :] + dot(co, attn[7])
        xhat, rstd = norm_stats(res)
        s["xh2"][rows, :] = xhat.astype(bf16)
        s["rs2"][rows, :] = rstd
        n2 = (xhat * gain[2]).astype(bf16)
        s["n2"][rows, :] = n2
        yield
        for c in range(0, FF, FCHUNK):
            hid, slope = gelu_both(dot(n2, win[:, c : c + FCHUNK]))
            hid = hid.astype(bf16)
            s["hid"][rows, c : c + FCHUNK] = hid
            s["gd"][rows, c : c + FCHUNK] = slope.astype(bf16)
            res = res + dot(hid, wout[c : c + FCHUNK, :])
            yield
        s["act"][rows, :] = res.astype(bf16)
        xhat, rstd = norm_stats(res)
        s["xh3"][rows, :] = xhat.astype(bf16)
        s["rs3"][rows, :] = rstd
        t = (xhat * gain[3]).astype(bf16)
        s["t"][rows, :] = t
        yield
        gate = jax.nn.sigmoid(jnp.sum(m * forget_w, -1, keepdims=True) + forget_bias)
        s["gate"][slots, :] = gate
        wq0, wq1 = head_halves(dot(mlow, attn[8]) * SCALE)
        s["wq"][0, slots, :] = wq0
        s["wq"][1, slots, :] = wq1
        wk = dot(t, attn[9]).astype(bf16)
        wv = dot(t, attn[10]).astype(bf16)
        s["wk"][rows, :] = wk
        s["wv"][rows, :] = wv
        yield
        pos = lax.broadcasted_iota(jnp.int32, (SEG, HEADS * SLOTS), 0) + seg * SEG
        s["wp"][seg], wo = attend(
            pair_queries(wq0, wq1), pair_lanes(wk), pair_lanes(wv), jnp.where(pos < ends[-1], 0.0, -1e30)
        )
        s["wo"][slots, :] = wo
        yield
        update = dot(wo, attn[11])
        s["upd"][slots, :] = mem - update
        s["mout"][slots, :] = (update + gate * (mem - update)).astype(bf16)
        yield

    together(self_forward(0))
    passed = []
    for seg in range(NSEG):
        mem = s["mem"][...] if seg == 0 else s["mout"][slot_cut(seg - 1), :]
        works = [forward(seg, mem.astype(f32))]
        if seg < NSEG - 1:
            works.append(self_forward(seg + 1))
        together(*works)
        if seg in (1, 2):
            passed.append(gather_forward(seg))

    def results(indices, do):
        for k in range(2):
            seg = 2 * core + k
            here = jnp.logical_and(seg == x, mine_here)
            peer = device_at(seg, y, z, owner)
            sources = [
                (s["act"].at[rows_at(seg * SEG, SEG)], act_out), (s["mout"].at[rows_at(seg * SLOTS, SLOTS)], mout_out),
                (s["gtok"].at[rows_at(seg * SEG, SEG)], gtok_out), (s["gmem"].at[rows_at(seg * SLOTS, SLOTS)], gmem_out),
            ]
            for i in indices:
                src, dst = sources[i]

                @pl.when(jnp.logical_not(here))
                def _():
                    do(
                        remote(src, dst.at[stream], s["out_send"].at[k, i], s["out_recv"].at[stream, i], peer),
                        remote(src, dst.at[k], s["out_send"].at[k, i], s["out_recv"].at[k, i], peer),
                    )

                @pl.when(here)
                def _():
                    do(pltpu.make_async_copy(src, dst.at[stream], s["out_local"].at[i]), None)

    def results_start(copy, back):
        copy.start()

    def results_finish(copy, back):
        if back is None:
            copy.wait()
        else:
            copy.wait_send()
            back.wait_recv()

    results((0, 1), results_start)
    for i in (1, 2):
        gather_finish(i, passed[i - 1])

    s["gain"][...] = jnp.zeros_like(s["gain"])
    s["bias"][...] = jnp.zeros_like(s["bias"])

    def backward(seg):
        rows, slots = row_cut(seg), slot_cut(seg)
        gz = s["mcot"][slots, :].astype(f32)
        if seg < NSEG - 1:
            gz = (gz + s["gmem"][slot_cut(seg + 1), :].astype(f32)).astype(bf16).astype(f32)
        gate = s["gate"][slots, :]
        gup = ((1.0 - gate) * gz).astype(bf16)
        s["gup"][slots, :] = gup
        g_wo = head_halves(dot(gup, attn_t[11][...]))
        yield
        dwq, dwk, dwv = attend_back(
            s["wp"][seg], pair_queries(*g_wo), pair_queries(s["wq"][0, slots, :], s["wq"][1, slots, :]),
            pair_lanes(s["wk"][rows, :]), pair_lanes(s["wv"][rows, :]),
        )
        s["dwq"][slots, :] = dwq
        s["dwk"][rows, :] = dwk
        s["dwv"][rows, :] = dwv
        yield
        gt = dot(dwk, attn_t[9][...]) + dot(dwv, attn_t[10][...])
        xhat = s["xh3"][rows, :].astype(f32)
        s["gain"][3:4, :] += jnp.sum(gt * xhat, 0, keepdims=True)
        gy = s["ocot"][rows, :].astype(f32) + norm_back(gt, gain[3], xhat, s["rs3"][rows, :])
        gyl = gy.astype(bf16)
        s["gyl"][rows, :] = gyl
        yield
        gn2 = jnp.zeros((SEG, D), f32)
        for c in range(0, FF, FCHUNK):
            ghid = dot(gyl, wout_t[:, c : c + FCHUNK])
            gul = (ghid * s["gd"][rows, c : c + FCHUNK].astype(f32)).astype(bf16)
            s["gul"][rows, c : c + FCHUNK] = gul
            gn2 = gn2 + dot(gul, win_t[c : c + FCHUNK, :])
            yield
        xhat = s["xh2"][rows, :].astype(f32)
        s["gain"][2:3, :] += jnp.sum(gn2 * xhat, 0, keepdims=True)
        gb = gy + norm_back(gn2, gain[2], xhat, s["rs2"][rows, :])
        s["res"][rows, :] = gb
        gbl = gb.astype(bf16)
        s["gbl"][rows, :] = gbl
        yield
        g_co = head_halves(dot(gbl, attn_t[7][...]))
        dgate = jnp.sum(gz * s["upd"][slots, :], -1, keepdims=True) * gate * (1.0 - gate)
        xh4 = s["xh4"][slots, :]
        s["gain"][5:6, :] += jnp.sum(dgate * (xh4 * gain[4]), 0, keepdims=True)
        s["bias"][...] += jnp.broadcast_to(dgate, (SLOTS, LANES))
        gm = dgate * forget_w + dot(dwq, attn_t[8][...])
        yield
        dcq, dck, dcv = attend_back(
            s["cp"][seg], pair_queries(*g_co), pair_queries(s["cq"][0, rows, :], s["cq"][1, rows, :]),
            pair_lanes(s["ck"][slots, :]), pair_lanes(s["cv"][slots, :]),
        )
        s["dcq"][rows, :] = dcq
        s["dck"][slots, :] = dck
        s["dcv"][slots, :] = dcv
        yield
        gm = gm + dot(dck, attn_t[5][...]) + dot(dcv, attn_t[6][...])
        s["gain"][4:5, :] += jnp.sum(gm * xh4, 0, keepdims=True)
        s["gmem"][slots, :] = (gate * gz + norm_back(gm, gain[4], xh4, s["rs4"][slots, :])).astype(bf16)
        yield

    def self_backward(seg):
        rows = row_cut(seg)
        gn1 = dot_nt(s["dcq"][rows, :], attn[4])
        yield
        xhat = s["xh1"][rows, :].astype(f32)
        s["gain"][1:2, :] += jnp.sum(gn1 * xhat, 0, keepdims=True)
        ga = s["res"][rows, :] + norm_back(gn1, gain[1], xhat, s["rs1"][rows, :])
        gal = ga.astype(bf16)
        s["gal"][rows, :] = gal
        yield
        g_o = head_halves(dot_nt(gal, attn[3]))
        yield
        dq, dk, dv = attend_back(
            s["p"][seg], pair_queries(*g_o), pair_queries(s["q"][0, rows, :], s["q"][1, rows, :]),
            pair_lanes(s["k"][rows, :]), pair_lanes(s["v"][rows, :]),
        )
        s["dq"][rows, :] = dq
        s["dk"][rows, :] = dk
        s["dv"][rows, :] = dv
        yield
        gh = dot_nt(dq, attn[0]) + dot_nt(dk, attn[1])
        yield
        gh = gh + dot_nt(dv, attn[2])
        xhat = s["xh0"][rows, :].astype(f32)
        s["gain"][0:1, :] += jnp.sum(gh * xhat, 0, keepdims=True)
        s["gtok"][rows, :] = (ga + norm_back(gh, gain[0], xhat, s["rs0"][rows, :])).astype(bf16)
        yield

    for seg in reversed(range(NSEG)):
        works = [backward(seg)]
        if seg < NSEG - 1:
            works.append(self_backward(seg + 1))
        together(*works)
    results((3,), results_start)

    cut = pl.ds(pl.multiple_of(core * BLOCK, BLOCK), BLOCK)

    def put(i, value):
        value = value.astype(bf16)
        for j in range(LANE_CUTS):
            s["dw"][(i * LANE_CUTS + j) * BLOCK : (i * LANE_CUTS + j + 1) * BLOCK, :] = value[:, j * LANES : (j + 1) * LANES]

    def put_products(base, names):
        for i, (left, right) in enumerate(names):
            put(base + i, dot_tn(s[left][:, cut], s[right][...]))

    def small_start(axis, value):
        here = place[axis]
        s["small"][axis, here] = value
        for step in range(1, 4):
            own = s["small"].at[axis, here]
            remote(own, own, s["small_send"].at[axis], s["small_recv"].at[axis], along(axis, (here + step) % 4)).start()

    def all_moved(ref, send_sem, recv_sem):
        copy = remote(ref, ref, send_sem, recv_sem, sibling)
        copy.wait_send()
        copy.wait_recv()

    def small_finish(axis):
        all_moved(s["small"].at[axis, pl.ds(0, 3)], s["small_send"].at[axis], s["small_recv"].at[axis])
        return (s["small"][axis, 0] + s["small"][axis, 1]) + (s["small"][axis, 2] + s["small"][axis, 3])

    def others(axis, i):
        return [((i + step) % 4, step - 1, along(axis, (i + step) % 4)) for step in range(1, 4)]

    def add(refs):
        total = refs[0][...].astype(f32)
        for ref in refs[1:]:
            total += ref[...].astype(f32)
        return total.astype(bf16)

    def part_place(chunk, part):
        r = CHUNKS[chunk][part] * UNIT
        base = 64 * UNIT * (sum(sum(c) for c in CHUNKS[:chunk]) + sum(CHUNKS[chunk][:part]))
        axes = [(part + i) % 3 for i in range(3)]
        return r, base, axes, [place[a] for a in axes]

    def part_steps(chunk, part):
        r, base, axes, (i1, i2, i3) = part_place(chunk, part)
        right, left = along(axes[0], (i1 + 1) % 4), along(axes[0], (i1 + 3) % 4)
        near, far, mid, quad, last = (s[name][chunk][part] for name in ("near", "far", "mid", "quad", "last"))
        dw, mine = s["dw"], full_ref.at[core]

        def copy(src, dst, device, i):
            remote(src, dst, s["send"].at[chunk], s["recv"].at[chunk, part, i], device).start()

        def arrived(ref, i):
            remote(ref, ref, s["send"].at[chunk], s["recv"].at[chunk, part, i], sibling).wait_recv()

        def block(b, first=0, count=16):
            return rows_at(base + (b % 4) * 16 * r + first * r, count * r)

        def pass_on(rows, device, i):
            copy(mine.at[rows], mine.at[rows], device, i)

        half0, half1 = pl.ds(0, 8 * r), pl.ds(8 * r, 8 * r)
        copy(dw.at[block(i1 + 2, 0, 8)], near.at[0], right, 0)
        copy(dw.at[block(i1 + 2, 8, 8)], near.at[1], left, 1)
        copy(dw.at[block(i1 + 1, 8, 8)], far.at[0, half1], right, 2)
        copy(dw.at[block(i1 + 3, 0, 8)], far.at[1, half0], left, 2)
        yield
        arrived(near.at[0], 0)
        near[0] = add([near.at[0], dw.at[block(i1 + 1, 0, 8)]])
        copy(near.at[0], far.at[0, half0], right, 2)
        arrived(near.at[1], 1)
        near[1] = add([near.at[1], dw.at[block(i1 + 3, 8, 8)]])
        copy(near.at[1], far.at[1, half1], left, 2)
        yield
        arrived(far, 2)
        far[0] = add([far.at[0], far.at[1], dw.at[block(i1)]])
        for b, slot, to in others(axes[1], i2):
            copy(far.at[0, rows_at(b * 4 * r, 4 * r)], mid.at[slot], to, 3)
        yield
        arrived(mid, 3)
        quad[i3] = add([mid.at[0], mid.at[1], mid.at[2], far.at[0, rows_at(i2 * 4 * r, 4 * r)]])
        for _, _, to in others(axes[2], i3):
            copy(quad.at[i3], quad.at[i3], to, 4)
        yield
        arrived(quad.at[pl.ds(0, 3)], 4)
        last[...] = add([quad.at[i] for i in range(4)])
        home = rows_at(base + (i1 * 16 + i2 * 4) * r, 4 * r)
        keep = pltpu.make_async_copy(last, mine.at[home], s["own"].at[chunk, part])
        keep.start()
        for _, _, to in others(axes[1], i2):
            copy(last, mine.at[home], to, 5)
        yield
        keep.wait()
        arrived(mine.at[rows_at(base, 12 * r)], 5)
        pass_on(block(i1), right, 6)
        pass_on(block(i1), left, 7)
        pass_on(block(i1), sibling, 9)
        yield
        arrived(mine.at[block(i1 + 3)], 6)
        pass_on(block(i1 + 3, 0, 8), right, 8)
        pass_on(block(i1 + 3), sibling, 9)
        arrived(mine.at[block(i1 + 1)], 7)
        pass_on(block(i1 + 1, 8, 8), left, 8)
        pass_on(block(i1 + 1), sibling, 9)
        yield
        arrived(mine.at[block(i1 + 2)], 8)
        pass_on(block(i1 + 2), sibling, 9)
        yield
        arrived(full_ref.at[1 - core, rows_at(base, 64 * r)], 9)
        if part == 2:
            sent = full_ref.at[core, rows_at(0, 196 * UNIT * sum(CHUNKS[chunk]))]
            remote(sent, sent, s["send"].at[chunk], s["recv"].at[chunk, part, 0], sibling).wait_send()
        yield

    def chunk_steps(chunk):
        parts = [part_steps(chunk, part) for part in range(3)]
        while True:
            for part in parts:
                next(part)
            yield

    chunks = [chunk_steps(chunk) for chunk in range(len(CHUNKS))]

    def go(*order):
        for chunk in order:
            next(chunks[chunk])

    for i in range(4):
        put(i, dot_tn(s["n2"][:, cut], s["gul"][:, i * D : (i + 1) * D]))
    for i in range(4):
        if i == 2:
            go(0)
        cut_i = pl.ds(pl.multiple_of(core * 4 * BLOCK + i * BLOCK, BLOCK), BLOCK)
        put(4 + i, dot_tn(s["hid"][:, cut_i], s["gyl"][...]))
    put_products(8, [("mlow", "dwq"), ("t", "dwk"), ("t", "dwv"), ("wo", "gup")])
    go(1)
    put_products(12, [("n1", "dcq"), ("mlow", "dck"), ("mlow", "dcv"), ("co", "gbl")])
    last_segment = self_backward(0)
    for _ in range(3):
        next(last_segment)
    put_products(16, [("o", "gal")])
    together(last_segment)
    s["gain"][6:7, 0:SLOTS] = jnp.sum(jnp.where(diagonal, s["bias"][:, 0:SLOTS], 0.0), 0, keepdims=True)
    go(2, 0)
    small_start(0, s["gain"][...])
    results((2,), results_start)
    put_products(17, [("h", "dq"), ("h", "dk"), ("h", "dv")])
    go(1, 3, 2, 0)
    total = small_finish(0)
    small_start(1, total)
    go(3, 1, 2, 0)
    total = small_finish(1)
    small_start(2, total)
    go(3, 1, 2, 3, 0, 1)
    small_out[...] = small_finish(2)
    go(2, 3, 0, 1, 3, 2, 0, 3, 1, 2, 3, 0, 1, 3, 2, 0, 1, 2)
    results((0, 1, 2, 3), results_finish)


def run_fused(tok, ocot, mcot, mem, lens, attn, win, wout, gains, fw, fb):
    vmem = pl.BlockSpec(memory_space=pltpu.VMEM)
    hbm = pl.BlockSpec(memory_space=pl.ANY)
    return pl.pallas_call(
        fused_kernel,
        out_shape=(
            jax.ShapeDtypeStruct((2, FLAT, LANES), bf16),
            jax.ShapeDtypeStruct((2, SEG, D), bf16),
            jax.ShapeDtypeStruct((2, SLOTS, D), bf16),
            jax.ShapeDtypeStruct((2, SEG, D), bf16),
            jax.ShapeDtypeStruct((2, SLOTS, D), bf16),
            jax.ShapeDtypeStruct((8, D), f32),
        ),
        in_specs=[hbm] * 4 + [vmem] + [hbm] * 3 + [vmem] * 3,
        out_specs=[hbm] * 5 + [vmem],
        scratch_shapes=[scratch_buffers()],
        compiler_params=pltpu.CompilerParams(collective_id=1, has_side_effects=True, vmem_limit_bytes=63 << 20),
        name="layer_and_sums",
    )(tok, ocot, mcot, mem, lens, attn, win, wout, gains, fw, fb)


def widen_kernel(
    full_ref, act_ref, mem_ref, gtok_ref, gmem_ref, small_ref,
    attn_ref, in_ref, out_ref, act_out, mem_out, gtok_out, gmem_out, gains_out, fw_out, fb_out,
    full_s, wide_s, load_sem, store_sem,
):
    def load(i):
        return [
            pltpu.make_async_copy(full_ref.at[half, i], full_s.at[i, half], load_sem.at[i, half]) for half in range(2)
        ]

    def target(i, half):
        if i < 4:
            return in_ref.at[pl.ds(half * BLOCK, BLOCK), pl.ds(i * D, D)]
        if i < 8:
            return out_ref.at[pl.ds(half * 4 * BLOCK + (i - 4) * BLOCK, BLOCK), :]
        return attn_ref.at[i if i < 12 else i - 8 if i < 16 else 3 if i == 16 else i - 17, pl.ds(half * BLOCK, BLOCK), :]

    def store(i, half):
        return pltpu.make_async_copy(wide_s.at[i, half], target(i, half), store_sem.at[i, half])

    for i in range(NBLOCKS):
        for copy in load(i):
            copy.start()
    act_out[...] = act_ref[...]
    mem_out[...] = mem_ref[...]
    gtok_out[...] = gtok_ref[...].astype(f32)
    gmem_out[...] = gmem_ref[...].astype(f32)
    gains_out[...] = small_ref[0:5, :]
    fw_out[...] = small_ref[5:6, :]
    fb_out[...] = small_ref[6:7, 0:SLOTS]
    for i in range(NBLOCKS):
        for half, copy in enumerate(load(i)):
            copy.wait()
            for j in range(LANE_CUTS):
                wide_s[i, half, :, j * LANES : (j + 1) * LANES] = full_s[i, half, j].astype(f32)
            store(i, half).start()
    for i in range(NBLOCKS):
        for half in range(2):
            store(i, half).wait()


def run_widen(full, *others):
    hbm = pl.BlockSpec(memory_space=pl.ANY)
    vmem = pl.BlockSpec(memory_space=pltpu.VMEM)
    return pl.pallas_call(
        widen_kernel,
        out_shape=(
            jax.ShapeDtypeStruct((12, D, D), f32),
            jax.ShapeDtypeStruct((D, FF), f32),
            jax.ShapeDtypeStruct((FF, D), f32),
            jax.ShapeDtypeStruct((2, SEG, D), bf16),
            jax.ShapeDtypeStruct((2, SLOTS, D), bf16),
            jax.ShapeDtypeStruct((2, SEG, D), f32),
            jax.ShapeDtypeStruct((2, SLOTS, D), f32),
            jax.ShapeDtypeStruct((5, D), f32),
            jax.ShapeDtypeStruct((1, D), f32),
            jax.ShapeDtypeStruct((1, SLOTS), f32),
        ),
        in_specs=[hbm] + [vmem] * 5,
        out_specs=[hbm] * 3 + [vmem] * 7,
        scratch_shapes=[
            pltpu.VMEM((NBLOCKS, 2, LANE_CUTS, BLOCK, LANES), bf16),
            pltpu.VMEM((NBLOCKS, 2, BLOCK, D), f32),
            pltpu.SemaphoreType.DMA((NBLOCKS, 2)),
            pltpu.SemaphoreType.DMA((NBLOCKS, 2)),
        ],
        compiler_params=pltpu.CompilerParams(vmem_limit_bytes=60 << 20),
        name="widen_gradients",
    )(full, *others)


def body(
    tokens, memory_start, doc_lengths, attn_weights, ffn_in, ffn_out, gains, forget_w, forget_bias,
    out_cotangent, memory_cotangent,
):
    full, *others = run_fused(
        tokens, out_cotangent, memory_cotangent, memory_start, doc_lengths,
        attn_weights.reshape(12, D, D), ffn_in, ffn_out, gains, forget_w.reshape(1, D), forget_bias.reshape(1, SLOTS),
    )
    grad_attn, grad_in, grad_out, acts, mems, gtok, gmem, grad_gains, grad_fw, grad_fb = run_widen(
        full.reshape(2, NBLOCKS, LANE_CUTS, BLOCK, LANES), *others
    )
    return (
        acts, mems, gtok, gmem, grad_attn.reshape(3, 4, D, D), grad_in, grad_out,
        grad_gains, grad_fw.reshape(D), grad_fb.reshape(SLOTS),
    )


def solution(mesh):
    return jax.shard_map(
        body,
        mesh=mesh,
        in_specs=(
            P("doc", "seg", None), P("doc", None, None), P("doc", None), P(), P(), P(), P(), P(), P(),
            P("doc", "seg", None), P("doc", "seg", None),
        ),
        out_specs=(
            P("doc", "seg", None), P("doc", "seg", None), P("doc", "seg", None), P("doc", "seg", None),
            P(), P(), P(), P(), P(), P(),
        ),
        check_vma=False,
    )
```

```python
import functools

import jax
import jax.numpy as jnp
from jax import lax
from jax.experimental import pallas as pl
from jax.experimental.pallas import tpu as pltpu
from jax.sharding import PartitionSpec as P

HEADS = 8
NDOC = 8
D = 512
FF = 2048
SLOTS = 64
SEG = 128
NSEG = 4
ROWS = NSEG * SEG
MROWS = NSEG * SLOTS
PAIRS = 4
PAIR = 128
FCHUNK = 2048
BLOCK = 256
NBLOCKS = 20
LANES = 128
LANE_CUTS = D // LANES
FLAT = NBLOCKS * BLOCK * LANE_CUTS
MESH = pl.DeviceIdType.MESH
SCALE = 0.125

f32 = jnp.float32
bf16 = jnp.bfloat16


def dot(a, b):
    return lax.dot_general(a, b, (((1,), (0,)), ((), ())), preferred_element_type=f32)


def dot_nt(a, b):
    return lax.dot_general(a, b, (((1,), (1,)), ((), ())), preferred_element_type=f32)


def dot_tn(a, b):
    return lax.dot_general(a, b, (((0,), (0,)), ((), ())), preferred_element_type=f32)


def norm_stats(values):
    centered = values - jnp.mean(values, -1, keepdims=True)
    rstd = lax.rsqrt(jnp.mean(centered * centered, -1, keepdims=True) + 1e-05)
    return centered * rstd, rstd


def norm_back(grad, gain, xhat, rstd):
    scaled = grad * gain
    mean_one = jnp.mean(scaled, -1, keepdims=True)
    mean_two = jnp.mean(scaled * xhat, -1, keepdims=True)
    return rstd * (scaled - mean_one - xhat * mean_two)


def head_halves(values):
    low_half = lax.broadcasted_iota(jnp.int32, (16, values.shape[1]), 1) % PAIR < PAIR // 2
    first = jnp.where(low_half, 1.0, 0.0).astype(bf16)[0:1, :]
    second = jnp.where(low_half, 0.0, 1.0).astype(bf16)[0:1, :]
    values = values.astype(bf16)
    return values * first, values * second


def join_halves(stacked):
    rows = stacked.shape[0] // 2
    low_half = lax.broadcasted_iota(jnp.int32, (rows, PAIR), 1) < PAIR // 2
    return jnp.where(low_half, stacked[:rows], stacked[rows:])


def attend(queries, keys, values, bias):
    scores = jnp.concatenate([dot_nt(k, q) for k, q in zip(keys, queries)], 1) + bias
    expd = jnp.exp(scores - jnp.max(scores, 0, keepdims=True))
    probs = (expd * (1.0 / jnp.sum(expd, 0, keepdims=True))).astype(bf16)
    width = queries[0].shape[0]
    mixed = [join_halves(dot_tn(probs[:, i * width : (i + 1) * width], v)) for i, v in enumerate(values)]
    return probs, jnp.concatenate(mixed, 1).astype(bf16)


def attend_back(probs, grads, queries, keys, values):
    width = queries[0].shape[0]
    wide = probs.astype(f32)
    dp = jnp.concatenate([dot_nt(v, g) for v, g in zip(values, grads)], 1)
    ds = (wide * (dp - jnp.sum(wide * dp, 0, keepdims=True))).astype(bf16)
    cuts = [slice(i * width, (i + 1) * width) for i in range(PAIRS)]
    dq = [join_halves(dot_tn(ds[:, cut], k)) for cut, k in zip(cuts, keys)]
    dk = [dot(ds[:, cut], q) for cut, q in zip(cuts, queries)]
    dv = [dot(probs[:, cut], g) for cut, g in zip(cuts, grads)]
    join = lambda parts: jnp.concatenate(parts, 1)
    return (join(dq) * SCALE).astype(bf16), join(dk).astype(bf16), join(dv).astype(bf16)


def pair_lanes(values):
    return [values[:, i * PAIR : (i + 1) * PAIR] for i in range(PAIRS)]


def pair_queries(first, second):
    return [jnp.concatenate(halves, 0) for halves in zip(pair_lanes(first), pair_lanes(second))]


def gelu_both(u):
    square = u * u
    tanh = jnp.tanh(0.7978845608028654 * u * (1.0 + 0.044715 * square))
    half = 0.5 + 0.5 * tanh
    hidden = u * half
    rest, square = (1.0 - tanh).astype(bf16), square.astype(bf16)
    slope = half.astype(bf16) + hidden.astype(bf16) * rest * (bf16(0.7978845608028654) + bf16(0.1070322243) * square)
    return hidden, slope


CHUNKS = ((2, 2, 2), (2, 2, 2), (1, 2, 2), (1, 1, 1))
UNIT = 16

TURNED = (5, 6, 7, 8, 9, 10, 11)


def scratch_buffers():
    def rows(dtype=bf16, width=D):
        return pltpu.VMEM((ROWS, width), dtype)

    def slots(dtype=bf16, width=D):
        return pltpu.VMEM((MROWS, width), dtype)

    def two(count):
        return pltpu.VMEM((2, count, D), bf16)

    def parts(shape_of):
        return [[pltpu.VMEM(shape_of(count * UNIT), bf16) for count in chunk] for chunk in CHUNKS]

    dma = pltpu.SemaphoreType.DMA
    return dict(
        attn=pltpu.VMEM((12, D, D), bf16), win=pltpu.VMEM((D, FF), bf16), wout=pltpu.VMEM((FF, D), bf16),
        attn_t=pltpu.VMEM((len(TURNED), D, D), bf16), win_t=pltpu.VMEM((FF, D), bf16), wout_t=pltpu.VMEM((D, FF), bf16),
        tok=rows(), ocot=rows(), mcot=slots(), mem=pltpu.VMEM((SLOTS, D), bf16),
        lens_own=pltpu.VMEM((8, LANES), jnp.int32), lens=pltpu.VMEM((8, LANES), jnp.int32),
        act=rows(), mout=slots(), gtok=rows(), gmem=slots(),
        h=rows(), q=two(ROWS), k=rows(), v=rows(), p=pltpu.VMEM((NSEG, SEG, HEADS * SEG), bf16), o=rows(),
        xh0=rows(), rs0=rows(f32, 1),
        res=rows(f32), n1=rows(), xh1=rows(), rs1=rows(f32, 1), cq=two(ROWS), ck=slots(), cv=slots(),
        cp=pltpu.VMEM((NSEG, SLOTS, HEADS * SEG), bf16), co=rows(),
        n2=rows(), xh2=rows(), rs2=rows(f32, 1), hid=rows(bf16, FF), gul=rows(bf16, FF),
        t=rows(), xh3=rows(), rs3=rows(f32, 1),
        xh4=slots(f32), rs4=slots(f32, 1), mlow=slots(), gate=slots(f32, 1), upd=slots(f32),
        wq=two(MROWS), wk=rows(), wv=rows(), wp=pltpu.VMEM((NSEG, SEG, HEADS * SLOTS), bf16), wo=slots(),
        gup=slots(), dwq=slots(), dwk=rows(), dwv=rows(), gyl=rows(), gbl=rows(),
        dcq=rows(), dck=slots(), dcv=slots(),
        gal=rows(), dq=rows(), dk=rows(), dv=rows(),
        gain=pltpu.VMEM((8, D), f32), bias=pltpu.VMEM((SLOTS, LANES), f32),
        dw=pltpu.VMEM((FLAT, LANES), bf16),
        near=parts(lambda r: (2, 8 * r, LANES)), far=parts(lambda r: (2, 16 * r, LANES)),
        mid=parts(lambda r: (3, 4 * r, LANES)), quad=parts(lambda r: (4, 4 * r, LANES)), last=parts(lambda r: (4 * r, LANES)),
        small=pltpu.VMEM((3, 5, 8, D), f32),
        in_send=dma((2, 2, 3)), in_recv=dma((4, 3)), first_send=dma((2,)), first_recv=dma((2,)),
        pass_send=dma((3, 3)), pass_recv=dma((3, 3)), in_local=dma((8,)), load=dma((4,)),
        send=dma((len(CHUNKS),)), recv=dma((len(CHUNKS), 3, 10)), own=dma((len(CHUNKS), 3)),
        out_send=dma((2, 4)), out_recv=dma((2, 4)), out_local=dma((4,)),
        small_send=dma((3,)), small_recv=dma((3,)),
    )


def my_place():
    doc = lax.axis_index("doc")
    return lax.axis_index("seg"), doc // 8, (doc // 2) % 4, doc % 2


def device_at(x, y, z, core):
    return (x, y * 8 + z * 2 + core)


def remote(src, dst, send_sem, recv_sem, device):
    return pltpu.make_async_remote_copy(
        src_ref=src, dst_ref=dst, send_sem=send_sem, recv_sem=recv_sem, device_id=device, device_id_type=MESH
    )


def signal(sem, device):
    pl.semaphore_signal(sem, inc=1, device_id=device, device_id_type=MESH)


def fused_kernel(
    tok_ref, ocot_ref, mcot_ref, mem_ref, len_ref, attn_ref, win_ref, wout_ref, gains_ref, fw_ref, fb_ref,
    full_ref, act_out, mout_out, gtok_out, gmem_out, small_out,
    s,
):
    place = my_place()
    x, y, z, core = place
    owner, stream = x // 2, x % 2
    mine_here = owner == core
    sibling = device_at(x, y, z, 1 - core)

    def along(axis, coordinate):
        there = list(place)
        there[axis] = coordinate
        return device_at(*there)

    def rows_at(first, count):
        return pl.ds(pl.multiple_of(first, UNIT), count)

    loads = [
        pltpu.make_async_copy(attn_ref.at[pl.ds(0, 4)], s["attn"].at[pl.ds(0, 4)], s["load"].at[0]),
        pltpu.make_async_copy(attn_ref.at[pl.ds(4, 8)], s["attn"].at[pl.ds(4, 8)], s["load"].at[1]),
        pltpu.make_async_copy(win_ref, s["win"], s["load"].at[2]),
        pltpu.make_async_copy(wout_ref, s["wout"], s["load"].at[3]),
    ]
    for i in (1, 2, 3, 0):
        loads[i].start()

    barrier = pltpu.get_barrier_semaphore()
    for step in range(1, 4):
        signal(barrier, device_at((x + step) % 4, y, z, owner))
    for axis in range(3):
        for step in range(1, 4):
            signal(barrier, along(axis, (place[axis] + step) % 4))
    signal(barrier, sibling)
    for k in range(2):

        @pl.when(jnp.logical_or(2 * core + k != x, owner != core))
        def _():
            signal(barrier, device_at(2 * core + k, y, z, owner))

    s["lens_own"][...] = jnp.zeros_like(s["lens_own"])
    s["lens_own"][0:2, 0:NDOC] = len_ref[...]
    pl.semaphore_wait(barrier, 16 - 3 * mine_here.astype(jnp.int32))

    arrays = [(tok_ref, s["tok"], SEG), (ocot_ref, s["ocot"], SEG), (mcot_ref, s["mcot"], SLOTS)]

    def gather_sends(i, start):
        src, dst, count = arrays[i]
        half = count // 2
        for st in range(2):
            chip = 2 * core + st

            @pl.when(chip != x)
            def _():
                for to_core in range(2):
                    copy = remote(
                        src.at[st, pl.ds(to_core * half, half)], dst.at[rows_at(x * count + to_core * half, half)],
                        s["in_send"].at[st, to_core, i], s["in_recv"].at[x, i], device_at(chip, y, z, to_core),
                    )
                    copy.start() if start else copy.wait_send()

            @pl.when(chip == x)
            def _():
                target = dst.at[rows_at(x * count, count)]
                local = pltpu.make_async_copy(src.at[st], target, s["in_local"].at[i])
                copy = remote(src.at[st], target, s["in_send"].at[st, 0, i], s["in_recv"].at[x, i], sibling)
                if start:
                    local.start()
                    copy.start()
                else:
                    local.wait()
                    copy.wait_send()

    def gather_forward(i):
        src, dst, count = arrays[i]
        half = count // 2
        copies = []
        for step in (1, 3, 2):
            seg = (x + step) % 4
            part = dst.at[rows_at(seg * count + core * half, half)]
            remote(
                part, part, s["in_send"].at[0, 0, i], s["in_recv"].at[seg, i], device_at(seg, y, z, owner)
            ).wait_recv()
            copies.append(remote(part, part, s["pass_send"].at[step - 1, i], s["pass_recv"].at[step - 1, i], sibling))
            copies[-1].start()
        return copies

    def gather_finish(i, copies):
        src, dst, count = arrays[i]
        gather_sends(i, False)
        for copy in copies:
            copy.wait()

        @pl.when(jnp.logical_not(mine_here))
        def _():
            whole = dst.at[rows_at(x * count, count)]
            remote(whole, whole, s["in_send"].at[0, 0, i], s["in_recv"].at[x, i], sibling).wait_recv()

    gather_sends(0, True)

    firsts = [(mem_ref.at[stream], s["mem"]), (s["lens_own"], s["lens"])]
    for i, (src, dst) in enumerate(firsts):

        @pl.when(mine_here)
        def _():
            remote(src, dst, s["first_send"].at[i], s["first_recv"].at[i], sibling).start()
            pltpu.make_async_copy(src, dst, s["in_local"].at[3 + i]).start()

    for load in loads[1:]:
        load.wait()
    for i, index in enumerate(TURNED):
        s["attn_t"][i] = jnp.transpose(s["attn"][index])
    for c in range(0, FF, D):
        s["win_t"][c : c + D, :] = jnp.transpose(s["win"][:, c : c + D])
        s["wout_t"][:, c : c + D] = jnp.transpose(s["wout"][c : c + D, :])
    loads[0].wait()

    for i, (src, dst) in enumerate(firsts):

        @pl.when(mine_here)
        def _():
            remote(src, dst, s["first_send"].at[i], s["first_recv"].at[i], sibling).wait_send()
            pltpu.make_async_copy(src, dst, s["in_local"].at[3 + i]).wait()

        @pl.when(jnp.logical_not(mine_here))
        def _():
            remote(src, dst, s["first_send"].at[i], s["first_recv"].at[i], sibling).wait_recv()

    attn, win, wout = s["attn"], s["win"], s["wout"]
    attn_t = {index: s["attn_t"].at[i] for i, index in enumerate(TURNED)}
    win_t, wout_t = s["win_t"], s["wout_t"]
    gain = [gains_ref[i : i + 1, :] for i in range(5)]
    forget_w = fw_ref[...]
    square = (SLOTS, SLOTS)
    diagonal = lax.broadcasted_iota(jnp.int32, square, 0) == lax.broadcasted_iota(jnp.int32, square, 1)
    forget_bias = jnp.sum(jnp.where(diagonal, jnp.broadcast_to(fb_ref[...], square), 0.0), -1, keepdims=True)

    ends = []
    for j in range(NDOC):
        ends.append(s["lens"][pl.ds(stream, 1), j : j + 1] + (ends[-1] if ends else 0))

    def doc_ids(shape, dim, base):
        pos = lax.broadcasted_iota(jnp.int32, shape, dim) + base
        return sum((end <= pos).astype(jnp.int32) for end in ends)

    def row_cut(seg):
        return pl.ds(pl.multiple_of(seg * SEG, SEG), SEG)

    def slot_cut(seg):
        return pl.ds(pl.multiple_of(seg * SLOTS, SLOTS), SLOTS)

    def together(*works):
        works = list(works)
        while works:
            for work in list(works):
                try:
                    next(work)
                except StopIteration:
                    works.remove(work)

    def self_forward(seg):
        rows = row_cut(seg)
        tok = s["tok"][rows, :].astype(f32)
        xhat, rstd = norm_stats(tok)
        s["xh0"][rows, :] = xhat.astype(bf16)
        s["rs0"][rows, :] = rstd
        h = (xhat * gain[0]).astype(bf16)
        s["h"][rows, :] = h
        yield
        q0, q1 = head_halves(dot(h, attn[0]) * SCALE)
        s["q"][0, rows, :] = q0
        s["q"][1, rows, :] = q1
        yield
        k = dot(h, attn[1]).astype(bf16)
        v = dot(h, attn[2]).astype(bf16)
        s["k"][rows, :] = k
        s["v"][rows, :] = v
        yield
        same = doc_ids((SEG, SEG), 0, seg * SEG) == doc_ids((SEG, SEG), 1, seg * SEG)
        bias = jnp.concatenate([jnp.where(same, 0.0, -1e30)] * HEADS, 1)
        s["p"][seg], o = attend(pair_queries(q0, q1), pair_lanes(k), pair_lanes(v), bias)
        s["o"][rows, :] = o
        yield
        res = tok + dot(o, attn[3])
        s["res"][rows, :] = res
        xhat, rstd = norm_stats(res)
        s["xh1"][rows, :] = xhat.astype(bf16)
        s["rs1"][rows, :] = rstd
        n1 = (xhat * gain[1]).astype(bf16)
        s["n1"][rows, :] = n1
        yield
        s["cq"][0, rows, :], s["cq"][1, rows, :] = head_halves(dot(n1, attn[4]) * SCALE)
        yield

    def forward(seg, mem):
        rows, slots = row_cut(seg), slot_cut(seg)
        xhat, rstd = norm_stats(mem)
        s["xh4"][slots, :] = xhat
        s["rs4"][slots, :] = rstd
        m = xhat * gain[4]
        mlow = m.astype(bf16)
        s["mlow"][slots, :] = mlow
        ck = dot(mlow, attn[5]).astype(bf16)
        cv = dot(mlow, attn[6]).astype(bf16)
        s["ck"][slots, :] = ck
        s["cv"][slots, :] = cv
        yield
        s["cp"][seg], co = attend(
            pair_queries(s["cq"][0, rows, :], s["cq"][1, rows, :]), pair_lanes(ck), pair_lanes(cv), 0.0
        )
        s["co"][rows, :] = co
        yield
        res = s["res"][rows, :] + dot(co, attn[7])
        xhat, rstd = norm_stats(res)
        s["xh2"][rows, :] = xhat.astype(bf16)
        s["rs2"][rows, :] = rstd
        n2 = (xhat * gain[2]).astype(bf16)
        s["n2"][rows, :] = n2
        yield
        for c in range(0, FF, FCHUNK):
            hid, slope = gelu_both(dot(n2, win[:, c : c + FCHUNK]))
            hid = hid.astype(bf16)
            s["hid"][rows, c : c + FCHUNK] = hid
            s["gul"][rows, c : c + FCHUNK] = slope
            res = res + dot(hid, wout[c : c + FCHUNK, :])
            yield
        s["act"][rows, :] = res.astype(bf16)
        xhat, rstd = norm_stats(res)
        s["xh3"][rows, :] = xhat.astype(bf16)
        s["rs3"][rows, :] = rstd
        t = (xhat * gain[3]).astype(bf16)
        s["t"][rows, :] = t
        yield
        gate = jax.nn.sigmoid(jnp.sum(m * forget_w, -1, keepdims=True) + forget_bias)
        s["gate"][slots, :] = gate
        wq0, wq1 = head_halves(dot(mlow, attn[8]) * SCALE)
        s["wq"][0, slots, :] = wq0
        s["wq"][1, slots, :] = wq1
        wk = dot(t, attn[9]).astype(bf16)
        wv = dot(t, attn[10]).astype(bf16)
        s["wk"][rows, :] = wk
        s["wv"][rows, :] = wv
        yield
        pos = lax.broadcasted_iota(jnp.int32, (SEG, HEADS * SLOTS), 0) + seg * SEG
        s["wp"][seg], wo = attend(
            pair_queries(wq0, wq1), pair_lanes(wk), pair_lanes(wv), jnp.where(pos < ends[-1], 0.0, -1e30)
        )
        s["wo"][slots, :] = wo
        yield
        update = dot(wo, attn[11])
        s["upd"][slots, :] = mem - update
        fresh = (update + gate * (mem - update)).astype(bf16)
        s["mout"][slots, :] = fresh
        s["mem"][...] = fresh
        yield

    first_step = forward(0, s["mem"][...].astype(f32))
    next(first_step)
    gather_finish(0, gather_forward(0))
    gather_sends(1, True)
    gather_sends(2, True)
    together(self_forward(0))
    together(first_step, self_forward(1))

    def forward_both(seg, carry):
        together(forward(seg, s["mem"][...].astype(f32)), self_forward(seg + 1))
        return carry

    lax.fori_loop(1, NSEG - 1, forward_both, 0)
    passed = [gather_forward(1), gather_forward(2)]
    together(forward(NSEG - 1, s["mem"][...].astype(f32)))

    def results(indices, do):
        for k in range(2):
            seg = 2 * core + k
            here = jnp.logical_and(seg == x, mine_here)
            peer = device_at(seg, y, z, owner)
            sources = [
                (s["act"].at[rows_at(seg * SEG, SEG)], act_out), (s["mout"].at[rows_at(seg * SLOTS, SLOTS)], mout_out),
                (s["gtok"].at[rows_at(seg * SEG, SEG)], gtok_out), (s["gmem"].at[rows_at(seg * SLOTS, SLOTS)], gmem_out),
            ]
            for i in indices:
                src, dst = sources[i]

                @pl.when(jnp.logical_not(here))
                def _():
                    do(
                        remote(src, dst.at[stream], s["out_send"].at[k, i], s["out_recv"].at[stream, i], peer),
                        remote(src, dst.at[k], s["out_send"].at[k, i], s["out_recv"].at[k, i], peer),
                    )

                @pl.when(here)
                def _():
                    do(pltpu.make_async_copy(src, dst.at[stream], s["out_local"].at[i]), None)

    def results_start(copy, back):
        copy.start()

    def results_finish(copy, back):
        if back is None:
            copy.wait()
        else:
            copy.wait_send()
            back.wait_recv()

    results((0, 1), results_start)
    for i in (1, 2):
        gather_finish(i, passed[i - 1])

    s["gain"][...] = jnp.zeros_like(s["gain"])
    s["bias"][...] = jnp.zeros_like(s["bias"])

    def backward(seg):
        rows, slots = row_cut(seg), slot_cut(seg)
        gz = (s["mcot"][slots, :].astype(f32) + s["mem"][...].astype(f32)).astype(bf16).astype(f32)
        gate = s["gate"][slots, :]
        gup = ((1.0 - gate) * gz).astype(bf16)
        s["gup"][slots, :] = gup
        g_wo = head_halves(dot(gup, attn_t[11][...]))
        yield
        dwq, dwk, dwv = attend_back(
            s["wp"][seg], pair_queries(*g_wo), pair_queries(s["wq"][0, slots, :], s["wq"][1, slots, :]),
            pair_lanes(s["wk"][rows, :]), pair_lanes(s["wv"][rows, :]),
        )
        s["dwq"][slots, :] = dwq
        s["dwk"][rows, :] = dwk
        s["dwv"][rows, :] = dwv
        yield
        gt = dot(dwk, attn_t[9][...]) + dot(dwv, attn_t[10][...])
        xhat = s["xh3"][rows, :].astype(f32)
        s["gain"][3:4, :] += jnp.sum(gt * xhat, 0, keepdims=True)
        gy = s["ocot"][rows, :].astype(f32) + norm_back(gt, gain[3], xhat, s["rs3"][rows, :])
        gyl = gy.astype(bf16)
        s["gyl"][rows, :] = gyl
        yield
        gn2 = jnp.zeros((SEG, D), f32)
        for c in range(0, FF, FCHUNK):
            ghid = dot(gyl, wout_t[:, c : c + FCHUNK])
            gul = (ghid * s["gul"][rows, c : c + FCHUNK].astype(f32)).astype(bf16)
            s["gul"][rows, c : c + FCHUNK] = gul
            gn2 = gn2 + dot(gul, win_t[c : c + FCHUNK, :])
            yield
        xhat = s["xh2"][rows, :].astype(f32)
        s["gain"][2:3, :] += jnp.sum(gn2 * xhat, 0, keepdims=True)
        gb = gy + norm_back(gn2, gain[2], xhat, s["rs2"][rows, :])
        s["res"][rows, :] = gb
        gbl = gb.astype(bf16)
        s["gbl"][rows, :] = gbl
        yield
        g_co = head_halves(dot(gbl, attn_t[7][...]))
        dgate = jnp.sum(gz * s["upd"][slots, :], -1, keepdims=True) * gate * (1.0 - gate)
        xh4 = s["xh4"][slots, :]
        s["gain"][5:6, :] += jnp.sum(dgate * (xh4 * gain[4]), 0, keepdims=True)
        s["bias"][...] += jnp.broadcast_to(dgate, (SLOTS, LANES))
        gm = dgate * forget_w + dot(dwq, attn_t[8][...])
        yield
        dcq, dck, dcv = attend_back(
            s["cp"][seg], pair_queries(*g_co), pair_queries(s["cq"][0, rows, :], s["cq"][1, rows, :]),
            pair_lanes(s["ck"][slots, :]), pair_lanes(s["cv"][slots, :]),
        )
        s["dcq"][rows, :] = dcq
        s["dck"][slots, :] = dck
        s["dcv"][slots, :] = dcv
        yield
        gm = gm + dot(dck, attn_t[5][...]) + dot(dcv, attn_t[6][...])
        s["gain"][4:5, :] += jnp.sum(gm * xh4, 0, keepdims=True)
        gmem = (gate * gz + norm_back(gm, gain[4], xh4, s["rs4"][slots, :])).astype(bf16)
        s["gmem"][slots, :] = gmem
        s["mem"][...] = gmem
        yield

    s["mem"][...] = jnp.zeros_like(s["mem"])

    def backward_one(step, carry):
        together(backward(NSEG - 1 - step))
        return carry

    lax.fori_loop(0, NSEG - 1, backward_one, 0)
    last_step = backward(0)
    for _ in range(3 + FF // FCHUNK):
        next(last_step)

    cut = pl.ds(pl.multiple_of(core * BLOCK, BLOCK), BLOCK)

    def put(i, value):
        value = value.astype(bf16)
        for j in range(LANE_CUTS):
            s["dw"][(i * LANE_CUTS + j) * BLOCK : (i * LANE_CUTS + j + 1) * BLOCK, :] = value[:, j * LANES : (j + 1) * LANES]

    def put_products(base, names):
        for i, (left, right) in enumerate(names):
            put(base + i, dot_tn(s[left][:, cut], s[right][...]))

    def small_start(axis, value):
        here = place[axis]
        s["small"][axis, here] = value
        for step in range(1, 4):
            own = s["small"].at[axis, here]
            remote(own, own, s["small_send"].at[axis], s["small_recv"].at[axis], along(axis, (here + step) % 4)).start()

    def all_moved(ref, send_sem, recv_sem):
        copy = remote(ref, ref, send_sem, recv_sem, sibling)
        copy.wait_send()
        copy.wait_recv()

    def small_finish(axis):
        all_moved(s["small"].at[axis, pl.ds(0, 3)], s["small_send"].at[axis], s["small_recv"].at[axis])
        return (s["small"][axis, 0] + s["small"][axis, 1]) + (s["small"][axis, 2] + s["small"][axis, 3])

    def others(axis, i):
        return [((i + step) % 4, step - 1, along(axis, (i + step) % 4)) for step in range(1, 4)]

    def add(refs):
        total = refs[0][...].astype(f32)
        for ref in refs[1:]:
            total += ref[...].astype(f32)
        return total.astype(bf16)

    def part_place(chunk, part):
        r = CHUNKS[chunk][part] * UNIT
        base = 64 * UNIT * (sum(sum(c) for c in CHUNKS[:chunk]) + sum(CHUNKS[chunk][:part]))
        axes = [(part + i) % 3 for i in range(3)]
        return r, base, axes, [place[a] for a in axes]

    def part_steps(chunk, part):
        r, base, axes, (i1, i2, i3) = part_place(chunk, part)
        right, left = along(axes[0], (i1 + 1) % 4), along(axes[0], (i1 + 3) % 4)
        near, far, mid, quad, last = (s[name][chunk][part] for name in ("near", "far", "mid", "quad", "last"))
        dw, mine = s["dw"], full_ref.at[core]

        def copy(src, dst, device, i):
            remote(src, dst, s["send"].at[chunk], s["recv"].at[chunk, part, i], device).start()

        def arrived(ref, i):
            remote(ref, ref, s["send"].at[chunk], s["recv"].at[chunk, part, i], sibling).wait_recv()

        def block(b, first=0, count=16):
            return rows_at(base + (b % 4) * 16 * r + first * r, count * r)

        def pass_on(rows, device, i):
            copy(mine.at[rows], mine.at[rows], device, i)

        half0, half1 = pl.ds(0, 8 * r), pl.ds(8 * r, 8 * r)
        copy(dw.at[block(i1 + 2, 0, 8)], near.at[0], right, 0)
        copy(dw.at[block(i1 + 2, 8, 8)], near.at[1], left, 1)
        copy(dw.at[block(i1 + 1, 8, 8)], far.at[0, half1], right, 2)
        copy(dw.at[block(i1 + 3, 0, 8)], far.at[1, half0], left, 2)
        yield
        arrived(near.at[0], 0)
        near[0] = add([near.at[0], dw.at[block(i1 + 1, 0, 8)]])
        copy(near.at[0], far.at[0, half0], right, 2)
        arrived(near.at[1], 1)
        near[1] = add([near.at[1], dw.at[block(i1 + 3, 8, 8)]])
        copy(near.at[1], far.at[1, half1], left, 2)
        yield
        arrived(far, 2)
        far[0] = add([far.at[0], far.at[1], dw.at[block(i1)]])
        for b, slot, to in others(axes[1], i2):
            copy(far.at[0, rows_at(b * 4 * r, 4 * r)], mid.at[slot], to, 3)
        yield
        arrived(mid, 3)
        quad[i3] = add([mid.at[0], mid.at[1], mid.at[2], far.at[0, rows_at(i2 * 4 * r, 4 * r)]])
        for _, _, to in others(axes[2], i3):
            copy(quad.at[i3], quad.at[i3], to, 4)
        yield
        arrived(quad.at[pl.ds(0, 3)], 4)
        last[...] = add([quad.at[i] for i in range(4)])
        home = rows_at(base + (i1 * 16 + i2 * 4) * r, 4 * r)
        keep = pltpu.make_async_copy(last, mine.at[home], s["own"].at[chunk, part])
        keep.start()
        for _, _, to in others(axes[1], i2):
            copy(last, mine.at[home], to, 5)
        yield
        keep.wait()
        arrived(mine.at[rows_at(base, 12 * r)], 5)
        pass_on(block(i1), right, 6)
        pass_on(block(i1), left, 7)
        pass_on(block(i1), sibling, 9)
        yield
        arrived(mine.at[block(i1 + 3)], 6)
        pass_on(block(i1 + 3, 0, 8), right, 8)
        pass_on(block(i1 + 3), sibling, 9)
        arrived(mine.at[block(i1 + 1)], 7)
        pass_on(block(i1 + 1, 8, 8), left, 8)
        pass_on(block(i1 + 1), sibling, 9)
        yield
        arrived(mine.at[block(i1 + 2)], 8)
        pass_on(block(i1 + 2), sibling, 9)
        yield
        arrived(full_ref.at[1 - core, rows_at(base, 64 * r)], 9)
        if part == 2:
            sent = full_ref.at[core, rows_at(0, 196 * UNIT * sum(CHUNKS[chunk]))]
            remote(sent, sent, s["send"].at[chunk], s["recv"].at[chunk, part, 0], sibling).wait_send()
        yield

    def chunk_steps(chunk):
        parts = [part_steps(chunk, part) for part in range(3)]
        while True:
            for part in parts:
                next(part)
            yield

    chunks = [chunk_steps(chunk) for chunk in range(len(CHUNKS))]

    def go(*order):
        for chunk in order:
            next(chunks[chunk])

    for i in range(4):
        put(i, dot_tn(s["n2"][:, cut], s["gul"][:, i * D : (i + 1) * D]))
    for i in range(4):
        if i == 2:
            go(0)
        cut_i = pl.ds(pl.multiple_of(core * 4 * BLOCK + i * BLOCK, BLOCK), BLOCK)
        put(4 + i, dot_tn(s["hid"][:, cut_i], s["gyl"][...]))
    put_products(8, [("mlow", "dwq"), ("t", "dwk"), ("t", "dwv"), ("wo", "gup")])
    go(1)
    together(last_step)
    results((3,), results_start)
    put_products(12, [("n1", "dcq"), ("mlow", "dck"), ("mlow", "dcv"), ("co", "gbl")])

    gn1 = dot_nt(s["dcq"][...], attn[4])
    xhat = s["xh1"][...].astype(f32)
    s["gain"][1:2, :] = jnp.sum(gn1 * xhat, 0, keepdims=True)
    ga = s["res"][...] + norm_back(gn1, gain[1], xhat, s["rs1"][...])
    s["res"][...] = ga
    gal = ga.astype(bf16)
    s["gal"][...] = gal
    s["cq"][0], s["cq"][1] = head_halves(dot_nt(gal, attn[3]))
    put_products(16, [("o", "gal")])
    go(2)

    def self_backward(seg):
        rows = row_cut(seg)
        s["dq"][rows, :], s["dk"][rows, :], s["dv"][rows, :] = attend_back(
            s["p"][seg], pair_queries(s["cq"][0, rows, :], s["cq"][1, rows, :]),
            pair_queries(s["q"][0, rows, :], s["q"][1, rows, :]),
            pair_lanes(s["k"][rows, :]), pair_lanes(s["v"][rows, :]),
        )

    self_backward(0)
    self_backward(1)
    self_backward(2)
    go(0)
    self_backward(3)
    gh = dot_nt(s["dq"][...], attn[0]) + dot_nt(s["dk"][...], attn[1]) + dot_nt(s["dv"][...], attn[2])
    go(1)
    xhat = s["xh0"][...].astype(f32)
    s["gain"][0:1, :] = jnp.sum(gh * xhat, 0, keepdims=True)
    s["gtok"][...] = (s["res"][...] + norm_back(gh, gain[0], xhat, s["rs0"][...])).astype(bf16)
    s["gain"][6:7, 0:SLOTS] = jnp.sum(jnp.where(diagonal, s["bias"][:, 0:SLOTS], 0.0), 0, keepdims=True)
    small_start(0, s["gain"][...])
    results((2,), results_start)
    put_products(17, [("h", "dq"), ("h", "dk"), ("h", "dv")])
    go(3, 2, 0)
    total = small_finish(0)
    small_start(1, total)
    go(1, 3, 2, 0)
    total = small_finish(1)
    small_start(2, total)
    go(3, 1, 2, 0, 3)
    small_out[...] = small_finish(2)
    go(1, 2, 3, 0, 1, 2, 3, 0, 3, 1, 2, 3, 0, 1, 3, 2, 0, 1, 2)
    results((0, 1, 2, 3), results_finish)


def run_fused(tok, ocot, mcot, mem, lens, attn, win, wout, gains, fw, fb):
    vmem = pl.BlockSpec(memory_space=pltpu.VMEM)
    hbm = pl.BlockSpec(memory_space=pl.ANY)
    return pl.pallas_call(
        fused_kernel,
        out_shape=(
            jax.ShapeDtypeStruct((2, FLAT, LANES), bf16),
            jax.ShapeDtypeStruct((2, SEG, D), bf16),
            jax.ShapeDtypeStruct((2, SLOTS, D), bf16),
            jax.ShapeDtypeStruct((2, SEG, D), bf16),
            jax.ShapeDtypeStruct((2, SLOTS, D), bf16),
            jax.ShapeDtypeStruct((8, D), f32),
        ),
        in_specs=[hbm] * 4 + [vmem] + [hbm] * 3 + [vmem] * 3,
        out_specs=[hbm] * 5 + [vmem],
        scratch_shapes=[scratch_buffers()],
        compiler_params=pltpu.CompilerParams(collective_id=1, has_side_effects=True, vmem_limit_bytes=63 << 20),
        name="layer_and_sums",
    )(tok, ocot, mcot, mem, lens, attn, win, wout, gains, fw, fb)


def widen_kernel(
    full_ref, act_ref, mem_ref, gtok_ref, gmem_ref, small_ref,
    attn_ref, in_ref, out_ref, act_out, mem_out, gtok_out, gmem_out, gains_out, fw_out, fb_out,
    full_s, wide_s, load_sem, store_sem,
):
    def load(i):
        return [
            pltpu.make_async_copy(full_ref.at[half, i], full_s.at[i, half], load_sem.at[i, half]) for half in range(2)
        ]

    def target(i, half):
        if i < 4:
            return in_ref.at[pl.ds(half * BLOCK, BLOCK), pl.ds(i * D, D)]
        if i < 8:
            return out_ref.at[pl.ds(half * 4 * BLOCK + (i - 4) * BLOCK, BLOCK), :]
        return attn_ref.at[i if i < 12 else i - 8 if i < 16 else 3 if i == 16 else i - 17, pl.ds(half * BLOCK, BLOCK), :]

    def store(i, half):
        return pltpu.make_async_copy(wide_s.at[i, half], target(i, half), store_sem)

    for i in range(NBLOCKS):
        for copy in load(i):
            copy.start()
    act_out[...] = act_ref[...]
    mem_out[...] = mem_ref[...]
    gtok_out[...] = gtok_ref[...].astype(f32)
    gmem_out[...] = gmem_ref[...].astype(f32)
    gains_out[...] = small_ref[0:5, :]
    fw_out[...] = small_ref[5:6, :]
    fb_out[...] = small_ref[6:7, 0:SLOTS]
    for i in range(NBLOCKS):
        for half, copy in enumerate(load(i)):
            copy.wait()
            for j in range(LANE_CUTS):
                wide_s[i, half, :, j * LANES : (j + 1) * LANES] = full_s[i, half, j].astype(f32)
            store(i, half).start()
    pltpu.make_async_copy(wide_s, wide_s, store_sem).wait()


def run_widen(full, *others):
    hbm = pl.BlockSpec(memory_space=pl.ANY)
    vmem = pl.BlockSpec(memory_space=pltpu.VMEM)
    return pl.pallas_call(
        widen_kernel,
        out_shape=(
            jax.ShapeDtypeStruct((12, D, D), f32),
            jax.ShapeDtypeStruct((D, FF), f32),
            jax.ShapeDtypeStruct((FF, D), f32),
            jax.ShapeDtypeStruct((2, SEG, D), bf16),
            jax.ShapeDtypeStruct((2, SLOTS, D), bf16),
            jax.ShapeDtypeStruct((2, SEG, D), f32),
            jax.ShapeDtypeStruct((2, SLOTS, D), f32),
            jax.ShapeDtypeStruct((5, D), f32),
            jax.ShapeDtypeStruct((1, D), f32),
            jax.ShapeDtypeStruct((1, SLOTS), f32),
        ),
        in_specs=[hbm] + [vmem] * 5,
        out_specs=[hbm] * 3 + [vmem] * 7,
        scratch_shapes=[
            pltpu.VMEM((NBLOCKS, 2, LANE_CUTS, BLOCK, LANES), bf16),
            pltpu.VMEM((NBLOCKS, 2, BLOCK, D), f32),
            pltpu.SemaphoreType.DMA((NBLOCKS, 2)),
            pltpu.SemaphoreType.DMA,
        ],
        compiler_params=pltpu.CompilerParams(vmem_limit_bytes=60 << 20),
        name="widen_gradients",
    )(full, *others)


def body(
    tokens, memory_start, doc_lengths, attn_weights, ffn_in, ffn_out, gains, forget_w, forget_bias,
    out_cotangent, memory_cotangent,
):
    full, *others = run_fused(
        tokens, out_cotangent, memory_cotangent, memory_start, doc_lengths,
        attn_weights.reshape(12, D, D), ffn_in, ffn_out, gains, forget_w.reshape(1, D), forget_bias.reshape(1, SLOTS),
    )
    grad_attn, grad_in, grad_out, acts, mems, gtok, gmem, grad_gains, grad_fw, grad_fb = run_widen(
        full.reshape(2, NBLOCKS, LANE_CUTS, BLOCK, LANES), *others
    )
    return (
        acts, mems, gtok, gmem, grad_attn.reshape(3, 4, D, D), grad_in, grad_out,
        grad_gains, grad_fw.reshape(D), grad_fb.reshape(SLOTS),
    )


def solution(mesh):
    return jax.shard_map(
        body,
        mesh=mesh,
        in_specs=(
            P("doc", "seg", None), P("doc", None, None), P("doc", None), P(), P(), P(), P(), P(), P(),
            P("doc", "seg", None), P("doc", "seg", None),
        ),
        out_specs=(
            P("doc", "seg", None), P("doc", "seg", None), P("doc", "seg", None), P("doc", "seg", None),
            P(), P(), P(), P(), P(), P(),
        ),
        check_vma=False,
    )
```

```python
import functools

import jax
import jax.numpy as jnp
from jax import lax
from jax.experimental import pallas as pl
from jax.experimental.pallas import tpu as pltpu
from jax.sharding import PartitionSpec as P

HEADS = 8
NDOC = 8
D = 512
FF = 2048
SLOTS = 64
SEG = 128
NSEG = 4
ROWS = NSEG * SEG
MROWS = NSEG * SLOTS
PAIRS = 4
PAIR = 128
FCHUNK = 2048
BLOCK = 256
NBLOCKS = 20
LANES = 128
LANE_CUTS = D // LANES
FLAT = NBLOCKS * BLOCK * LANE_CUTS
MESH = pl.DeviceIdType.MESH
SCALE = 0.125

f32 = jnp.float32
bf16 = jnp.bfloat16


def dot(a, b):
    return lax.dot_general(a, b, (((1,), (0,)), ((), ())), preferred_element_type=f32)


def dot_nt(a, b):
    return lax.dot_general(a, b, (((1,), (1,)), ((), ())), preferred_element_type=f32)


def dot_tn(a, b):
    return lax.dot_general(a, b, (((0,), (0,)), ((), ())), preferred_element_type=f32)


def norm_stats(values):
    centered = values - jnp.mean(values, -1, keepdims=True)
    rstd = lax.rsqrt(jnp.mean(centered * centered, -1, keepdims=True) + 1e-05)
    return centered * rstd, rstd


def norm_back(grad, gain, xhat, rstd):
    scaled = grad * gain
    mean_one = jnp.mean(scaled, -1, keepdims=True)
    mean_two = jnp.mean(scaled * xhat, -1, keepdims=True)
    return rstd * (scaled - mean_one - xhat * mean_two)


def head_halves(values):
    low_half = lax.broadcasted_iota(jnp.int32, (16, values.shape[1]), 1) % PAIR < PAIR // 2
    first = jnp.where(low_half, 1.0, 0.0).astype(bf16)[0:1, :]
    second = jnp.where(low_half, 0.0, 1.0).astype(bf16)[0:1, :]
    values = values.astype(bf16)
    return values * first, values * second


def join_halves(stacked):
    rows = stacked.shape[0] // 2
    low_half = lax.broadcasted_iota(jnp.int32, (rows, PAIR), 1) < PAIR // 2
    return jnp.where(low_half, stacked[:rows], stacked[rows:])


def attend(queries, keys, values, bias):
    scores = jnp.concatenate([dot_nt(k, q) for k, q in zip(keys, queries)], 1) + bias
    expd = jnp.exp(scores - jnp.max(scores, 0, keepdims=True))
    probs = (expd * (1.0 / jnp.sum(expd, 0, keepdims=True))).astype(bf16)
    width = queries[0].shape[0]
    mixed = [join_halves(dot_tn(probs[:, i * width : (i + 1) * width], v)) for i, v in enumerate(values)]
    return probs, jnp.concatenate(mixed, 1).astype(bf16)


def attend_back(probs, grads, queries, keys, values):
    width = queries[0].shape[0]
    wide = probs.astype(f32)
    dp = jnp.concatenate([dot_nt(v, g) for v, g in zip(values, grads)], 1)
    ds = (wide * (dp - jnp.sum(wide * dp, 0, keepdims=True))).astype(bf16)
    cuts = [slice(i * width, (i + 1) * width) for i in range(PAIRS)]
    dq = [join_halves(dot_tn(ds[:, cut], k)) for cut, k in zip(cuts, keys)]
    dk = [dot(ds[:, cut], q) for cut, q in zip(cuts, queries)]
    dv = [dot(probs[:, cut], g) for cut, g in zip(cuts, grads)]
    join = lambda parts: jnp.concatenate(parts, 1)
    return (join(dq) * SCALE).astype(bf16), join(dk).astype(bf16), join(dv).astype(bf16)


def pair_lanes(values):
    return [values[:, i * PAIR : (i + 1) * PAIR] for i in range(PAIRS)]


def pair_queries(first, second):
    return [jnp.concatenate(halves, 0) for halves in zip(pair_lanes(first), pair_lanes(second))]


def gelu_both(u):
    square = u * u
    tanh = jnp.tanh(0.7978845608028654 * u * (1.0 + 0.044715 * square))
    half = 0.5 + 0.5 * tanh
    hidden = u * half
    rest, square = (1.0 - tanh).astype(bf16), square.astype(bf16)
    slope = half.astype(bf16) + hidden.astype(bf16) * rest * (bf16(0.7978845608028654) + bf16(0.1070322243) * square)
    return hidden, slope


CHUNKS = ((2, 2, 2), (2, 2, 2), (1, 2, 2), (1, 1, 1))
UNIT = 16

TURNED = (7, 11, 8, 5, 6, 9, 10)


def scratch_buffers():
    def rows(dtype=bf16, width=D):
        return pltpu.VMEM((ROWS, width), dtype)

    def slots(dtype=bf16, width=D):
        return pltpu.VMEM((MROWS, width), dtype)

    def two(count):
        return pltpu.VMEM((2, count, D), bf16)

    def parts(shape_of):
        return [[pltpu.VMEM(shape_of(count * UNIT), bf16) for count in chunk] for chunk in CHUNKS]

    dma = pltpu.SemaphoreType.DMA
    return dict(
        attn=pltpu.VMEM((12, D, D), bf16), win=pltpu.VMEM((D, FF), bf16), wout=pltpu.VMEM((FF, D), bf16),
        attn_t=pltpu.VMEM((len(TURNED), D, D), bf16), win_t=pltpu.VMEM((FF, D), bf16), wout_t=pltpu.VMEM((D, FF), bf16),
        tok=rows(), ocot=rows(), mcot=slots(), mem=pltpu.VMEM((SLOTS, D), bf16),
        lens_own=pltpu.VMEM((8, LANES), jnp.int32), lens=pltpu.VMEM((8, LANES), jnp.int32),
        act=rows(), mout=slots(), gtok=rows(), gmem=slots(),
        h=rows(), q=two(ROWS), k=rows(), v=rows(), p=pltpu.VMEM((NSEG, SEG, HEADS * SEG), bf16), o=rows(),
        xh0=rows(), rs0=rows(f32, 1),
        res=rows(f32), n1=rows(), xh1=rows(), rs1=rows(f32, 1), cq=two(ROWS), ck=slots(), cv=slots(),
        cp=pltpu.VMEM((NSEG, SLOTS, HEADS * SEG), bf16), co=rows(),
        n2=rows(), xh2=rows(), rs2=rows(f32, 1), hid=rows(bf16, FF), gul=rows(bf16, FF),
        t=rows(), xh3=rows(), rs3=rows(f32, 1),
        xh4=slots(f32), rs4=slots(f32, 1), mlow=slots(), gate=slots(f32, 1), upd=slots(f32),
        wq=two(MROWS), wk=rows(), wv=rows(), wp=pltpu.VMEM((NSEG, SEG, HEADS * SLOTS), bf16), wo=slots(),
        gup=slots(), dwq=slots(), dwk=rows(), dwv=rows(), gyl=rows(), gbl=rows(),
        dcq=rows(), dck=slots(), dcv=slots(),
        gal=rows(), dq=rows(), dk=rows(), dv=rows(),
        gain=pltpu.VMEM((8, D), f32), bias=pltpu.VMEM((SLOTS, LANES), f32),
        dw=pltpu.VMEM((FLAT, LANES), bf16),
        near=parts(lambda r: (2, 8 * r, LANES)), far=parts(lambda r: (2, 16 * r, LANES)),
        mid=parts(lambda r: (3, 4 * r, LANES)), quad=parts(lambda r: (4, 4 * r, LANES)), last=parts(lambda r: (4 * r, LANES)),
        small=pltpu.VMEM((3, 5, 8, D), f32),
        in_send=dma((2, 2, 3)), in_recv=dma((4, 3)), first_send=dma((2,)), first_recv=dma((2,)),
        pass_send=dma((3,)), pass_recv=dma((3,)), in_local=dma((5,)), load=dma((8,)),
        gains=pltpu.VMEM((5, D), f32), fw=pltpu.VMEM((1, D), f32), fb=pltpu.VMEM((1, SLOTS), f32),
        lens_in=pltpu.VMEM((2, NDOC), jnp.int32),
        send=dma((len(CHUNKS),)), recv=dma((len(CHUNKS), 3, 7)), over=dma((len(CHUNKS),)), own=dma((len(CHUNKS), 3)),
        out_send=dma((2, 4)), out_recv=dma((2, 4)), out_local=dma((4,)),
        small_send=dma((3,)), small_recv=dma((3,)),
    )


def my_place():
    doc = lax.axis_index("doc")
    return lax.axis_index("seg"), doc // 8, (doc // 2) % 4, doc % 2


def device_at(x, y, z, core):
    return (x, y * 8 + z * 2 + core)


def remote(src, dst, send_sem, recv_sem, device):
    return pltpu.make_async_remote_copy(
        src_ref=src, dst_ref=dst, send_sem=send_sem, recv_sem=recv_sem, device_id=device, device_id_type=MESH
    )


def signal(sem, device):
    pl.semaphore_signal(sem, inc=1, device_id=device, device_id_type=MESH)


def fused_kernel(
    tok_ref, ocot_ref, mcot_ref, mem_ref, len_ref, attn_ref, win_ref, wout_ref, gains_ref, fw_ref, fb_ref,
    full_ref, act_out, mout_out, gtok_out, gmem_out, small_out,
    s,
):
    place = my_place()
    x, y, z, core = place
    owner, stream = x // 2, x % 2
    mine_here = owner == core
    sibling = device_at(x, y, z, 1 - core)

    def along(axis, coordinate):
        there = list(place)
        there[axis] = coordinate
        return device_at(*there)

    def rows_at(first, count):
        return pl.ds(pl.multiple_of(first, UNIT), count)

    loads = [
        pltpu.make_async_copy(attn_ref.at[pl.ds(0, 4)], s["attn"].at[pl.ds(0, 4)], s["load"].at[0]),
        pltpu.make_async_copy(attn_ref.at[pl.ds(4, 8)], s["attn"].at[pl.ds(4, 8)], s["load"].at[1]),
        pltpu.make_async_copy(win_ref, s["win"], s["load"].at[2]),
        pltpu.make_async_copy(wout_ref, s["wout"], s["load"].at[3]),
    ]
    small_loads = [
        pltpu.make_async_copy(src, s[name], s["load"].at[4 + i])
        for i, (src, name) in enumerate([(len_ref, "lens_in"), (gains_ref, "gains"), (fw_ref, "fw"), (fb_ref, "fb")])
    ]
    for load in small_loads:
        load.start()
    for i in (1, 2, 3, 0):
        loads[i].start()

    barrier = pltpu.get_barrier_semaphore()
    for step in range(1, 4):
        signal(barrier, device_at((x + step) % 4, y, z, owner))
    for axis in range(3):
        for step in range(1, 4):
            signal(barrier, along(axis, (place[axis] + step) % 4))
    signal(barrier, sibling)
    for k in range(2):

        @pl.when(jnp.logical_or(2 * core + k != x, owner != core))
        def _():
            signal(barrier, device_at(2 * core + k, y, z, owner))

    small_loads[0].wait()
    s["lens_own"][...] = jnp.zeros_like(s["lens_own"])
    s["lens_own"][0:2, 0:NDOC] = s["lens_in"][...]
    pl.semaphore_wait(barrier, 16 - 3 * mine_here.astype(jnp.int32))

    arrays = [(tok_ref, s["tok"], SEG), (ocot_ref, s["ocot"], SEG), (mcot_ref, s["mcot"], SLOTS)]

    def gather_sends(i, start):
        src, dst, count = arrays[i]
        half = count // 2
        for st in range(2):
            chip = 2 * core + st

            @pl.when(chip != x)
            def _():
                for to_core in range(2):
                    copy = remote(
                        src.at[st, pl.ds(to_core * half, half)], dst.at[rows_at(x * count + to_core * half, half)],
                        s["in_send"].at[st, to_core, i], s["in_recv"].at[x, i], device_at(chip, y, z, to_core),
                    )
                    copy.start() if start else copy.wait_send()

            @pl.when(chip == x)
            def _():
                target = dst.at[rows_at(x * count, count)]
                copy = remote(src.at[st], target, s["in_send"].at[st, 0, i], s["in_recv"].at[x, i], sibling)
                if start:
                    pltpu.make_async_copy(src.at[st], target, s["in_local"].at[i]).start()
                    copy.start()
                else:
                    copy.wait_send()

    def gather_own(i):
        src, dst, count = arrays[i]
        whole = dst.at[rows_at(x * count, count)]

        @pl.when(mine_here)
        def _():
            pltpu.make_async_copy(src.at[stream], whole, s["in_local"].at[i]).wait()

        @pl.when(jnp.logical_not(mine_here))
        def _():
            remote(whole, whole, s["in_send"].at[0, 0, i], s["in_recv"].at[x, i], sibling).wait_recv()

    def all_moved(ref, send_sem, recv_sem):
        copy = remote(ref, ref, send_sem, recv_sem, sibling)
        copy.wait_send()
        copy.wait_recv()

    def gather_forward(i):
        src, dst, count = arrays[i]
        half = count // 2
        for step in (1, 3, 2):
            seg = (x + step) % 4
            part = dst.at[rows_at(seg * count + core * half, half)]
            remote(
                part, part, s["in_send"].at[0, 0, i], s["in_recv"].at[seg, i], device_at(seg, y, z, owner)
            ).wait_recv()
            remote(part, part, s["pass_send"].at[i], s["pass_recv"].at[i], sibling).start()

    def gather_finish(i):
        src, dst, count = arrays[i]
        gather_sends(i, False)
        three_halves = dst.at[pl.ds(0, 3 * count // 2)]
        all_moved(three_halves, s["pass_send"].at[i], s["pass_recv"].at[i])

    gather_sends(0, True)

    firsts = [(mem_ref.at[stream], s["mem"]), (s["lens_own"], s["lens"])]
    for i, (src, dst) in enumerate(firsts):

        @pl.when(mine_here)
        def _():
            remote(src, dst, s["first_send"].at[i], s["first_recv"].at[i], sibling).start()
            pltpu.make_async_copy(src, dst, s["in_local"].at[3 + i]).start()

    loads[1].wait()
    for i, index in enumerate(TURNED):
        s["attn_t"][i] = jnp.transpose(s["attn"][index])
    loads[2].wait()
    for c in range(0, FF, D):
        s["win_t"][c : c + D, :] = jnp.transpose(s["win"][:, c : c + D])
    loads[3].wait()
    for c in range(0, FF, D):
        s["wout_t"][:, c : c + D] = jnp.transpose(s["wout"][c : c + D, :])
    loads[0].wait()

    for i, (src, dst) in enumerate(firsts):

        @pl.when(mine_here)
        def _():
            remote(src, dst, s["first_send"].at[i], s["first_recv"].at[i], sibling).wait_send()
            pltpu.make_async_copy(src, dst, s["in_local"].at[3 + i]).wait()

        @pl.when(jnp.logical_not(mine_here))
        def _():
            remote(src, dst, s["first_send"].at[i], s["first_recv"].at[i], sibling).wait_recv()

    attn, win, wout = s["attn"], s["win"], s["wout"]
    attn_t = {index: s["attn_t"].at[i] for i, index in enumerate(TURNED)}
    win_t, wout_t = s["win_t"], s["wout_t"]
    for load in small_loads[1:]:
        load.wait()
    gain = [s["gains"][i : i + 1, :] for i in range(5)]
    forget_w = s["fw"][...]
    square = (SLOTS, SLOTS)
    diagonal = lax.broadcasted_iota(jnp.int32, square, 0) == lax.broadcasted_iota(jnp.int32, square, 1)
    forget_bias = jnp.sum(jnp.where(diagonal, jnp.broadcast_to(s["fb"][...], square), 0.0), -1, keepdims=True)

    ends = []
    for j in range(NDOC):
        ends.append(s["lens"][pl.ds(stream, 1), j : j + 1] + (ends[-1] if ends else 0))

    def doc_ids(shape, dim, base):
        pos = lax.broadcasted_iota(jnp.int32, shape, dim) + base
        return sum((end <= pos).astype(jnp.int32) for end in ends)

    def row_cut(seg):
        return pl.ds(pl.multiple_of(seg * SEG, SEG), SEG)

    def slot_cut(seg):
        return pl.ds(pl.multiple_of(seg * SLOTS, SLOTS), SLOTS)

    def together(*works):
        works = list(works)
        while works:
            for work in list(works):
                try:
                    next(work)
                except StopIteration:
                    works.remove(work)

    def self_forward(seg):
        rows = row_cut(seg)
        tok = s["tok"][rows, :].astype(f32)
        xhat, rstd = norm_stats(tok)
        s["xh0"][rows, :] = xhat.astype(bf16)
        s["rs0"][rows, :] = rstd
        h = (xhat * gain[0]).astype(bf16)
        s["h"][rows, :] = h
        yield
        q0, q1 = head_halves(dot(h, attn[0]) * SCALE)
        s["q"][0, rows, :] = q0
        s["q"][1, rows, :] = q1
        yield
        k = dot(h, attn[1]).astype(bf16)
        v = dot(h, attn[2]).astype(bf16)
        s["k"][rows, :] = k
        s["v"][rows, :] = v
        yield
        same = doc_ids((SEG, SEG), 0, seg * SEG) == doc_ids((SEG, SEG), 1, seg * SEG)
        bias = jnp.concatenate([jnp.where(same, 0.0, -1e30)] * HEADS, 1)
        s["p"][seg], o = attend(pair_queries(q0, q1), pair_lanes(k), pair_lanes(v), bias)
        s["o"][rows, :] = o
        yield
        res = tok + dot(o, attn[3])
        s["res"][rows, :] = res
        xhat, rstd = norm_stats(res)
        s["xh1"][rows, :] = xhat.astype(bf16)
        s["rs1"][rows, :] = rstd
        n1 = (xhat * gain[1]).astype(bf16)
        s["n1"][rows, :] = n1
        yield
        s["cq"][0, rows, :], s["cq"][1, rows, :] = head_halves(dot(n1, attn[4]) * SCALE)
        yield

    def forward(seg, mem):
        rows, slots = row_cut(seg), slot_cut(seg)
        xhat, rstd = norm_stats(mem)
        s["xh4"][slots, :] = xhat
        s["rs4"][slots, :] = rstd
        m = xhat * gain[4]
        mlow = m.astype(bf16)
        s["mlow"][slots, :] = mlow
        ck = dot(mlow, attn[5]).astype(bf16)
        cv = dot(mlow, attn[6]).astype(bf16)
        s["ck"][slots, :] = ck
        s["cv"][slots, :] = cv
        yield
        s["cp"][seg], co = attend(
            pair_queries(s["cq"][0, rows, :], s["cq"][1, rows, :]), pair_lanes(ck), pair_lanes(cv), 0.0
        )
        s["co"][rows, :] = co
        yield
        res = s["res"][rows, :] + dot(co, attn[7])
        xhat, rstd = norm_stats(res)
        s["xh2"][rows, :] = xhat.astype(bf16)
        s["rs2"][rows, :] = rstd
        n2 = (xhat * gain[2]).astype(bf16)
        s["n2"][rows, :] = n2
        yield
        for c in range(0, FF, FCHUNK):
            hid, slope = gelu_both(dot(n2, win[:, c : c + FCHUNK]))
            hid = hid.astype(bf16)
            s["hid"][rows, c : c + FCHUNK] = hid
            s["gul"][rows, c : c + FCHUNK] = slope
            res = res + dot(hid, wout[c : c + FCHUNK, :])
            yield
        s["act"][rows, :] = res.astype(bf16)
        xhat, rstd = norm_stats(res)
        s["xh3"][rows, :] = xhat.astype(bf16)
        s["rs3"][rows, :] = rstd
        t = (xhat * gain[3]).astype(bf16)
        s["t"][rows, :] = t
        yield
        gate = jax.nn.sigmoid(jnp.sum(m * forget_w, -1, keepdims=True) + forget_bias)
        s["gate"][slots, :] = gate
        wq0, wq1 = head_halves(dot(mlow, attn[8]) * SCALE)
        s["wq"][0, slots, :] = wq0
        s["wq"][1, slots, :] = wq1
        wk = dot(t, attn[9]).astype(bf16)
        wv = dot(t, attn[10]).astype(bf16)
        s["wk"][rows, :] = wk
        s["wv"][rows, :] = wv
        yield
        pos = lax.broadcasted_iota(jnp.int32, (SEG, HEADS * SLOTS), 0) + seg * SEG
        s["wp"][seg], wo = attend(
            pair_queries(wq0, wq1), pair_lanes(wk), pair_lanes(wv), jnp.where(pos < ends[-1], 0.0, -1e30)
        )
        s["wo"][slots, :] = wo
        yield
        update = dot(wo, attn[11])
        s["upd"][slots, :] = mem - update
        fresh = (update + gate * (mem - update)).astype(bf16)
        s["mout"][slots, :] = fresh
        s["mem"][...] = fresh
        yield

    first_step = forward(0, s["mem"][...].astype(f32))
    next(first_step)
    gather_forward(0)
    gather_own(0)
    together(self_forward(x))
    gather_finish(0)
    gather_sends(1, True)
    gather_sends(2, True)
    rest = [step + (x <= step).astype(jnp.int32) for step in range(NSEG - 1)]
    together(self_forward(rest[0]))
    together(first_step, self_forward(rest[1]))
    together(forward(1, s["mem"][...].astype(f32)), self_forward(rest[2]))
    together(forward(2, s["mem"][...].astype(f32)))
    gather_forward(1)
    gather_forward(2)
    together(forward(NSEG - 1, s["mem"][...].astype(f32)))

    def results(indices, do):
        for k in range(2):
            seg = 2 * core + k
            here = jnp.logical_and(seg == x, mine_here)
            peer = device_at(seg, y, z, owner)
            sources = [
                (s["act"].at[rows_at(seg * SEG, SEG)], act_out), (s["mout"].at[rows_at(seg * SLOTS, SLOTS)], mout_out),
                (s["gtok"].at[rows_at(seg * SEG, SEG)], gtok_out), (s["gmem"].at[rows_at(seg * SLOTS, SLOTS)], gmem_out),
            ]
            for i in indices:
                src, dst = sources[i]

                @pl.when(jnp.logical_not(here))
                def _():
                    do(
                        remote(src, dst.at[stream], s["out_send"].at[k, i], s["out_recv"].at[stream, i], peer),
                        remote(src, dst.at[k], s["out_send"].at[k, i], s["out_recv"].at[k, i], peer),
                    )

                @pl.when(here)
                def _():
                    do(pltpu.make_async_copy(src, dst.at[stream], s["out_local"].at[i]), None)

    def results_start(copy, back):
        copy.start()

    def results_finish(copy, back):
        if back is None:
            copy.wait()
        else:
            copy.wait_send()
            back.wait_recv()

    results((0, 1), results_start)
    for i in (1, 2):
        gather_own(i)
        gather_finish(i)

    s["gain"][...] = jnp.zeros_like(s["gain"])
    s["bias"][...] = jnp.zeros_like(s["bias"])

    def backward(seg):
        rows, slots = row_cut(seg), slot_cut(seg)
        gz = (s["mcot"][slots, :].astype(f32) + s["mem"][...].astype(f32)).astype(bf16).astype(f32)
        gate = s["gate"][slots, :]
        gup = ((1.0 - gate) * gz).astype(bf16)
        s["gup"][slots, :] = gup
        g_wo = head_halves(dot(gup, attn_t[11][...]))
        yield
        dwq, dwk, dwv = attend_back(
            s["wp"][seg], pair_queries(*g_wo), pair_queries(s["wq"][0, slots, :], s["wq"][1, slots, :]),
            pair_lanes(s["wk"][rows, :]), pair_lanes(s["wv"][rows, :]),
        )
        s["dwq"][slots, :] = dwq
        s["dwk"][rows, :] = dwk
        s["dwv"][rows, :] = dwv
        yield
        gt = dot(jnp.concatenate([dwk, dwv], 1), s["attn_t"][5:7].reshape(2 * D, D))
        xhat = s["xh3"][rows, :].astype(f32)
        s["gain"][3:4, :] += jnp.sum(gt * xhat, 0, keepdims=True)
        gy = s["ocot"][rows, :].astype(f32) + norm_back(gt, gain[3], xhat, s["rs3"][rows, :])
        gyl = gy.astype(bf16)
        s["gyl"][rows, :] = gyl
        yield
        gn2 = jnp.zeros((SEG, D), f32)
        for c in range(0, FF, FCHUNK):
            ghid = dot(gyl, wout_t[:, c : c + FCHUNK])
            gul = (ghid * s["gul"][rows, c : c + FCHUNK].astype(f32)).astype(bf16)
            s["gul"][rows, c : c + FCHUNK] = gul
            gn2 = gn2 + dot(gul, win_t[c : c + FCHUNK, :])
            yield
        xhat = s["xh2"][rows, :].astype(f32)
        s["gain"][2:3, :] += jnp.sum(gn2 * xhat, 0, keepdims=True)
        gb = gy + norm_back(gn2, gain[2], xhat, s["rs2"][rows, :])
        s["res"][rows, :] = gb
        gbl = gb.astype(bf16)
        s["gbl"][rows, :] = gbl
        yield
        g_co = head_halves(dot(gbl, attn_t[7][...]))
        dgate = jnp.sum(gz * s["upd"][slots, :], -1, keepdims=True) * gate * (1.0 - gate)
        xh4 = s["xh4"][slots, :]
        s["gain"][5:6, :] += jnp.sum(dgate * (xh4 * gain[4]), 0, keepdims=True)
        s["bias"][...] += jnp.broadcast_to(dgate, (SLOTS, LANES))
        gm = dgate * forget_w
        yield
        dcq, dck, dcv = attend_back(
            s["cp"][seg], pair_queries(*g_co), pair_queries(s["cq"][0, rows, :], s["cq"][1, rows, :]),
            pair_lanes(s["ck"][slots, :]), pair_lanes(s["cv"][slots, :]),
        )
        s["dcq"][rows, :] = dcq
        s["dck"][slots, :] = dck
        s["dcv"][slots, :] = dcv
        yield
        gm = gm + dot(jnp.concatenate([dwq, dck, dcv], 1), s["attn_t"][2:5].reshape(3 * D, D))
        s["gain"][4:5, :] += jnp.sum(gm * xh4, 0, keepdims=True)
        gmem = (gate * gz + norm_back(gm, gain[4], xh4, s["rs4"][slots, :])).astype(bf16)
        s["gmem"][slots, :] = gmem
        s["mem"][...] = gmem
        yield

    s["mem"][...] = jnp.zeros_like(s["mem"])

    def backward_one(step, carry):
        together(backward(NSEG - 1 - step))
        return carry

    lax.fori_loop(0, NSEG - 1, backward_one, 0)
    last_step = backward(0)
    for _ in range(3):
        next(last_step)

    cut = pl.ds(pl.multiple_of(core * BLOCK, BLOCK), BLOCK)

    def put(i, value):
        value = value.astype(bf16)
        for j in range(LANE_CUTS):
            s["dw"][(i * LANE_CUTS + j) * BLOCK : (i * LANE_CUTS + j + 1) * BLOCK, :] = value[:, j * LANES : (j + 1) * LANES]

    def put_products(base, names):
        for i, (left, right) in enumerate(names):
            put(base + i, dot_tn(s[left][:, cut], s[right][...]))

    def small_start(axis, value):
        here = place[axis]
        s["small"][axis, here] = value
        for step in range(1, 4):
            own = s["small"].at[axis, here]
            remote(own, own, s["small_send"].at[axis], s["small_recv"].at[axis], along(axis, (here + step) % 4)).start()

    def small_finish(axis):
        all_moved(s["small"].at[axis, pl.ds(0, 3)], s["small_send"].at[axis], s["small_recv"].at[axis])
        return (s["small"][axis, 0] + s["small"][axis, 1]) + (s["small"][axis, 2] + s["small"][axis, 3])

    def others(axis, i):
        return [((i + step) % 4, step - 1, along(axis, (i + step) % 4)) for step in range(1, 4)]

    def add(refs):
        total = refs[0][...].astype(f32)
        for ref in refs[1:]:
            total += ref[...].astype(f32)
        return total.astype(bf16)

    def part_place(chunk, part):
        r = CHUNKS[chunk][part] * UNIT
        base = 64 * UNIT * (sum(sum(c) for c in CHUNKS[:chunk]) + sum(CHUNKS[chunk][:part]))
        axes = [(part + i) % 3 for i in range(3)]
        return r, base, axes, [place[a] for a in axes]

    def part_steps(chunk, part):
        r, base, axes, (i1, i2, i3) = part_place(chunk, part)
        right, left = along(axes[0], (i1 + 1) % 4), along(axes[0], (i1 + 3) % 4)
        near, far, mid, quad, last = (s[name][chunk][part] for name in ("near", "far", "mid", "quad", "last"))
        dw, mine = s["dw"], full_ref.at[core]

        def copy(src, dst, device, i):
            remote(src, dst, s["send"].at[chunk], s["recv"].at[chunk, part, i], device).start()

        def arrived(ref, i):
            remote(ref, ref, s["send"].at[chunk], s["recv"].at[chunk, part, i], sibling).wait_recv()

        def block(b, first=0, count=16):
            return rows_at(base + (b % 4) * 16 * r + first * r, count * r)

        def pass_on(rows, device, i):
            copy(mine.at[rows], mine.at[rows], device, i)

        def pass_over(rows):
            remote(mine.at[rows], mine.at[rows], s["send"].at[chunk], s["over"].at[chunk], sibling).start()

        half0, half1 = pl.ds(0, 8 * r), pl.ds(8 * r, 8 * r)
        copy(dw.at[block(i1 + 2, 0, 8)], near.at[0], right, 0)
        copy(dw.at[block(i1 + 2, 8, 8)], near.at[1], left, 0)
        copy(dw.at[block(i1 + 1, 8, 8)], far.at[0, half1], right, 1)
        copy(dw.at[block(i1 + 3, 0, 8)], far.at[1, half0], left, 1)
        yield
        arrived(near, 0)
        near[0] = add([near.at[0], dw.at[block(i1 + 1, 0, 8)]])
        copy(near.at[0], far.at[0, half0], right, 1)
        near[1] = add([near.at[1], dw.at[block(i1 + 3, 8, 8)]])
        copy(near.at[1], far.at[1, half1], left, 1)
        yield
        arrived(far, 1)
        far[0] = add([far.at[0], far.at[1], dw.at[block(i1)]])
        for b, slot, to in others(axes[1], i2):
            copy(far.at[0, rows_at(b * 4 * r, 4 * r)], mid.at[slot], to, 2)
        yield
        arrived(mid, 2)
        middle = [mid.at[0], mid.at[1], mid.at[2], far.at[0, rows_at(i2 * 4 * r, 4 * r)]]
        home = rows_at(base + (i1 * 16 + i2 * 4) * r, 4 * r)
        quad[i3] = add(middle)
        for _, _, to in others(axes[2], i3):
            copy(quad.at[i3], quad.at[i3], to, 3)
        yield
        arrived(quad.at[pl.ds(0, 3)], 3)
        last[...] = add([quad.at[i] for i in range(4)])
        keep = pltpu.make_async_copy(last, mine.at[home], s["own"].at[chunk, part])
        keep.start()
        for _, _, to in others(axes[1], i2):
            copy(last, mine.at[home], to, 4)
        yield
        keep.wait()
        arrived(mine.at[rows_at(base, 12 * r)], 4)
        pass_on(block(i1), right, 5)
        pass_on(block(i1), left, 5)
        pass_over(block(i1))
        yield
        arrived(mine.at[rows_at(base, 32 * r)], 5)
        pass_on(block(i1 + 3, 0, 8), right, 6)
        pass_on(block(i1 + 1, 8, 8), left, 6)
        pass_over(block(i1 + 3))
        pass_over(block(i1 + 1))
        yield
        arrived(mine.at[block(i1 + 2)], 6)
        pass_over(block(i1 + 2))
        yield
        if part == 2:
            units = sum(CHUNKS[chunk]) * UNIT
            start = base + 64 * r - 64 * units
            got = full_ref.at[1 - core, rows_at(start, 64 * units)]
            remote(got, got, s["send"].at[chunk], s["over"].at[chunk], sibling).wait_recv()
            sent = full_ref.at[core, rows_at(0, 196 * units)]
            remote(sent, sent, s["send"].at[chunk], s["over"].at[chunk], sibling).wait_send()
        yield

    chunks = [[part_steps(chunk, part) for part in range(3)] for chunk in range(len(CHUNKS))]

    def go(*order):
        for chunk in order:
            for part in chunks[chunk]:
                next(part)

    for i in range(4):
        cut_i = pl.ds(pl.multiple_of(core * 4 * BLOCK + i * BLOCK, BLOCK), BLOCK)
        put(i, dot_tn(s["hid"][:, cut_i], s["gyl"][...]))
        if i % 2:
            next(chunks[0][i // 2])
    put_products(4, [("mlow", "dwq"), ("t", "dwk")])
    next(chunks[0][2])
    for _ in range(FF // FCHUNK):
        next(last_step)
    put_products(6, [("t", "dwv"), ("wo", "gup")])
    for i in range(4):
        put(8 + i, dot_tn(s["n2"][:, cut], s["gul"][:, i * D : (i + 1) * D]))
    go(1)
    together(last_step)
    results((3,), results_start)
    put_products(12, [("n1", "dcq"), ("mlow", "dck"), ("mlow", "dcv"), ("co", "gbl")])

    gn1 = dot_nt(s["dcq"][...], attn[4])
    xhat = s["xh1"][...].astype(f32)
    s["gain"][1:2, :] = jnp.sum(gn1 * xhat, 0, keepdims=True)
    ga = s["res"][...] + norm_back(gn1, gain[1], xhat, s["rs1"][...])
    s["res"][...] = ga
    gal = ga.astype(bf16)
    s["gal"][...] = gal
    s["cq"][0], s["cq"][1] = head_halves(dot_nt(gal, attn[3]))
    put_products(16, [("o", "gal")])
    go(2)

    def self_backward(seg):
        rows = row_cut(seg)
        s["dq"][rows, :], s["dk"][rows, :], s["dv"][rows, :] = attend_back(
            s["p"][seg], pair_queries(s["cq"][0, rows, :], s["cq"][1, rows, :]),
            pair_queries(s["q"][0, rows, :], s["q"][1, rows, :]),
            pair_lanes(s["k"][rows, :]), pair_lanes(s["v"][rows, :]),
        )

    self_backward(0)
    self_backward(1)
    self_backward(2)
    go(0)
    self_backward(3)
    gh = dot_nt(s["dq"][...], attn[0]) + dot_nt(s["dk"][...], attn[1]) + dot_nt(s["dv"][...], attn[2])
    go(1)
    xhat = s["xh0"][...].astype(f32)
    s["gain"][0:1, :] = jnp.sum(gh * xhat, 0, keepdims=True)
    s["gtok"][...] = (s["res"][...] + norm_back(gh, gain[0], xhat, s["rs0"][...])).astype(bf16)
    s["gain"][6:7, 0:SLOTS] = jnp.sum(jnp.where(diagonal, s["bias"][:, 0:SLOTS], 0.0), 0, keepdims=True)
    small_start(0, s["gain"][...])
    results((2,), results_start)
    put_products(17, [("h", "dq"), ("h", "dk"), ("h", "dv")])
    go(3, 2, 0)
    total = small_finish(0)
    small_start(1, total)
    go(1, 3, 2, 0)
    total = small_finish(1)
    small_start(2, total)
    go(3, 1, 2, 0, 3)
    small_out[...] = small_finish(2)
    go(1, 2, 3, 0, 1, 2, 3, 0, 3, 1, 2, 3, 0, 1, 3, 2, 0, 1, 2)
    results((0, 1, 2, 3), results_finish)


def run_fused(tok, ocot, mcot, mem, lens, attn, win, wout, gains, fw, fb):
    vmem = pl.BlockSpec(memory_space=pltpu.VMEM)
    hbm = pl.BlockSpec(memory_space=pl.ANY)
    return pl.pallas_call(
        fused_kernel,
        out_shape=(
            jax.ShapeDtypeStruct((2, FLAT, LANES), bf16),
            jax.ShapeDtypeStruct((2, SEG, D), bf16),
            jax.ShapeDtypeStruct((2, SLOTS, D), bf16),
            jax.ShapeDtypeStruct((2, SEG, D), bf16),
            jax.ShapeDtypeStruct((2, SLOTS, D), bf16),
            jax.ShapeDtypeStruct((8, D), f32),
        ),
        in_specs=[hbm] * 11,
        out_specs=[hbm] * 5 + [vmem],
        scratch_shapes=[scratch_buffers()],
        compiler_params=pltpu.CompilerParams(collective_id=1, has_side_effects=True, vmem_limit_bytes=63 << 20),
        name="layer_and_sums",
    )(tok, ocot, mcot, mem, lens, attn, win, wout, gains, fw, fb)


def widen_kernel(
    full_ref, act_ref, mem_ref, gtok_ref, gmem_ref, small_ref,
    attn_ref, in_ref, out_ref, act_out, mem_out, gtok_out, gmem_out, gains_out, fw_out, fb_out,
    full_s, wide_s, load_sem, store_sem,
):
    def load(i):
        return [
            pltpu.make_async_copy(full_ref.at[half, i], full_s.at[i, half], load_sem.at[i, half]) for half in range(2)
        ]

    def target(i, half):
        if i < 4:
            return out_ref.at[pl.ds(half * 4 * BLOCK + i * BLOCK, BLOCK), :]
        if 8 <= i < 12:
            return in_ref.at[pl.ds(half * BLOCK, BLOCK), pl.ds((i - 8) * D, D)]
        index = i + 4 if i < 8 else i - 8 if i < 16 else 3 if i == 16 else i - 17
        return attn_ref.at[index, pl.ds(half * BLOCK, BLOCK), :]

    def store(i, half):
        return pltpu.make_async_copy(wide_s.at[i, half], target(i, half), store_sem)

    for i in range(NBLOCKS):
        for copy in load(i):
            copy.start()
    act_out[...] = act_ref[...]
    mem_out[...] = mem_ref[...]
    gtok_out[...] = gtok_ref[...].astype(f32)
    gmem_out[...] = gmem_ref[...].astype(f32)
    gains_out[...] = small_ref[0:5, :]
    fw_out[...] = small_ref[5:6, :]
    fb_out[...] = small_ref[6:7, 0:SLOTS]
    for i in range(NBLOCKS):
        for half, copy in enumerate(load(i)):
            copy.wait()
            for j in range(LANE_CUTS):
                wide_s[i, half, :, j * LANES : (j + 1) * LANES] = full_s[i, half, j].astype(f32)
            store(i, half).start()
    pltpu.make_async_copy(wide_s, wide_s, store_sem).wait()


def run_widen(full, *others):
    hbm = pl.BlockSpec(memory_space=pl.ANY)
    vmem = pl.BlockSpec(memory_space=pltpu.VMEM)
    return pl.pallas_call(
        widen_kernel,
        out_shape=(
            jax.ShapeDtypeStruct((12, D, D), f32),
            jax.ShapeDtypeStruct((D, FF), f32),
            jax.ShapeDtypeStruct((FF, D), f32),
            jax.ShapeDtypeStruct((2, SEG, D), bf16),
            jax.ShapeDtypeStruct((2, SLOTS, D), bf16),
            jax.ShapeDtypeStruct((2, SEG, D), f32),
            jax.ShapeDtypeStruct((2, SLOTS, D), f32),
            jax.ShapeDtypeStruct((5, D), f32),
            jax.ShapeDtypeStruct((1, D), f32),
            jax.ShapeDtypeStruct((1, SLOTS), f32),
        ),
        in_specs=[hbm] + [vmem] * 5,
        out_specs=[hbm] * 3 + [vmem] * 7,
        scratch_shapes=[
            pltpu.VMEM((NBLOCKS, 2, LANE_CUTS, BLOCK, LANES), bf16),
            pltpu.VMEM((NBLOCKS, 2, BLOCK, D), f32),
            pltpu.SemaphoreType.DMA((NBLOCKS, 2)),
            pltpu.SemaphoreType.DMA,
        ],
        compiler_params=pltpu.CompilerParams(vmem_limit_bytes=60 << 20),
        name="widen_gradients",
    )(full, *others)


def body(
    tokens, memory_start, doc_lengths, attn_weights, ffn_in, ffn_out, gains, forget_w, forget_bias,
    out_cotangent, memory_cotangent,
):
    full, *others = run_fused(
        tokens, out_cotangent, memory_cotangent, memory_start, doc_lengths,
        attn_weights.reshape(12, D, D), ffn_in, ffn_out, gains, forget_w.reshape(1, D), forget_bias.reshape(1, SLOTS),
    )
    grad_attn, grad_in, grad_out, acts, mems, gtok, gmem, grad_gains, grad_fw, grad_fb = run_widen(
        full.reshape(2, NBLOCKS, LANE_CUTS, BLOCK, LANES), *others
    )
    return (
        acts, mems, gtok, gmem, grad_attn.reshape(3, 4, D, D), grad_in, grad_out,
        grad_gains, grad_fw.reshape(D), grad_fb.reshape(SLOTS),
    )


def solution(mesh):
    return jax.shard_map(
        body,
        mesh=mesh,
        in_specs=(
            P("doc", "seg", None), P("doc", None, None), P("doc", None), P(), P(), P(), P(), P(), P(),
            P("doc", "seg", None), P("doc", "seg", None),
        ),
        out_specs=(
            P("doc", "seg", None), P("doc", "seg", None), P("doc", "seg", None), P("doc", "seg", None),
            P(), P(), P(), P(), P(), P(),
        ),
        check_vma=False,
    )
```

```python
from types import SimpleNamespace

import jax
import jax.numpy as jnp
from jax import lax
from jax.experimental import pallas as pl
from jax.experimental.pallas import tpu as pltpu
from jax.sharding import PartitionSpec as P

HEADS = 8
NDOC = 8
D = 512
FF = 2048
SLOTS = 64
SEG = 128
NSEG = 4
ROWS = NSEG * SEG
MROWS = NSEG * SLOTS
PAIRS = 4
PAIR = 128
FCHUNK = 2048
BLOCK = 256
NBLOCKS = 20
LANES = 128
LANE_CUTS = D // LANES
FLAT = NBLOCKS * BLOCK * LANE_CUTS
MESH = pl.DeviceIdType.MESH
SCALE = 0.125

f32 = jnp.float32
bf16 = jnp.bfloat16


def dot(a, b):
    return lax.dot_general(a, b, (((1,), (0,)), ((), ())), preferred_element_type=f32)


def dot_nt(a, b):
    return lax.dot_general(a, b, (((1,), (1,)), ((), ())), preferred_element_type=f32)


def dot_tn(a, b):
    return lax.dot_general(a, b, (((0,), (0,)), ((), ())), preferred_element_type=f32)


def norm_stats(values):
    centered = values - jnp.mean(values, -1, keepdims=True)
    rstd = lax.rsqrt(jnp.mean(centered * centered, -1, keepdims=True) + 1e-05)
    return centered * rstd, rstd


def norm_back(grad, gain, xhat, rstd):
    scaled = grad * gain
    mean_one = jnp.mean(scaled, -1, keepdims=True)
    mean_two = jnp.mean(scaled * xhat, -1, keepdims=True)
    return rstd * (scaled - mean_one - xhat * mean_two)


def head_halves(values):
    low_half = lax.broadcasted_iota(jnp.int32, (16, values.shape[1]), 1) % PAIR < PAIR // 2
    first = jnp.where(low_half, 1.0, 0.0).astype(bf16)[0:1, :]
    second = jnp.where(low_half, 0.0, 1.0).astype(bf16)[0:1, :]
    values = values.astype(bf16)
    return values * first, values * second


def join_halves(stacked):
    rows = stacked.shape[0] // 2
    low_half = lax.broadcasted_iota(jnp.int32, (rows, PAIR), 1) < PAIR // 2
    return jnp.where(low_half, stacked[:rows], stacked[rows:])


def attend(queries, keys, values, bias):
    scores = jnp.concatenate([dot_nt(k, q) for k, q in zip(keys, queries)], 1) + bias
    expd = jnp.exp(scores - jnp.max(scores, 0, keepdims=True))
    probs = (expd * (1.0 / jnp.sum(expd, 0, keepdims=True))).astype(bf16)
    width = queries[0].shape[0]
    mixed = [join_halves(dot_tn(probs[:, i * width : (i + 1) * width], v)) for i, v in enumerate(values)]
    return probs, jnp.concatenate(mixed, 1).astype(bf16)


def attend_back(probs, grads, queries, keys, values):
    width = queries[0].shape[0]
    wide = probs.astype(f32)
    dp = jnp.concatenate([dot_nt(v, g) for v, g in zip(values, grads)], 1)
    ds = (wide * (dp - jnp.sum(wide * dp, 0, keepdims=True))).astype(bf16)
    cuts = [slice(i * width, (i + 1) * width) for i in range(PAIRS)]
    dq = [join_halves(dot_tn(ds[:, cut], k)) for cut, k in zip(cuts, keys)]
    dk = [dot(ds[:, cut], q) for cut, q in zip(cuts, queries)]
    dv = [dot(probs[:, cut], g) for cut, g in zip(cuts, grads)]
    join = lambda parts: jnp.concatenate(parts, 1)
    return (join(dq) * SCALE).astype(bf16), join(dk).astype(bf16), join(dv).astype(bf16)


def pair_lanes(values):
    return [values[:, i * PAIR : (i + 1) * PAIR] for i in range(PAIRS)]


def pair_queries(first, second):
    return [jnp.concatenate(halves, 0) for halves in zip(pair_lanes(first), pair_lanes(second))]


def gelu_both(u):
    square = u * u
    tanh = jnp.tanh(0.7978845608028654 * u * (1.0 + 0.044715 * square))
    half = 0.5 + 0.5 * tanh
    hidden = u * half
    rest, square = (1.0 - tanh).astype(bf16), square.astype(bf16)
    slope = half.astype(bf16) + hidden.astype(bf16) * rest * (bf16(0.7978845608028654) + bf16(0.1070322243) * square)
    return hidden, slope


CHUNKS = ((2, 2, 2), (2, 2, 2), (1, 2, 2), (1, 1, 1))
UNIT = 16

TURNED = (7, 11, 8, 5, 6, 9, 10)


def scratch_buffers():
    def rows(dtype=bf16, width=D):
        return pltpu.VMEM((ROWS, width), dtype)

    def slots(dtype=bf16, width=D):
        return pltpu.VMEM((MROWS, width), dtype)

    def two(count):
        return pltpu.VMEM((2, count, D), bf16)

    def parts(shape_of):
        return [[pltpu.VMEM(shape_of(count * UNIT), bf16) for count in chunk] for chunk in CHUNKS]

    dma = pltpu.SemaphoreType.DMA
    return dict(
        attn=pltpu.VMEM((12, D, D), bf16), win=pltpu.VMEM((D, FF), bf16), wout=pltpu.VMEM((FF, D), bf16),
        attn_t=pltpu.VMEM((len(TURNED), D, D), bf16), win_t=pltpu.VMEM((FF, D), bf16), wout_t=pltpu.VMEM((D, FF), bf16),
        tok=rows(), ocot=rows(), mcot=slots(), mem=pltpu.VMEM((SLOTS, D), bf16),
        lens_own=pltpu.VMEM((8, LANES), jnp.int32), lens=pltpu.VMEM((8, LANES), jnp.int32),
        act=rows(), mout=slots(), gtok=rows(), gmem=slots(),
        h=rows(), q=two(ROWS), k=rows(), v=rows(), p=pltpu.VMEM((NSEG, SEG, HEADS * SEG), bf16), o=rows(),
        xh0=rows(), rs0=rows(f32, 1),
        res=rows(f32), n1=rows(), xh1=rows(), rs1=rows(f32, 1), cq=two(ROWS), ck=slots(), cv=slots(),
        cp=pltpu.VMEM((NSEG, SLOTS, HEADS * SEG), bf16), co=rows(),
        n2=rows(), xh2=rows(), rs2=rows(f32, 1), hid=rows(bf16, FF), gul=rows(bf16, FF),
        t=rows(), xh3=rows(), rs3=rows(f32, 1),
        xh4=slots(f32), rs4=slots(f32, 1), mlow=slots(), gate=slots(f32, 1), upd=slots(f32),
        wq=two(MROWS), wk=rows(), wv=rows(), wp=pltpu.VMEM((NSEG, SEG, HEADS * SLOTS), bf16), wo=slots(),
        gup=slots(), dwq=slots(), dwk=rows(), dwv=rows(), gyl=rows(), gbl=rows(),
        dcq=rows(), dck=slots(), dcv=slots(),
        gal=rows(), dq=rows(), dk=rows(), dv=rows(),
        gain=pltpu.VMEM((8, D), f32), bias=pltpu.VMEM((SLOTS, LANES), f32),
        dw=pltpu.VMEM((FLAT, LANES), bf16),
        near=parts(lambda r: (2, 8 * r, LANES)), far=parts(lambda r: (2, 16 * r, LANES)),
        mid=parts(lambda r: (3, 4 * r, LANES)), quad=parts(lambda r: (4, 4 * r, LANES)), last=parts(lambda r: (4 * r, LANES)),
        small=pltpu.VMEM((3, 5, 8, D), f32),
        in_send=dma((2, 2, 3)), in_recv=dma((4, 3)), first_send=dma((2,)), first_recv=dma((2,)),
        pass_send=dma((3,)), pass_recv=dma((3,)), in_local=dma((5,)), load=dma((8,)),
        gains=pltpu.VMEM((5, D), f32), fw=pltpu.VMEM((1, D), f32), fb=pltpu.VMEM((1, SLOTS), f32),
        lens_in=pltpu.VMEM((2, NDOC), jnp.int32),
        send=dma((len(CHUNKS),)), recv=dma((len(CHUNKS), 3, 7)), over=dma((len(CHUNKS),)), own=dma((len(CHUNKS), 3)),
        out_send=dma((2, 4)), out_recv=dma((2, 4)), out_local=dma((4,)),
        small_send=dma((3,)), small_recv=dma((3,)),
    )


def my_place():
    doc = lax.axis_index("doc")
    return lax.axis_index("seg"), doc // 8, (doc // 2) % 4, doc % 2


def device_at(x, y, z, core):
    return (x, y * 8 + z * 2 + core)


def remote(src, dst, send_sem, recv_sem, device):
    return pltpu.make_async_remote_copy(
        src_ref=src, dst_ref=dst, send_sem=send_sem, recv_sem=recv_sem, device_id=device, device_id_type=MESH
    )


def signal(sem, device):
    pl.semaphore_signal(sem, inc=1, device_id=device, device_id_type=MESH)


def fused_kernel(
    tok_ref, ocot_ref, mcot_ref, mem_ref, len_ref, attn_ref, win_ref, wout_ref, gains_ref, fw_ref, fb_ref,
    full_ref, act_out, mout_out, gtok_out, gmem_out, small_out,
    scratch,
):
    s = SimpleNamespace(**scratch)
    place = my_place()
    x, y, z, core = place
    owner, stream = x // 2, x % 2
    mine_here = owner == core
    sibling = device_at(x, y, z, 1 - core)

    def along(axis, coordinate):
        there = list(place)
        there[axis] = coordinate
        return device_at(*there)

    def rows_at(first, count):
        return pl.ds(pl.multiple_of(first, UNIT), count)

    loads = [
        pltpu.make_async_copy(attn_ref.at[pl.ds(0, 4)], s.attn.at[pl.ds(0, 4)], s.load.at[0]),
        pltpu.make_async_copy(attn_ref.at[pl.ds(4, 8)], s.attn.at[pl.ds(4, 8)], s.load.at[1]),
        pltpu.make_async_copy(win_ref, s.win, s.load.at[2]),
        pltpu.make_async_copy(wout_ref, s.wout, s.load.at[3]),
    ]
    small_loads = [
        pltpu.make_async_copy(src, dst, s.load.at[4 + i])
        for i, (src, dst) in enumerate([(len_ref, s.lens_in), (gains_ref, s.gains), (fw_ref, s.fw), (fb_ref, s.fb)])
    ]
    for load in small_loads:
        load.start()
    for i in (1, 2, 3, 0):
        loads[i].start()

    barrier = pltpu.get_barrier_semaphore()
    for step in range(1, 4):
        signal(barrier, device_at((x + step) % 4, y, z, owner))
    for axis in range(3):
        for step in range(1, 4):
            signal(barrier, along(axis, (place[axis] + step) % 4))
    signal(barrier, sibling)
    for k in range(2):

        @pl.when(jnp.logical_or(2 * core + k != x, owner != core))
        def _():
            signal(barrier, device_at(2 * core + k, y, z, owner))

    small_loads[0].wait()
    s.lens_own[...] = jnp.zeros_like(s.lens_own)
    s.lens_own[0:2, 0:NDOC] = s.lens_in[...]
    pl.semaphore_wait(barrier, 16 - 3 * mine_here.astype(jnp.int32))

    arrays = [(tok_ref, s.tok, SEG), (ocot_ref, s.ocot, SEG), (mcot_ref, s.mcot, SLOTS)]

    def gather_sends(i, start):
        src, dst, count = arrays[i]
        half = count // 2
        for st in range(2):
            chip = 2 * core + st

            @pl.when(chip != x)
            def _():
                for to_core in range(2):
                    copy = remote(
                        src.at[st, pl.ds(to_core * half, half)], dst.at[rows_at(x * count + to_core * half, half)],
                        s.in_send.at[st, to_core, i], s.in_recv.at[x, i], device_at(chip, y, z, to_core),
                    )
                    copy.start() if start else copy.wait_send()

            @pl.when(chip == x)
            def _():
                target = dst.at[rows_at(x * count, count)]
                copy = remote(src.at[st], target, s.in_send.at[st, 0, i], s.in_recv.at[x, i], sibling)
                if start:
                    pltpu.make_async_copy(src.at[st], target, s.in_local.at[i]).start()
                    copy.start()
                else:
                    copy.wait_send()

    def gather_own(i):
        src, dst, count = arrays[i]
        whole = dst.at[rows_at(x * count, count)]

        @pl.when(mine_here)
        def _():
            pltpu.make_async_copy(src.at[stream], whole, s.in_local.at[i]).wait()

        @pl.when(jnp.logical_not(mine_here))
        def _():
            remote(whole, whole, s.in_send.at[0, 0, i], s.in_recv.at[x, i], sibling).wait_recv()

    def all_moved(ref, send_sem, recv_sem):
        copy = remote(ref, ref, send_sem, recv_sem, sibling)
        copy.wait_send()
        copy.wait_recv()

    def gather_forward(i):
        src, dst, count = arrays[i]
        half = count // 2
        for step in (1, 3, 2):
            seg = (x + step) % 4
            part = dst.at[rows_at(seg * count + core * half, half)]
            remote(
                part, part, s.in_send.at[0, 0, i], s.in_recv.at[seg, i], device_at(seg, y, z, owner)
            ).wait_recv()
            remote(part, part, s.pass_send.at[i], s.pass_recv.at[i], sibling).start()

    def gather_finish(i):
        src, dst, count = arrays[i]
        gather_sends(i, False)
        three_halves = dst.at[pl.ds(0, 3 * count // 2)]
        all_moved(three_halves, s.pass_send.at[i], s.pass_recv.at[i])

    gather_sends(0, True)

    firsts = [(mem_ref.at[stream], s.mem), (s.lens_own, s.lens)]
    for i, (src, dst) in enumerate(firsts):

        @pl.when(mine_here)
        def _():
            remote(src, dst, s.first_send.at[i], s.first_recv.at[i], sibling).start()
            pltpu.make_async_copy(src, dst, s.in_local.at[3 + i]).start()

    loads[1].wait()
    for i, index in enumerate(TURNED):
        s.attn_t[i] = jnp.transpose(s.attn[index])
    loads[2].wait()
    for c in range(0, FF, D):
        s.win_t[c : c + D, :] = jnp.transpose(s.win[:, c : c + D])
    loads[3].wait()
    for c in range(0, FF, D):
        s.wout_t[:, c : c + D] = jnp.transpose(s.wout[c : c + D, :])
    loads[0].wait()

    for i, (src, dst) in enumerate(firsts):

        @pl.when(mine_here)
        def _():
            remote(src, dst, s.first_send.at[i], s.first_recv.at[i], sibling).wait_send()
            pltpu.make_async_copy(src, dst, s.in_local.at[3 + i]).wait()

        @pl.when(jnp.logical_not(mine_here))
        def _():
            remote(src, dst, s.first_send.at[i], s.first_recv.at[i], sibling).wait_recv()

    attn, win, wout = s.attn, s.win, s.wout
    attn_t = {index: s.attn_t.at[i] for i, index in enumerate(TURNED)}
    win_t, wout_t = s.win_t, s.wout_t
    for load in small_loads[1:]:
        load.wait()
    gain = [s.gains[i : i + 1, :] for i in range(5)]
    forget_w = s.fw[...]
    square = (SLOTS, SLOTS)
    diagonal = lax.broadcasted_iota(jnp.int32, square, 0) == lax.broadcasted_iota(jnp.int32, square, 1)
    forget_bias = jnp.sum(jnp.where(diagonal, jnp.broadcast_to(s.fb[...], square), 0.0), -1, keepdims=True)

    ends = []
    for j in range(NDOC):
        ends.append(s.lens[pl.ds(stream, 1), j : j + 1] + (ends[-1] if ends else 0))

    def doc_ids(shape, dim, base):
        pos = lax.broadcasted_iota(jnp.int32, shape, dim) + base
        return sum((end <= pos).astype(jnp.int32) for end in ends)

    def row_cut(seg):
        return pl.ds(pl.multiple_of(seg * SEG, SEG), SEG)

    def slot_cut(seg):
        return pl.ds(pl.multiple_of(seg * SLOTS, SLOTS), SLOTS)

    def together(*works):
        works = list(works)
        while works:
            for work in list(works):
                try:
                    next(work)
                except StopIteration:
                    works.remove(work)

    def self_forward(seg):
        rows = row_cut(seg)
        tok = s.tok[rows, :].astype(f32)
        xhat, rstd = norm_stats(tok)
        s.xh0[rows, :] = xhat.astype(bf16)
        s.rs0[rows, :] = rstd
        h = (xhat * gain[0]).astype(bf16)
        s.h[rows, :] = h
        yield
        q0, q1 = head_halves(dot(h, attn[0]) * SCALE)
        s.q[0, rows, :] = q0
        s.q[1, rows, :] = q1
        yield
        k = dot(h, attn[1]).astype(bf16)
        v = dot(h, attn[2]).astype(bf16)
        s.k[rows, :] = k
        s.v[rows, :] = v
        yield
        same = doc_ids((SEG, SEG), 0, seg * SEG) == doc_ids((SEG, SEG), 1, seg * SEG)
        bias = jnp.concatenate([jnp.where(same, 0.0, -1e30)] * HEADS, 1)
        s.p[seg], o = attend(pair_queries(q0, q1), pair_lanes(k), pair_lanes(v), bias)
        s.o[rows, :] = o
        yield
        res = tok + dot(o, attn[3])
        s.res[rows, :] = res
        xhat, rstd = norm_stats(res)
        s.xh1[rows, :] = xhat.astype(bf16)
        s.rs1[rows, :] = rstd
        n1 = (xhat * gain[1]).astype(bf16)
        s.n1[rows, :] = n1
        yield
        s.cq[0, rows, :], s.cq[1, rows, :] = head_halves(dot(n1, attn[4]) * SCALE)
        yield

    def forward(seg, mem):
        rows, slots = row_cut(seg), slot_cut(seg)
        xhat, rstd = norm_stats(mem)
        s.xh4[slots, :] = xhat
        s.rs4[slots, :] = rstd
        m = xhat * gain[4]
        mlow = m.astype(bf16)
        s.mlow[slots, :] = mlow
        ck = dot(mlow, attn[5]).astype(bf16)
        cv = dot(mlow, attn[6]).astype(bf16)
        s.ck[slots, :] = ck
        s.cv[slots, :] = cv
        yield
        s.cp[seg], co = attend(
            pair_queries(s.cq[0, rows, :], s.cq[1, rows, :]), pair_lanes(ck), pair_lanes(cv), 0.0
        )
        s.co[rows, :] = co
        yield
        res = s.res[rows, :] + dot(co, attn[7])
        xhat, rstd = norm_stats(res)
        s.xh2[rows, :] = xhat.astype(bf16)
        s.rs2[rows, :] = rstd
        n2 = (xhat * gain[2]).astype(bf16)
        s.n2[rows, :] = n2
        yield
        for c in range(0, FF, FCHUNK):
            hid, slope = gelu_both(dot(n2, win[:, c : c + FCHUNK]))
            hid = hid.astype(bf16)
            s.hid[rows, c : c + FCHUNK] = hid
            s.gul[rows, c : c + FCHUNK] = slope
            res = res + dot(hid, wout[c : c + FCHUNK, :])
            yield
        s.act[rows, :] = res.astype(bf16)
        xhat, rstd = norm_stats(res)
        s.xh3[rows, :] = xhat.astype(bf16)
        s.rs3[rows, :] = rstd
        t = (xhat * gain[3]).astype(bf16)
        s.t[rows, :] = t
        yield
        gate = jax.nn.sigmoid(jnp.sum(m * forget_w, -1, keepdims=True) + forget_bias)
        s.gate[slots, :] = gate
        wq0, wq1 = head_halves(dot(mlow, attn[8]) * SCALE)
        s.wq[0, slots, :] = wq0
        s.wq[1, slots, :] = wq1
        wk = dot(t, attn[9]).astype(bf16)
        wv = dot(t, attn[10]).astype(bf16)
        s.wk[rows, :] = wk
        s.wv[rows, :] = wv
        yield
        pos = lax.broadcasted_iota(jnp.int32, (SEG, HEADS * SLOTS), 0) + seg * SEG
        s.wp[seg], wo = attend(
            pair_queries(wq0, wq1), pair_lanes(wk), pair_lanes(wv), jnp.where(pos < ends[-1], 0.0, -1e30)
        )
        s.wo[slots, :] = wo
        yield
        update = dot(wo, attn[11])
        s.upd[slots, :] = mem - update
        fresh = (update + gate * (mem - update)).astype(bf16)
        s.mout[slots, :] = fresh
        s.mem[...] = fresh
        yield

    first_step = forward(0, s.mem[...].astype(f32))
    next(first_step)
    gather_forward(0)
    gather_own(0)
    together(self_forward(x))
    gather_finish(0)
    gather_sends(1, True)
    gather_sends(2, True)
    rest = [step + (x <= step).astype(jnp.int32) for step in range(NSEG - 1)]
    together(self_forward(rest[0]))
    together(first_step, self_forward(rest[1]))
    together(forward(1, s.mem[...].astype(f32)), self_forward(rest[2]))
    together(forward(2, s.mem[...].astype(f32)))
    gather_forward(1)
    gather_forward(2)
    together(forward(NSEG - 1, s.mem[...].astype(f32)))

    def results(indices, do):
        for k in range(2):
            seg = 2 * core + k
            here = jnp.logical_and(seg == x, mine_here)
            peer = device_at(seg, y, z, owner)
            sources = [
                (s.act.at[rows_at(seg * SEG, SEG)], act_out), (s.mout.at[rows_at(seg * SLOTS, SLOTS)], mout_out),
                (s.gtok.at[rows_at(seg * SEG, SEG)], gtok_out), (s.gmem.at[rows_at(seg * SLOTS, SLOTS)], gmem_out),
            ]
            for i in indices:
                src, dst = sources[i]

                @pl.when(jnp.logical_not(here))
                def _():
                    do(
                        remote(src, dst.at[stream], s.out_send.at[k, i], s.out_recv.at[stream, i], peer),
                        remote(src, dst.at[k], s.out_send.at[k, i], s.out_recv.at[k, i], peer),
                    )

                @pl.when(here)
                def _():
                    do(pltpu.make_async_copy(src, dst.at[stream], s.out_local.at[i]), None)

    def results_start(copy, back):
        copy.start()

    def results_finish(copy, back):
        if back is None:
            copy.wait()
        else:
            copy.wait_send()
            back.wait_recv()

    results((0, 1), results_start)
    for i in (1, 2):
        gather_own(i)
        gather_finish(i)

    s.gain[...] = jnp.zeros_like(s.gain)
    s.bias[...] = jnp.zeros_like(s.bias)

    def backward(seg):
        rows, slots = row_cut(seg), slot_cut(seg)
        gz = (s.mcot[slots, :].astype(f32) + s.mem[...].astype(f32)).astype(bf16).astype(f32)
        gate = s.gate[slots, :]
        gup = ((1.0 - gate) * gz).astype(bf16)
        s.gup[slots, :] = gup
        g_wo = head_halves(dot(gup, attn_t[11][...]))
        yield
        dwq, dwk, dwv = attend_back(
            s.wp[seg], pair_queries(*g_wo), pair_queries(s.wq[0, slots, :], s.wq[1, slots, :]),
            pair_lanes(s.wk[rows, :]), pair_lanes(s.wv[rows, :]),
        )
        s.dwq[slots, :] = dwq
        s.dwk[rows, :] = dwk
        s.dwv[rows, :] = dwv
        yield
        gt = dot(jnp.concatenate([dwk, dwv], 1), s.attn_t[5:7].reshape(2 * D, D))
        xhat = s.xh3[rows, :].astype(f32)
        s.gain[3:4, :] += jnp.sum(gt * xhat, 0, keepdims=True)
        gy = s.ocot[rows, :].astype(f32) + norm_back(gt, gain[3], xhat, s.rs3[rows, :])
        gyl = gy.astype(bf16)
        s.gyl[rows, :] = gyl
        yield
        gn2 = jnp.zeros((SEG, D), f32)
        for c in range(0, FF, FCHUNK):
            ghid = dot(gyl, wout_t[:, c : c + FCHUNK])
            gul = (ghid * s.gul[rows, c : c + FCHUNK].astype(f32)).astype(bf16)
            s.gul[rows, c : c + FCHUNK] = gul
            gn2 = gn2 + dot(gul, win_t[c : c + FCHUNK, :])
            yield
        xhat = s.xh2[rows, :].astype(f32)
        s.gain[2:3, :] += jnp.sum(gn2 * xhat, 0, keepdims=True)
        gb = gy + norm_back(gn2, gain[2], xhat, s.rs2[rows, :])
        s.res[rows, :] = gb
        gbl = gb.astype(bf16)
        s.gbl[rows, :] = gbl
        yield
        g_co = head_halves(dot(gbl, attn_t[7][...]))
        dgate = jnp.sum(gz * s.upd[slots, :], -1, keepdims=True) * gate * (1.0 - gate)
        xh4 = s.xh4[slots, :]
        s.gain[5:6, :] += jnp.sum(dgate * (xh4 * gain[4]), 0, keepdims=True)
        s.bias[...] += jnp.broadcast_to(dgate, (SLOTS, LANES))
        gm = dgate * forget_w
        yield
        dcq, dck, dcv = attend_back(
            s.cp[seg], pair_queries(*g_co), pair_queries(s.cq[0, rows, :], s.cq[1, rows, :]),
            pair_lanes(s.ck[slots, :]), pair_lanes(s.cv[slots, :]),
        )
        s.dcq[rows, :] = dcq
        s.dck[slots, :] = dck
        s.dcv[slots, :] = dcv
        yield
        gm = gm + dot(jnp.concatenate([dwq, dck, dcv], 1), s.attn_t[2:5].reshape(3 * D, D))
        s.gain[4:5, :] += jnp.sum(gm * xh4, 0, keepdims=True)
        gmem = (gate * gz + norm_back(gm, gain[4], xh4, s.rs4[slots, :])).astype(bf16)
        s.gmem[slots, :] = gmem
        s.mem[...] = gmem
        yield

    s.mem[...] = jnp.zeros_like(s.mem)

    def backward_one(step, carry):
        together(backward(NSEG - 1 - step))
        return carry

    lax.fori_loop(0, NSEG - 1, backward_one, 0)
    last_step = backward(0)
    for _ in range(3):
        next(last_step)

    cut = pl.ds(pl.multiple_of(core * BLOCK, BLOCK), BLOCK)

    def put(i, value):
        value = value.astype(bf16)
        for j in range(LANE_CUTS):
            s.dw[(i * LANE_CUTS + j) * BLOCK : (i * LANE_CUTS + j + 1) * BLOCK, :] = value[:, j * LANES : (j + 1) * LANES]

    def put_products(base, names):
        for i, (left, right) in enumerate(names):
            put(base + i, dot_tn(left[:, cut], right[...]))

    def small_start(axis, value):
        here = place[axis]
        s.small[axis, here] = value
        for step in range(1, 4):
            own = s.small.at[axis, here]
            remote(own, own, s.small_send.at[axis], s.small_recv.at[axis], along(axis, (here + step) % 4)).start()

    def small_finish(axis):
        all_moved(s.small.at[axis, pl.ds(0, 3)], s.small_send.at[axis], s.small_recv.at[axis])
        return (s.small[axis, 0] + s.small[axis, 1]) + (s.small[axis, 2] + s.small[axis, 3])

    def others(axis, i):
        return [((i + step) % 4, step - 1, along(axis, (i + step) % 4)) for step in range(1, 4)]

    def add(refs):
        total = refs[0][...].astype(f32)
        for ref in refs[1:]:
            total += ref[...].astype(f32)
        return total.astype(bf16)

    def part_place(chunk, part):
        r = CHUNKS[chunk][part] * UNIT
        base = 64 * UNIT * (sum(sum(c) for c in CHUNKS[:chunk]) + sum(CHUNKS[chunk][:part]))
        axes = [(part + i) % 3 for i in range(3)]
        return r, base, axes, [place[a] for a in axes]

    def part_steps(chunk, part):
        r, base, axes, (i1, i2, i3) = part_place(chunk, part)
        right, left = along(axes[0], (i1 + 1) % 4), along(axes[0], (i1 + 3) % 4)
        near, far, mid, quad, last = (refs[chunk][part] for refs in (s.near, s.far, s.mid, s.quad, s.last))
        dw, mine = s.dw, full_ref.at[core]

        def copy(src, dst, device, i):
            remote(src, dst, s.send.at[chunk], s.recv.at[chunk, part, i], device).start()

        def arrived(ref, i):
            remote(ref, ref, s.send.at[chunk], s.recv.at[chunk, part, i], sibling).wait_recv()

        def block(b, first=0, count=16):
            return rows_at(base + (b % 4) * 16 * r + first * r, count * r)

        def pass_on(rows, device, i):
            copy(mine.at[rows], mine.at[rows], device, i)

        def pass_over(rows):
            remote(mine.at[rows], mine.at[rows], s.send.at[chunk], s.over.at[chunk], sibling).start()

        half0, half1 = pl.ds(0, 8 * r), pl.ds(8 * r, 8 * r)
        copy(dw.at[block(i1 + 2, 0, 8)], near.at[0], right, 0)
        copy(dw.at[block(i1 + 2, 8, 8)], near.at[1], left, 0)
        copy(dw.at[block(i1 + 1, 8, 8)], far.at[0, half1], right, 1)
        copy(dw.at[block(i1 + 3, 0, 8)], far.at[1, half0], left, 1)
        yield
        arrived(near, 0)
        near[0] = add([near.at[0], dw.at[block(i1 + 1, 0, 8)]])
        copy(near.at[0], far.at[0, half0], right, 1)
        near[1] = add([near.at[1], dw.at[block(i1 + 3, 8, 8)]])
        copy(near.at[1], far.at[1, half1], left, 1)
        yield
        arrived(far, 1)
        far[0] = add([far.at[0], far.at[1], dw.at[block(i1)]])
        for b, slot, to in others(axes[1], i2):
            copy(far.at[0, rows_at(b * 4 * r, 4 * r)], mid.at[slot], to, 2)
        yield
        arrived(mid, 2)
        middle = [mid.at[0], mid.at[1], mid.at[2], far.at[0, rows_at(i2 * 4 * r, 4 * r)]]
        home = rows_at(base + (i1 * 16 + i2 * 4) * r, 4 * r)
        quad[i3] = add(middle)
        for _, _, to in others(axes[2], i3):
            copy(quad.at[i3], quad.at[i3], to, 3)
        yield
        arrived(quad.at[pl.ds(0, 3)], 3)
        last[...] = add([quad.at[i] for i in range(4)])
        keep = pltpu.make_async_copy(last, mine.at[home], s.own.at[chunk, part])
        keep.start()
        for _, _, to in others(axes[1], i2):
            copy(last, mine.at[home], to, 4)
        yield
        keep.wait()
        arrived(mine.at[rows_at(base, 12 * r)], 4)
        pass_on(block(i1), right, 5)
        pass_on(block(i1), left, 5)
        pass_over(block(i1))
        yield
        arrived(mine.at[rows_at(base, 32 * r)], 5)
        pass_on(block(i1 + 3, 0, 8), right, 6)
        pass_on(block(i1 + 1, 8, 8), left, 6)
        pass_over(block(i1 + 3))
        pass_over(block(i1 + 1))
        yield
        arrived(mine.at[block(i1 + 2)], 6)
        pass_over(block(i1 + 2))
        yield
        if part == 2:
            units = sum(CHUNKS[chunk]) * UNIT
            start = base + 64 * r - 64 * units
            got = full_ref.at[1 - core, rows_at(start, 64 * units)]
            remote(got, got, s.send.at[chunk], s.over.at[chunk], sibling).wait_recv()
            sent = full_ref.at[core, rows_at(0, 196 * units)]
            remote(sent, sent, s.send.at[chunk], s.over.at[chunk], sibling).wait_send()
        yield

    chunks = [[part_steps(chunk, part) for part in range(3)] for chunk in range(len(CHUNKS))]

    def go(*order):
        for chunk in order:
            for part in chunks[chunk]:
                next(part)

    for i in range(4):
        cut_i = pl.ds(pl.multiple_of(core * 4 * BLOCK + i * BLOCK, BLOCK), BLOCK)
        put(i, dot_tn(s.hid[:, cut_i], s.gyl[...]))
        if i % 2:
            next(chunks[0][i // 2])
    put_products(4, [(s.mlow, s.dwq), (s.t, s.dwk)])
    next(chunks[0][2])
    for _ in range(FF // FCHUNK):
        next(last_step)
    put_products(6, [(s.t, s.dwv), (s.wo, s.gup)])
    for i in range(4):
        put(8 + i, dot_tn(s.n2[:, cut], s.gul[:, i * D : (i + 1) * D]))
    go(1)
    together(last_step)
    results((3,), results_start)
    put_products(12, [(s.n1, s.dcq), (s.mlow, s.dck), (s.mlow, s.dcv), (s.co, s.gbl)])

    gn1 = dot_nt(s.dcq[...], attn[4])
    xhat = s.xh1[...].astype(f32)
    s.gain[1:2, :] = jnp.sum(gn1 * xhat, 0, keepdims=True)
    ga = s.res[...] + norm_back(gn1, gain[1], xhat, s.rs1[...])
    s.res[...] = ga
    gal = ga.astype(bf16)
    s.gal[...] = gal
    s.cq[0], s.cq[1] = head_halves(dot_nt(gal, attn[3]))
    put_products(16, [(s.o, s.gal)])
    go(2)

    def self_backward(seg):
        rows = row_cut(seg)
        s.dq[rows, :], s.dk[rows, :], s.dv[rows, :] = attend_back(
            s.p[seg], pair_queries(s.cq[0, rows, :], s.cq[1, rows, :]),
            pair_queries(s.q[0, rows, :], s.q[1, rows, :]),
            pair_lanes(s.k[rows, :]), pair_lanes(s.v[rows, :]),
        )

    self_backward(0)
    self_backward(1)
    self_backward(2)
    go(0)
    self_backward(3)
    gh = dot_nt(s.dq[...], attn[0]) + dot_nt(s.dk[...], attn[1]) + dot_nt(s.dv[...], attn[2])
    go(1)
    xhat = s.xh0[...].astype(f32)
    s.gain[0:1, :] = jnp.sum(gh * xhat, 0, keepdims=True)
    s.gtok[...] = (s.res[...] + norm_back(gh, gain[0], xhat, s.rs0[...])).astype(bf16)
    s.gain[6:7, 0:SLOTS] = jnp.sum(jnp.where(diagonal, s.bias[:, 0:SLOTS], 0.0), 0, keepdims=True)
    small_start(0, s.gain[...])
    results((2,), results_start)
    put_products(17, [(s.h, s.dq), (s.h, s.dk), (s.h, s.dv)])
    go(3, 2, 0)
    total = small_finish(0)
    small_start(1, total)
    go(1, 3, 2, 0)
    total = small_finish(1)
    small_start(2, total)
    go(3, 1, 2, 0, 3)
    small_out[...] = small_finish(2)
    go(1, 2, 3, 0, 1, 2, 3, 0, 3, 1, 2, 3, 0, 1, 3, 2, 0, 1, 2)
    results((0, 1, 2, 3), results_finish)


def run_fused(tok, ocot, mcot, mem, lens, attn, win, wout, gains, fw, fb):
    vmem = pl.BlockSpec(memory_space=pltpu.VMEM)
    hbm = pl.BlockSpec(memory_space=pl.ANY)
    return pl.pallas_call(
        fused_kernel,
        out_shape=(
            jax.ShapeDtypeStruct((2, FLAT, LANES), bf16),
            jax.ShapeDtypeStruct((2, SEG, D), bf16),
            jax.ShapeDtypeStruct((2, SLOTS, D), bf16),
            jax.ShapeDtypeStruct((2, SEG, D), bf16),
            jax.ShapeDtypeStruct((2, SLOTS, D), bf16),
            jax.ShapeDtypeStruct((8, D), f32),
        ),
        in_specs=[hbm] * 11,
        out_specs=[hbm] * 5 + [vmem],
        scratch_shapes=[scratch_buffers()],
        compiler_params=pltpu.CompilerParams(collective_id=1, has_side_effects=True, vmem_limit_bytes=63 << 20),
        name="layer_and_sums",
    )(tok, ocot, mcot, mem, lens, attn, win, wout, gains, fw, fb)


def widen_kernel(
    full_ref, act_ref, mem_ref, gtok_ref, gmem_ref, small_ref,
    attn_ref, in_ref, out_ref, act_out, mem_out, gtok_out, gmem_out, gains_out, fw_out, fb_out,
    full_s, wide_s, load_sem, store_sem,
):
    def load(i):
        return [
            pltpu.make_async_copy(full_ref.at[half, i], full_s.at[i, half], load_sem.at[i, half]) for half in range(2)
        ]

    def target(i, half):
        if i < 4:
            return out_ref.at[pl.ds(half * 4 * BLOCK + i * BLOCK, BLOCK), :]
        if 8 <= i < 12:
            return in_ref.at[pl.ds(half * BLOCK, BLOCK), pl.ds((i - 8) * D, D)]
        index = i + 4 if i < 8 else i - 8 if i < 16 else 3 if i == 16 else i - 17
        return attn_ref.at[index, pl.ds(half * BLOCK, BLOCK), :]

    def store(i, half):
        return pltpu.make_async_copy(wide_s.at[i, half], target(i, half), store_sem)

    for i in range(NBLOCKS):
        for copy in load(i):
            copy.start()
    act_out[...] = act_ref[...]
    mem_out[...] = mem_ref[...]
    gtok_out[...] = gtok_ref[...].astype(f32)
    gmem_out[...] = gmem_ref[...].astype(f32)
    gains_out[...] = small_ref[0:5, :]
    fw_out[...] = small_ref[5:6, :]
    fb_out[...] = small_ref[6:7, 0:SLOTS]
    for i in range(NBLOCKS):
        for half, copy in enumerate(load(i)):
            copy.wait()
            for j in range(LANE_CUTS):
                wide_s[i, half, :, j * LANES : (j + 1) * LANES] = full_s[i, half, j].astype(f32)
            store(i, half).start()
    pltpu.make_async_copy(wide_s, wide_s, store_sem).wait()


def run_widen(full, *others):
    hbm = pl.BlockSpec(memory_space=pl.ANY)
    vmem = pl.BlockSpec(memory_space=pltpu.VMEM)
    return pl.pallas_call(
        widen_kernel,
        out_shape=(
            jax.ShapeDtypeStruct((12, D, D), f32),
            jax.ShapeDtypeStruct((D, FF), f32),
            jax.ShapeDtypeStruct((FF, D), f32),
            jax.ShapeDtypeStruct((2, SEG, D), bf16),
            jax.ShapeDtypeStruct((2, SLOTS, D), bf16),
            jax.ShapeDtypeStruct((2, SEG, D), f32),
            jax.ShapeDtypeStruct((2, SLOTS, D), f32),
            jax.ShapeDtypeStruct((5, D), f32),
            jax.ShapeDtypeStruct((1, D), f32),
            jax.ShapeDtypeStruct((1, SLOTS), f32),
        ),
        in_specs=[hbm] + [vmem] * 5,
        out_specs=[hbm] * 3 + [vmem] * 7,
        scratch_shapes=[
            pltpu.VMEM((NBLOCKS, 2, LANE_CUTS, BLOCK, LANES), bf16),
            pltpu.VMEM((NBLOCKS, 2, BLOCK, D), f32),
            pltpu.SemaphoreType.DMA((NBLOCKS, 2)),
            pltpu.SemaphoreType.DMA,
        ],
        compiler_params=pltpu.CompilerParams(vmem_limit_bytes=60 << 20),
        name="widen_gradients",
    )(full, *others)


def body(
    tokens, memory_start, doc_lengths, attn_weights, ffn_in, ffn_out, gains, forget_w, forget_bias,
    out_cotangent, memory_cotangent,
):
    full, *others = run_fused(
        tokens, out_cotangent, memory_cotangent, memory_start, doc_lengths,
        attn_weights.reshape(12, D, D), ffn_in, ffn_out, gains, forget_w.reshape(1, D), forget_bias.reshape(1, SLOTS),
    )
    grad_attn, grad_in, grad_out, acts, mems, gtok, gmem, grad_gains, grad_fw, grad_fb = run_widen(
        full.reshape(2, NBLOCKS, LANE_CUTS, BLOCK, LANES), *others
    )
    return (
        acts, mems, gtok, gmem, grad_attn.reshape(3, 4, D, D), grad_in, grad_out,
        grad_gains, grad_fw.reshape(D), grad_fb.reshape(SLOTS),
    )


def solution(mesh):
    return jax.shard_map(
        body,
        mesh=mesh,
        in_specs=(
            P("doc", "seg", None), P("doc", None, None), P("doc", None), P(), P(), P(), P(), P(), P(),
            P("doc", "seg", None), P("doc", "seg", None),
        ),
        out_specs=(
            P("doc", "seg", None), P("doc", "seg", None), P("doc", "seg", None), P("doc", "seg", None),
            P(), P(), P(), P(), P(), P(),
        ),
        check_vma=False,
    )
```

```python
from types import SimpleNamespace

import jax
import jax.numpy as jnp
from jax import lax
from jax.experimental import pallas as pl
from jax.experimental.pallas import tpu as pltpu
from jax.sharding import PartitionSpec as P

HEADS = 8
NDOC = 8
D = 512
FF = 2048
SLOTS = 64
SEG = 128
NSEG = 4
ROWS = NSEG * SEG
MROWS = NSEG * SLOTS
PAIRS = 4
PAIR = 128
FCHUNK = 2048
BLOCK = 256
NBLOCKS = 20
LANES = 128
LANE_CUTS = D // LANES
FLAT = NBLOCKS * BLOCK * LANE_CUTS
MESH = pl.DeviceIdType.MESH
SCALE = 0.125

f32 = jnp.float32
bf16 = jnp.bfloat16


def dot(a, b):
    return lax.dot_general(a, b, (((1,), (0,)), ((), ())), preferred_element_type=f32)


def dot_nt(a, b):
    return lax.dot_general(a, b, (((1,), (1,)), ((), ())), preferred_element_type=f32)


def dot_tn(a, b):
    return lax.dot_general(a, b, (((0,), (0,)), ((), ())), preferred_element_type=f32)


def norm_stats(values):
    centered = values - jnp.mean(values, -1, keepdims=True)
    rstd = lax.rsqrt(jnp.mean(centered * centered, -1, keepdims=True) + 1e-05)
    return centered * rstd, rstd


def norm_back(grad, gain, xhat, rstd):
    scaled = grad * gain
    mean_one = jnp.mean(scaled, -1, keepdims=True)
    mean_two = jnp.mean(scaled * xhat, -1, keepdims=True)
    return rstd * (scaled - mean_one - xhat * mean_two)


def head_halves(values):
    low_half = lax.broadcasted_iota(jnp.int32, (16, values.shape[1]), 1) % PAIR < PAIR // 2
    first = jnp.where(low_half, 1.0, 0.0).astype(bf16)[0:1, :]
    second = jnp.where(low_half, 0.0, 1.0).astype(bf16)[0:1, :]
    values = values.astype(bf16)
    return values * first, values * second


def join_halves(stacked):
    rows = stacked.shape[0] // 2
    low_half = lax.broadcasted_iota(jnp.int32, (rows, PAIR), 1) < PAIR // 2
    return jnp.where(low_half, stacked[:rows], stacked[rows:])


def attend(queries, keys, values, bias):
    scores = jnp.concatenate([dot_nt(k, q) for k, q in zip(keys, queries)], 1) + bias
    expd = jnp.exp(scores - jnp.max(scores, 0, keepdims=True))
    probs = (expd * (1.0 / jnp.sum(expd, 0, keepdims=True))).astype(bf16)
    width = queries[0].shape[0]
    mixed = [join_halves(dot_tn(probs[:, i * width : (i + 1) * width], v)) for i, v in enumerate(values)]
    return probs, jnp.concatenate(mixed, 1).astype(bf16)


def attend_back(probs, grads, queries, keys, values):
    width = queries[0].shape[0]
    wide = probs.astype(f32)
    dp = jnp.concatenate([dot_nt(v, g) for v, g in zip(values, grads)], 1)
    ds = (wide * (dp - jnp.sum(wide * dp, 0, keepdims=True))).astype(bf16)
    cuts = [slice(i * width, (i + 1) * width) for i in range(PAIRS)]
    dq = [join_halves(dot_tn(ds[:, cut], k)) for cut, k in zip(cuts, keys)]
    dk = [dot(ds[:, cut], q) for cut, q in zip(cuts, queries)]
    dv = [dot(probs[:, cut], g) for cut, g in zip(cuts, grads)]
    join = lambda parts: jnp.concatenate(parts, 1)
    return (join(dq) * SCALE).astype(bf16), join(dk).astype(bf16), join(dv).astype(bf16)


def pair_lanes(values):
    return [values[:, i * PAIR : (i + 1) * PAIR] for i in range(PAIRS)]


def pair_queries(first, second):
    return [jnp.concatenate(halves, 0) for halves in zip(pair_lanes(first), pair_lanes(second))]


def gelu_both(u):
    square = u * u
    tanh = jnp.tanh(0.7978845608028654 * u * (1.0 + 0.044715 * square))
    half = 0.5 + 0.5 * tanh
    hidden = u * half
    rest, square = (1.0 - tanh).astype(bf16), square.astype(bf16)
    slope = half.astype(bf16) + hidden.astype(bf16) * rest * (bf16(0.7978845608028654) + bf16(0.1070322243) * square)
    return hidden, slope


CHUNKS = ((2, 2, 2), (2, 2, 2), (1, 2, 2), (1, 1, 1))
UNIT = 16

TURNED = (7, 11, 8, 5, 6, 9, 10)


def scratch_buffers():
    def rows(dtype=bf16, width=D):
        return pltpu.VMEM((ROWS, width), dtype)

    def slots(dtype=bf16, width=D):
        return pltpu.VMEM((MROWS, width), dtype)

    def two(count):
        return pltpu.VMEM((2, count, D), bf16)

    def parts(shape_of):
        return [[pltpu.VMEM(shape_of(count * UNIT), bf16) for count in chunk] for chunk in CHUNKS]

    dma = pltpu.SemaphoreType.DMA
    return dict(
        attn=pltpu.VMEM((12, D, D), bf16), win=pltpu.VMEM((D, FF), bf16), wout=pltpu.VMEM((FF, D), bf16),
        attn_t=pltpu.VMEM((len(TURNED), D, D), bf16), win_t=pltpu.VMEM((FF, D), bf16), wout_t=pltpu.VMEM((D, FF), bf16),
        tok=rows(), ocot=rows(), mcot=slots(), mem=pltpu.VMEM((SLOTS, D), bf16),
        lens_own=pltpu.VMEM((8, LANES), jnp.int32), lens=pltpu.VMEM((8, LANES), jnp.int32),
        act=rows(), mout=slots(), gtok=rows(), gmem=slots(),
        h=rows(), q=two(ROWS), k=rows(), v=rows(), p=pltpu.VMEM((NSEG, SEG, HEADS * SEG), bf16), o=rows(),
        xh0=rows(), rs0=rows(f32, 1),
        res=rows(f32), n1=rows(), xh1=rows(), rs1=rows(f32, 1), cq=two(ROWS), ck=slots(), cv=slots(),
        cp=pltpu.VMEM((NSEG, SLOTS, HEADS * SEG), bf16), co=rows(),
        n2=rows(), xh2=rows(), rs2=rows(f32, 1), hid=rows(bf16, FF), gul=rows(bf16, FF),
        t=rows(), xh3=rows(), rs3=rows(f32, 1),
        xh4=slots(f32), rs4=slots(f32, 1), mlow=slots(), gate=slots(f32, 1), upd=slots(f32),
        wq=two(MROWS), wk=rows(), wv=rows(), wp=pltpu.VMEM((NSEG, SEG, HEADS * SLOTS), bf16), wo=slots(),
        gup=slots(), dwq=slots(), dwk=rows(), dwv=rows(), gyl=rows(), gbl=rows(),
        dcq=rows(), dck=slots(), dcv=slots(),
        gal=rows(), dq=rows(), dk=rows(), dv=rows(),
        gain=pltpu.VMEM((8, D), f32), bias=pltpu.VMEM((SLOTS, LANES), f32),
        dw=pltpu.VMEM((FLAT, LANES), bf16),
        near=parts(lambda r: (2, 8 * r, LANES)), far=parts(lambda r: (2, 16 * r, LANES)),
        mid=parts(lambda r: (3, 4 * r, LANES)), quad=parts(lambda r: (4, 4 * r, LANES)), last=parts(lambda r: (4 * r, LANES)),
        small=pltpu.VMEM((3, 5, 8, D), f32),
        in_send=dma((2, 2, 3)), in_recv=dma((4, 3)), first_send=dma((2,)), first_recv=dma((2,)),
        pass_send=dma((3,)), pass_recv=dma((3,)), in_local=dma((5,)), load=dma((8,)),
        gains=pltpu.VMEM((5, D), f32), fw=pltpu.VMEM((1, D), f32), fb=pltpu.VMEM((1, SLOTS), f32),
        lens_in=pltpu.VMEM((2, NDOC), jnp.int32),
        send=dma((len(CHUNKS),)), recv=dma((len(CHUNKS), 3, 7)), over=dma((len(CHUNKS),)), own=dma((len(CHUNKS), 3)),
        out_send=dma((2, 4)), out_recv=dma((2, 4)), out_local=dma((4,)),
        small_send=dma((3,)), small_recv=dma((3,)),
    )


def my_place():
    doc = lax.axis_index("doc")
    return lax.axis_index("seg"), doc // 8, (doc // 2) % 4, doc % 2


def device_at(x, y, z, core):
    return (x, y * 8 + z * 2 + core)


def remote(src, dst, send_sem, recv_sem, device):
    return pltpu.make_async_remote_copy(
        src_ref=src, dst_ref=dst, send_sem=send_sem, recv_sem=recv_sem, device_id=device, device_id_type=MESH
    )


def signal(sem, device):
    pl.semaphore_signal(sem, inc=1, device_id=device, device_id_type=MESH)


def fused_kernel(
    tok_ref, ocot_ref, mcot_ref, mem_ref, len_ref, attn_ref, win_ref, wout_ref, gains_ref, fw_ref, fb_ref,
    full_ref, act_out, mout_out, gtok_out, gmem_out, small_out,
    scratch,
):
    s = SimpleNamespace(**scratch)
    place = my_place()
    x, y, z, core = place
    owner, stream = x // 2, x % 2
    mine_here = owner == core
    sibling = device_at(x, y, z, 1 - core)

    def along(axis, coordinate):
        there = list(place)
        there[axis] = coordinate
        return device_at(*there)

    def rows_at(first, count):
        return pl.ds(pl.multiple_of(first, UNIT), count)

    loads = [
        pltpu.make_async_copy(attn_ref.at[pl.ds(0, 4)], s.attn.at[pl.ds(0, 4)], s.load.at[0]),
        pltpu.make_async_copy(attn_ref.at[pl.ds(4, 8)], s.attn.at[pl.ds(4, 8)], s.load.at[1]),
        pltpu.make_async_copy(win_ref, s.win, s.load.at[2]),
        pltpu.make_async_copy(wout_ref, s.wout, s.load.at[3]),
    ]
    small_loads = [
        pltpu.make_async_copy(src, dst, s.load.at[4 + i])
        for i, (src, dst) in enumerate([(len_ref, s.lens_in), (gains_ref, s.gains), (fw_ref, s.fw), (fb_ref, s.fb)])
    ]
    for load in small_loads:
        load.start()
    for i in (1, 2, 3, 0):
        loads[i].start()

    barrier = pltpu.get_barrier_semaphore()
    for step in range(1, 4):
        signal(barrier, device_at((x + step) % 4, y, z, owner))
    for axis in range(3):
        for step in range(1, 4):
            signal(barrier, along(axis, (place[axis] + step) % 4))
    signal(barrier, sibling)
    for k in range(2):

        @pl.when(jnp.logical_or(2 * core + k != x, owner != core))
        def _():
            signal(barrier, device_at(2 * core + k, y, z, owner))

    small_loads[0].wait()
    s.lens_own[...] = jnp.zeros_like(s.lens_own)
    s.lens_own[0:2, 0:NDOC] = s.lens_in[...]
    pl.semaphore_wait(barrier, 16 - 3 * mine_here.astype(jnp.int32))

    arrays = [(tok_ref, s.tok, SEG), (ocot_ref, s.ocot, SEG), (mcot_ref, s.mcot, SLOTS)]

    def gather_sends(i, start):
        src, dst, count = arrays[i]
        half = count // 2
        for st in range(2):
            chip = 2 * core + st

            @pl.when(chip != x)
            def _():
                for to_core in range(2):
                    copy = remote(
                        src.at[st, pl.ds(to_core * half, half)], dst.at[rows_at(x * count + to_core * half, half)],
                        s.in_send.at[st, to_core, i], s.in_recv.at[x, i], device_at(chip, y, z, to_core),
                    )
                    copy.start() if start else copy.wait_send()

            @pl.when(chip == x)
            def _():
                target = dst.at[rows_at(x * count, count)]
                copy = remote(src.at[st], target, s.in_send.at[st, 0, i], s.in_recv.at[x, i], sibling)
                if start:
                    pltpu.make_async_copy(src.at[st], target, s.in_local.at[i]).start()
                    copy.start()
                else:
                    copy.wait_send()

    def gather_own(i):
        src, dst, count = arrays[i]
        whole = dst.at[rows_at(x * count, count)]

        @pl.when(mine_here)
        def _():
            pltpu.make_async_copy(src.at[stream], whole, s.in_local.at[i]).wait()

        @pl.when(jnp.logical_not(mine_here))
        def _():
            remote(whole, whole, s.in_send.at[0, 0, i], s.in_recv.at[x, i], sibling).wait_recv()

    def all_moved(ref, send_sem, recv_sem):
        copy = remote(ref, ref, send_sem, recv_sem, sibling)
        copy.wait_send()
        copy.wait_recv()

    def gather_forward(i):
        src, dst, count = arrays[i]
        half = count // 2
        for step in (1, 3, 2):
            seg = (x + step) % 4
            part = dst.at[rows_at(seg * count + core * half, half)]
            remote(
                part, part, s.in_send.at[0, 0, i], s.in_recv.at[seg, i], device_at(seg, y, z, owner)
            ).wait_recv()
            remote(part, part, s.pass_send.at[i], s.pass_recv.at[i], sibling).start()

    def gather_finish(i):
        src, dst, count = arrays[i]
        gather_sends(i, False)
        three_halves = dst.at[pl.ds(0, 3 * count // 2)]
        all_moved(three_halves, s.pass_send.at[i], s.pass_recv.at[i])

    gather_sends(0, True)

    firsts = [(mem_ref.at[stream], s.mem), (s.lens_own, s.lens)]
    for i, (src, dst) in enumerate(firsts):

        @pl.when(mine_here)
        def _():
            remote(src, dst, s.first_send.at[i], s.first_recv.at[i], sibling).start()
            pltpu.make_async_copy(src, dst, s.in_local.at[3 + i]).start()

    loads[1].wait()
    for i, index in enumerate(TURNED):
        s.attn_t[i] = jnp.transpose(s.attn[index])
    loads[2].wait()
    for c in range(0, FF, D):
        s.win_t[c : c + D, :] = jnp.transpose(s.win[:, c : c + D])
    loads[3].wait()
    for c in range(0, FF, D):
        s.wout_t[:, c : c + D] = jnp.transpose(s.wout[c : c + D, :])
    loads[0].wait()

    for i, (src, dst) in enumerate(firsts):

        @pl.when(mine_here)
        def _():
            remote(src, dst, s.first_send.at[i], s.first_recv.at[i], sibling).wait_send()
            pltpu.make_async_copy(src, dst, s.in_local.at[3 + i]).wait()

        @pl.when(jnp.logical_not(mine_here))
        def _():
            remote(src, dst, s.first_send.at[i], s.first_recv.at[i], sibling).wait_recv()

    attn, win, wout = s.attn, s.win, s.wout
    attn_t = {index: s.attn_t.at[i] for i, index in enumerate(TURNED)}
    win_t, wout_t = s.win_t, s.wout_t
    for load in small_loads[1:]:
        load.wait()
    gain = [s.gains[i : i + 1, :] for i in range(5)]
    forget_w = s.fw[...]
    square = (SLOTS, SLOTS)
    diagonal = lax.broadcasted_iota(jnp.int32, square, 0) == lax.broadcasted_iota(jnp.int32, square, 1)
    forget_bias = jnp.sum(jnp.where(diagonal, jnp.broadcast_to(s.fb[...], square), 0.0), -1, keepdims=True)

    ends = []
    for j in range(NDOC):
        ends.append(s.lens[pl.ds(stream, 1), j : j + 1] + (ends[-1] if ends else 0))

    def doc_ids(shape, dim, base):
        pos = lax.broadcasted_iota(jnp.int32, shape, dim) + base
        return sum((end <= pos).astype(jnp.int32) for end in ends)

    def row_cut(seg):
        return pl.ds(pl.multiple_of(seg * SEG, SEG), SEG)

    def slot_cut(seg):
        return pl.ds(pl.multiple_of(seg * SLOTS, SLOTS), SLOTS)

    def together(*works):
        works = list(works)
        while works:
            for work in list(works):
                try:
                    next(work)
                except StopIteration:
                    works.remove(work)

    def self_forward(seg):
        rows = row_cut(seg)
        tok = s.tok[rows, :].astype(f32)
        xhat, rstd = norm_stats(tok)
        s.xh0[rows, :] = xhat.astype(bf16)
        s.rs0[rows, :] = rstd
        h = (xhat * gain[0]).astype(bf16)
        s.h[rows, :] = h
        yield
        q0, q1 = head_halves(dot(h, attn[0]) * SCALE)
        s.q[0, rows, :] = q0
        s.q[1, rows, :] = q1
        yield
        k = dot(h, attn[1]).astype(bf16)
        v = dot(h, attn[2]).astype(bf16)
        s.k[rows, :] = k
        s.v[rows, :] = v
        yield
        same = doc_ids((SEG, SEG), 0, seg * SEG) == doc_ids((SEG, SEG), 1, seg * SEG)
        bias = jnp.concatenate([jnp.where(same, 0.0, -1e30)] * HEADS, 1)
        s.p[seg], o = attend(pair_queries(q0, q1), pair_lanes(k), pair_lanes(v), bias)
        s.o[rows, :] = o
        yield
        res = tok + dot(o, attn[3])
        s.res[rows, :] = res
        xhat, rstd = norm_stats(res)
        s.xh1[rows, :] = xhat.astype(bf16)
        s.rs1[rows, :] = rstd
        n1 = (xhat * gain[1]).astype(bf16)
        s.n1[rows, :] = n1
        yield
        s.cq[0, rows, :], s.cq[1, rows, :] = head_halves(dot(n1, attn[4]) * SCALE)
        yield

    def forward(seg, mem):
        rows, slots = row_cut(seg), slot_cut(seg)
        xhat, rstd = norm_stats(mem)
        s.xh4[slots, :] = xhat
        s.rs4[slots, :] = rstd
        m = xhat * gain[4]
        mlow = m.astype(bf16)
        s.mlow[slots, :] = mlow
        ck = dot(mlow, attn[5]).astype(bf16)
        cv = dot(mlow, attn[6]).astype(bf16)
        s.ck[slots, :] = ck
        s.cv[slots, :] = cv
        yield
        s.cp[seg], co = attend(
            pair_queries(s.cq[0, rows, :], s.cq[1, rows, :]), pair_lanes(ck), pair_lanes(cv), 0.0
        )
        s.co[rows, :] = co
        yield
        res = s.res[rows, :] + dot(co, attn[7])
        xhat, rstd = norm_stats(res)
        s.xh2[rows, :] = xhat.astype(bf16)
        s.rs2[rows, :] = rstd
        n2 = (xhat * gain[2]).astype(bf16)
        s.n2[rows, :] = n2
        yield
        for c in range(0, FF, FCHUNK):
            hid, slope = gelu_both(dot(n2, win[:, c : c + FCHUNK]))
            hid = hid.astype(bf16)
            s.hid[rows, c : c + FCHUNK] = hid
            s.gul[rows, c : c + FCHUNK] = slope
            res = res + dot(hid, wout[c : c + FCHUNK, :])
            yield
        s.act[rows, :] = res.astype(bf16)
        xhat, rstd = norm_stats(res)
        s.xh3[rows, :] = xhat.astype(bf16)
        s.rs3[rows, :] = rstd
        t = (xhat * gain[3]).astype(bf16)
        s.t[rows, :] = t
        yield
        gate = jax.nn.sigmoid(jnp.sum(m * forget_w, -1, keepdims=True) + forget_bias)
        s.gate[slots, :] = gate
        wq0, wq1 = head_halves(dot(mlow, attn[8]) * SCALE)
        s.wq[0, slots, :] = wq0
        s.wq[1, slots, :] = wq1
        wk = dot(t, attn[9]).astype(bf16)
        wv = dot(t, attn[10]).astype(bf16)
        s.wk[rows, :] = wk
        s.wv[rows, :] = wv
        yield
        pos = lax.broadcasted_iota(jnp.int32, (SEG, HEADS * SLOTS), 0) + seg * SEG
        s.wp[seg], wo = attend(
            pair_queries(wq0, wq1), pair_lanes(wk), pair_lanes(wv), jnp.where(pos < ends[-1], 0.0, -1e30)
        )
        s.wo[slots, :] = wo
        yield
        update = dot(wo, attn[11])
        s.upd[slots, :] = mem - update
        fresh = (update + gate * (mem - update)).astype(bf16)
        s.mout[slots, :] = fresh
        s.mem[...] = fresh
        yield

    first_step = forward(0, s.mem[...].astype(f32))
    next(first_step)
    gather_forward(0)
    gather_own(0)
    together(self_forward(x))
    gather_finish(0)
    gather_sends(1, True)
    gather_sends(2, True)
    rest = [step + (x <= step).astype(jnp.int32) for step in range(NSEG - 1)]
    together(self_forward(rest[0]))
    together(first_step, self_forward(rest[1]))
    together(forward(1, s.mem[...].astype(f32)), self_forward(rest[2]))
    together(forward(2, s.mem[...].astype(f32)))
    gather_forward(1)
    gather_forward(2)
    together(forward(NSEG - 1, s.mem[...].astype(f32)))

    def results(indices, do):
        for k in range(2):
            seg = 2 * core + k
            here = jnp.logical_and(seg == x, mine_here)
            peer = device_at(seg, y, z, owner)
            sources = [
                (s.act.at[rows_at(seg * SEG, SEG)], act_out), (s.mout.at[rows_at(seg * SLOTS, SLOTS)], mout_out),
                (s.gtok.at[rows_at(seg * SEG, SEG)], gtok_out), (s.gmem.at[rows_at(seg * SLOTS, SLOTS)], gmem_out),
            ]
            for i in indices:
                src, dst = sources[i]

                @pl.when(jnp.logical_not(here))
                def _():
                    do(
                        remote(src, dst.at[stream], s.out_send.at[k, i], s.out_recv.at[stream, i], peer),
                        remote(src, dst.at[k], s.out_send.at[k, i], s.out_recv.at[k, i], peer),
                    )

                @pl.when(here)
                def _():
                    do(pltpu.make_async_copy(src, dst.at[stream], s.out_local.at[i]), None)

    def results_start(copy, back):
        copy.start()

    def results_finish(copy, back):
        if back is None:
            copy.wait()
        else:
            copy.wait_send()
            back.wait_recv()

    results((0, 1), results_start)
    for i in (1, 2):
        gather_own(i)
        gather_finish(i)

    s.gain[...] = jnp.zeros_like(s.gain)
    s.bias[...] = jnp.zeros_like(s.bias)

    def backward(seg):
        rows, slots = row_cut(seg), slot_cut(seg)
        gz = (s.mcot[slots, :].astype(f32) + s.mem[...].astype(f32)).astype(bf16).astype(f32)
        gate = s.gate[slots, :]
        gup = ((1.0 - gate) * gz).astype(bf16)
        s.gup[slots, :] = gup
        g_wo = head_halves(dot(gup, attn_t[11][...]))
        yield
        dwq, dwk, dwv = attend_back(
            s.wp[seg], pair_queries(*g_wo), pair_queries(s.wq[0, slots, :], s.wq[1, slots, :]),
            pair_lanes(s.wk[rows, :]), pair_lanes(s.wv[rows, :]),
        )
        s.dwq[slots, :] = dwq
        s.dwk[rows, :] = dwk
        s.dwv[rows, :] = dwv
        yield
        gt = dot(jnp.concatenate([dwk, dwv], 1), s.attn_t[5:7].reshape(2 * D, D))
        xhat = s.xh3[rows, :].astype(f32)
        s.gain[3:4, :] += jnp.sum(gt * xhat, 0, keepdims=True)
        gy = s.ocot[rows, :].astype(f32) + norm_back(gt, gain[3], xhat, s.rs3[rows, :])
        gyl = gy.astype(bf16)
        s.gyl[rows, :] = gyl
        yield
        gn2 = jnp.zeros((SEG, D), f32)
        for c in range(0, FF, FCHUNK):
            ghid = dot(gyl, wout_t[:, c : c + FCHUNK])
            gul = (ghid * s.gul[rows, c : c + FCHUNK].astype(f32)).astype(bf16)
            s.gul[rows, c : c + FCHUNK] = gul
            gn2 = gn2 + dot(gul, win_t[c : c + FCHUNK, :])
            yield
        xhat = s.xh2[rows, :].astype(f32)
        s.gain[2:3, :] += jnp.sum(gn2 * xhat, 0, keepdims=True)
        gb = gy + norm_back(gn2, gain[2], xhat, s.rs2[rows, :])
        s.res[rows, :] = gb
        gbl = gb.astype(bf16)
        s.gbl[rows, :] = gbl
        yield
        g_co = head_halves(dot(gbl, attn_t[7][...]))
        dgate = jnp.sum(gz * s.upd[slots, :], -1, keepdims=True) * gate * (1.0 - gate)
        xh4 = s.xh4[slots, :]
        s.gain[5:6, :] += jnp.sum(dgate * (xh4 * gain[4]), 0, keepdims=True)
        s.bias[...] += jnp.broadcast_to(dgate, (SLOTS, LANES))
        gm = dgate * forget_w
        yield
        dcq, dck, dcv = attend_back(
            s.cp[seg], pair_queries(*g_co), pair_queries(s.cq[0, rows, :], s.cq[1, rows, :]),
            pair_lanes(s.ck[slots, :]), pair_lanes(s.cv[slots, :]),
        )
        s.dcq[rows, :] = dcq
        s.dck[slots, :] = dck
        s.dcv[slots, :] = dcv
        yield
        gm = gm + dot(jnp.concatenate([dwq, dck, dcv], 1), s.attn_t[2:5].reshape(3 * D, D))
        s.gain[4:5, :] += jnp.sum(gm * xh4, 0, keepdims=True)
        gmem = (gate * gz + norm_back(gm, gain[4], xh4, s.rs4[slots, :])).astype(bf16)
        s.gmem[slots, :] = gmem
        s.mem[...] = gmem
        yield

    s.mem[...] = jnp.zeros_like(s.mem)

    def backward_one(step, carry):
        together(backward(NSEG - 1 - step))
        return carry

    lax.fori_loop(0, NSEG - 1, backward_one, 0)
    last_step = backward(0)
    for _ in range(3):
        next(last_step)

    cut = pl.ds(pl.multiple_of(core * BLOCK, BLOCK), BLOCK)

    def put(i, value):
        value = value.astype(bf16)
        for j in range(LANE_CUTS):
            s.dw[(i * LANE_CUTS + j) * BLOCK : (i * LANE_CUTS + j + 1) * BLOCK, :] = value[:, j * LANES : (j + 1) * LANES]

    def put_products(base, names):
        for i, (left, right) in enumerate(names):
            put(base + i, dot_tn(left[:, cut], right[...]))

    def small_start(axis, value):
        here = place[axis]
        s.small[axis, here] = value
        for step in range(1, 4):
            own = s.small.at[axis, here]
            remote(own, own, s.small_send.at[axis], s.small_recv.at[axis], along(axis, (here + step) % 4)).start()

    def small_finish(axis):
        all_moved(s.small.at[axis, pl.ds(0, 3)], s.small_send.at[axis], s.small_recv.at[axis])
        return (s.small[axis, 0] + s.small[axis, 1]) + (s.small[axis, 2] + s.small[axis, 3])

    def others(axis, i):
        return [((i + step) % 4, step - 1, along(axis, (i + step) % 4)) for step in range(1, 4)]

    def add(refs):
        total = refs[0][...].astype(f32)
        for ref in refs[1:]:
            total += ref[...].astype(f32)
        return total.astype(bf16)

    def part_place(chunk, part):
        r = CHUNKS[chunk][part] * UNIT
        base = 64 * UNIT * (sum(sum(c) for c in CHUNKS[:chunk]) + sum(CHUNKS[chunk][:part]))
        axes = [(part + i) % 3 for i in range(3)]
        return r, base, axes, [place[a] for a in axes]

    def part_steps(chunk, part):
        r, base, axes, (i1, i2, i3) = part_place(chunk, part)
        right, left = along(axes[0], (i1 + 1) % 4), along(axes[0], (i1 + 3) % 4)
        near, far, mid, quad, last = (refs[chunk][part] for refs in (s.near, s.far, s.mid, s.quad, s.last))
        dw, mine = s.dw, full_ref.at[core]

        def copy(src, dst, device, i):
            remote(src, dst, s.send.at[chunk], s.recv.at[chunk, part, i], device).start()

        def arrived(ref, i):
            remote(ref, ref, s.send.at[chunk], s.recv.at[chunk, part, i], sibling).wait_recv()

        def block(b, first=0, count=16):
            return rows_at(base + (b % 4) * 16 * r + first * r, count * r)

        def pass_on(rows, device, i):
            copy(mine.at[rows], mine.at[rows], device, i)

        def pass_over(rows):
            remote(mine.at[rows], mine.at[rows], s.send.at[chunk], s.over.at[chunk], sibling).start()

        half0, half1 = pl.ds(0, 8 * r), pl.ds(8 * r, 8 * r)
        copy(dw.at[block(i1 + 2, 0, 8)], near.at[0], right, 0)
        copy(dw.at[block(i1 + 2, 8, 8)], near.at[1], left, 0)
        copy(dw.at[block(i1 + 1, 8, 8)], far.at[0, half1], right, 1)
        copy(dw.at[block(i1 + 3, 0, 8)], far.at[1, half0], left, 1)
        yield
        arrived(near, 0)
        near[0] = add([near.at[0], dw.at[block(i1 + 1, 0, 8)]])
        copy(near.at[0], far.at[0, half0], right, 1)
        near[1] = add([near.at[1], dw.at[block(i1 + 3, 8, 8)]])
        copy(near.at[1], far.at[1, half1], left, 1)
        yield
        arrived(far, 1)
        far[0] = add([far.at[0], far.at[1], dw.at[block(i1)]])
        for b, slot, to in others(axes[1], i2):
            copy(far.at[0, rows_at(b * 4 * r, 4 * r)], mid.at[slot], to, 2)
        yield
        arrived(mid, 2)
        middle = [mid.at[0], mid.at[1], mid.at[2], far.at[0, rows_at(i2 * 4 * r, 4 * r)]]
        home = rows_at(base + (i1 * 16 + i2 * 4) * r, 4 * r)
        quad[i3] = add(middle)
        for _, _, to in others(axes[2], i3):
            copy(quad.at[i3], quad.at[i3], to, 3)
        yield
        arrived(quad.at[pl.ds(0, 3)], 3)
        last[...] = add([quad.at[i] for i in range(4)])
        keep = pltpu.make_async_copy(last, mine.at[home], s.own.at[chunk, part])
        keep.start()
        for _, _, to in others(axes[1], i2):
            copy(last, mine.at[home], to, 4)
        yield
        keep.wait()
        arrived(mine.at[rows_at(base, 12 * r)], 4)
        pass_on(block(i1), right, 5)
        pass_on(block(i1), left, 5)
        pass_over(block(i1))
        yield
        arrived(mine.at[rows_at(base, 32 * r)], 5)
        pass_on(block(i1 + 3, 0, 8), right, 6)
        pass_on(block(i1 + 1, 8, 8), left, 6)
        pass_over(block(i1 + 3))
        pass_over(block(i1 + 1))
        yield
        arrived(mine.at[block(i1 + 2)], 6)
        pass_over(block(i1 + 2))
        yield
        if part == 2:
            units = sum(CHUNKS[chunk]) * UNIT
            start = base + 64 * r - 64 * units
            got = full_ref.at[1 - core, rows_at(start, 64 * units)]
            remote(got, got, s.send.at[chunk], s.over.at[chunk], sibling).wait_recv()
            sent = full_ref.at[core, rows_at(0, 196 * units)]
            remote(sent, sent, s.send.at[chunk], s.over.at[chunk], sibling).wait_send()
        yield

    chunks = [[part_steps(chunk, part) for part in range(3)] for chunk in range(len(CHUNKS))]

    def go(*order):
        for chunk in order:
            for part in chunks[chunk]:
                next(part)

    for i in range(4):
        cut_i = pl.ds(pl.multiple_of(core * 4 * BLOCK + i * BLOCK, BLOCK), BLOCK)
        put(i, dot_tn(s.hid[:, cut_i], s.gyl[...]))
        if i % 2:
            next(chunks[0][i // 2])
    put_products(4, [(s.mlow, s.dwq), (s.t, s.dwk)])
    next(chunks[0][2])
    put_products(6, [(s.t, s.dwv), (s.wo, s.gup)])
    next(chunks[1][0])
    for _ in range(FF // FCHUNK):
        next(last_step)
    for i in range(4):
        put(8 + i, dot_tn(s.n2[:, cut], s.gul[:, i * D : (i + 1) * D]))
        if i % 2:
            next(chunks[1][1 + i // 2])
    together(last_step)
    results((3,), results_start)
    put_products(12, [(s.n1, s.dcq), (s.mlow, s.dck), (s.mlow, s.dcv), (s.co, s.gbl)])

    gn1 = dot_nt(s.dcq[...], attn[4])
    xhat = s.xh1[...].astype(f32)
    s.gain[1:2, :] = jnp.sum(gn1 * xhat, 0, keepdims=True)
    ga = s.res[...] + norm_back(gn1, gain[1], xhat, s.rs1[...])
    s.res[...] = ga
    gal = ga.astype(bf16)
    s.gal[...] = gal
    s.cq[0], s.cq[1] = head_halves(dot_nt(gal, attn[3]))
    put_products(16, [(s.o, s.gal)])
    go(2)

    def self_backward(seg):
        rows = row_cut(seg)
        s.dq[rows, :], s.dk[rows, :], s.dv[rows, :] = attend_back(
            s.p[seg], pair_queries(s.cq[0, rows, :], s.cq[1, rows, :]),
            pair_queries(s.q[0, rows, :], s.q[1, rows, :]),
            pair_lanes(s.k[rows, :]), pair_lanes(s.v[rows, :]),
        )

    self_backward(0)
    self_backward(1)
    self_backward(2)
    go(0)
    self_backward(3)
    gh = dot_nt(s.dq[...], attn[0]) + dot_nt(s.dk[...], attn[1]) + dot_nt(s.dv[...], attn[2])
    go(1)
    xhat = s.xh0[...].astype(f32)
    s.gain[0:1, :] = jnp.sum(gh * xhat, 0, keepdims=True)
    s.gtok[...] = (s.res[...] + norm_back(gh, gain[0], xhat, s.rs0[...])).astype(bf16)
    s.gain[6:7, 0:SLOTS] = jnp.sum(jnp.where(diagonal, s.bias[:, 0:SLOTS], 0.0), 0, keepdims=True)
    small_start(0, s.gain[...])
    results((2,), results_start)
    put_products(17, [(s.h, s.dq), (s.h, s.dk), (s.h, s.dv)])
    go(3, 2, 0)
    total = small_finish(0)
    small_start(1, total)
    go(1, 3, 2, 0)
    total = small_finish(1)
    small_start(2, total)
    go(3, 1, 2, 0, 3)
    small_out[...] = small_finish(2)
    go(1, 2, 3, 0, 1, 2, 3, 0, 3, 1, 2, 3, 0, 1, 3, 2, 0, 1, 2)
    results((0, 1, 2, 3), results_finish)


def run_fused(tok, ocot, mcot, mem, lens, attn, win, wout, gains, fw, fb):
    vmem = pl.BlockSpec(memory_space=pltpu.VMEM)
    hbm = pl.BlockSpec(memory_space=pl.ANY)
    return pl.pallas_call(
        fused_kernel,
        out_shape=(
            jax.ShapeDtypeStruct((2, FLAT, LANES), bf16),
            jax.ShapeDtypeStruct((2, SEG, D), bf16),
            jax.ShapeDtypeStruct((2, SLOTS, D), bf16),
            jax.ShapeDtypeStruct((2, SEG, D), bf16),
            jax.ShapeDtypeStruct((2, SLOTS, D), bf16),
            jax.ShapeDtypeStruct((8, D), f32),
        ),
        in_specs=[hbm] * 11,
        out_specs=[hbm] * 5 + [vmem],
        scratch_shapes=[scratch_buffers()],
        compiler_params=pltpu.CompilerParams(collective_id=1, has_side_effects=True, vmem_limit_bytes=63 << 20),
        name="layer_and_sums",
    )(tok, ocot, mcot, mem, lens, attn, win, wout, gains, fw, fb)


def widen_kernel(
    full_ref, act_ref, mem_ref, gtok_ref, gmem_ref, small_ref,
    attn_ref, in_ref, out_ref, act_out, mem_out, gtok_out, gmem_out, gains_out, fw_out, fb_out,
    full_s, wide_s, load_sem, store_sem,
):
    def load(i):
        return [
            pltpu.make_async_copy(full_ref.at[half, i], full_s.at[i, half], load_sem.at[i, half]) for half in range(2)
        ]

    def target(i, half):
        if i < 4:
            return out_ref.at[pl.ds(half * 4 * BLOCK + i * BLOCK, BLOCK), :]
        if 8 <= i < 12:
            return in_ref.at[pl.ds(half * BLOCK, BLOCK), pl.ds((i - 8) * D, D)]
        index = i + 4 if i < 8 else i - 8 if i < 16 else 3 if i == 16 else i - 17
        return attn_ref.at[index, pl.ds(half * BLOCK, BLOCK), :]

    def store(i, half):
        return pltpu.make_async_copy(wide_s.at[i, half], target(i, half), store_sem)

    for i in range(NBLOCKS):
        for copy in load(i):
            copy.start()
    act_out[...] = act_ref[...]
    mem_out[...] = mem_ref[...]
    gtok_out[...] = gtok_ref[...].astype(f32)
    gmem_out[...] = gmem_ref[...].astype(f32)
    gains_out[...] = small_ref[0:5, :]
    fw_out[...] = small_ref[5:6, :]
    fb_out[...] = small_ref[6:7, 0:SLOTS]
    for i in range(NBLOCKS):
        for half, copy in enumerate(load(i)):
            copy.wait()
            for j in range(LANE_CUTS):
                wide_s[i, half, :, j * LANES : (j + 1) * LANES] = full_s[i, half, j].astype(f32)
            store(i, half).start()
    pltpu.make_async_copy(wide_s, wide_s, store_sem).wait()


def run_widen(full, *others):
    hbm = pl.BlockSpec(memory_space=pl.ANY)
    vmem = pl.BlockSpec(memory_space=pltpu.VMEM)
    return pl.pallas_call(
        widen_kernel,
        out_shape=(
            jax.ShapeDtypeStruct((12, D, D), f32),
            jax.ShapeDtypeStruct((D, FF), f32),
            jax.ShapeDtypeStruct((FF, D), f32),
            jax.ShapeDtypeStruct((2, SEG, D), bf16),
            jax.ShapeDtypeStruct((2, SLOTS, D), bf16),
            jax.ShapeDtypeStruct((2, SEG, D), f32),
            jax.ShapeDtypeStruct((2, SLOTS, D), f32),
            jax.ShapeDtypeStruct((5, D), f32),
            jax.ShapeDtypeStruct((1, D), f32),
            jax.ShapeDtypeStruct((1, SLOTS), f32),
        ),
        in_specs=[hbm] + [vmem] * 5,
        out_specs=[hbm] * 3 + [vmem] * 7,
        scratch_shapes=[
            pltpu.VMEM((NBLOCKS, 2, LANE_CUTS, BLOCK, LANES), bf16),
            pltpu.VMEM((NBLOCKS, 2, BLOCK, D), f32),
            pltpu.SemaphoreType.DMA((NBLOCKS, 2)),
            pltpu.SemaphoreType.DMA,
        ],
        compiler_params=pltpu.CompilerParams(vmem_limit_bytes=60 << 20),
        name="widen_gradients",
    )(full, *others)


def body(
    tokens, memory_start, doc_lengths, attn_weights, ffn_in, ffn_out, gains, forget_w, forget_bias,
    out_cotangent, memory_cotangent,
):
    full, *others = run_fused(
        tokens, out_cotangent, memory_cotangent, memory_start, doc_lengths,
        attn_weights.reshape(12, D, D), ffn_in, ffn_out, gains, forget_w.reshape(1, D), forget_bias.reshape(1, SLOTS),
    )
    grad_attn, grad_in, grad_out, acts, mems, gtok, gmem, grad_gains, grad_fw, grad_fb = run_widen(
        full.reshape(2, NBLOCKS, LANE_CUTS, BLOCK, LANES), *others
    )
    return (
        acts, mems, gtok, gmem, grad_attn.reshape(3, 4, D, D), grad_in, grad_out,
        grad_gains, grad_fw.reshape(D), grad_fb.reshape(SLOTS),
    )


def solution(mesh):
    return jax.shard_map(
        body,
        mesh=mesh,
        in_specs=(
            P("doc", "seg", None), P("doc", None, None), P("doc", None), P(), P(), P(), P(), P(), P(),
            P("doc", "seg", None), P("doc", "seg", None),
        ),
        out_specs=(
            P("doc", "seg", None), P("doc", "seg", None), P("doc", "seg", None), P("doc", "seg", None),
            P(), P(), P(), P(), P(), P(),
        ),
        check_vma=False,
    )
```
